32 devices in a mesh: group: 4 (over y, core), member: 8 (over z, x).
Axes of the slice: x: 2, y: 2, z: 4, core: 2. Of those that a mesh axis runs over, the one named last changes fastest.
Arguments:
- encoded: float32 [8192, 256], P(('group', 'member'))
- item_table: float32 [131072, 256], P(('group', 'member'))
- target_owner: int32 [8192, 1], P(('group', 'member')), may hold values from 0 to 31; in each aligned block of 256 rows (0 to 255, 256 to 511, ...) at most 32 rows name the same one
- target_local: int32 [8192], P(('group', 'member')), may hold values from 0 to 4095
- negative_ids: int32 [16384], P(('group', 'member')), may hold values from 0 to 131071, as said below
- valid: int32 [8192], P(('group', 'member')), may hold values 0 or 1
Outputs:
- encoded_grad: float32 [8192, 256], P(('group', 'member'))
- table_grad: float32 [131072, 256], P(('group', 'member'))
The draws below stay inside these ranges and needn't reach their ends.
Inputs may be any that keep to these rules, and one draw needn't show every extreme that they name: `target_owner`: the positions of one device name any one owner at most 32 times; some owner is named exactly 32 times by some device. `negative_ids`: id // 4096 is the owning device; the 512 ids of one device name every owning device exactly 16 times.
All inputs are finite; a program needn't handle non-finite values. No bound on the sum of `valid` on one device may be relied on, other than what follows from the above.
Results may differ from the reference program's by a relative error of at most 0.0003.
Values sent between devices are 32-bit elements; how exact they have to be, the bound alone decides.
No kernel may reach another device: no remote copies, remote signals or barrier semaphores. Data moves between devices by JAX's collectives and lax.ppermute only.
A program may use at most 128 MiB of HBM per device.

```python
import math
import jax
import jax.numpy as jnp
import numpy as np
from jax import lax

D = 256
TOK_DEV = 256
NEG_DEV = 512
ROWS_DEV = 4096
TOKENS = 8192
ROWS = 131072
NEG = 4096
CAP = 32
N_GROUP = 4
N_MEMBER = 8
DEVICES = 32


def negative_table(key):
    owner_key = jax.random.fold_in(key, 501)
    local_key = jax.random.fold_in(key, 502)
    blocks = DEVICES

    def one_block(block_key):
        return jax.random.permutation(block_key, NEG_DEV) % DEVICES
    owners = jax.vmap(one_block)(jax.random.split(owner_key, blocks)).reshape(-1)
    locals_drawn = jax.random.randint(local_key, (blocks * NEG_DEV,), 0, ROWS_DEV)
    return (owners * ROWS_DEV + locals_drawn).astype(jnp.int32)


def table_rows(key, ids):
    base = jax.random.fold_in(key, 601)

    def one_row(item):
        row_key = jax.random.fold_in(base, item)
        return 0.2 * jax.random.normal(row_key, (D,), jnp.float32)
    return jax.vmap(one_row)(ids)


def draw_item_table(key, part):
    return table_rows(key, jnp.arange(ROWS, dtype=jnp.int32)).astype(jnp.float32)


def draw_negative_ids(key, part):
    return negative_table(key)


def draw_encoded(key, part):
    return jax.random.normal(jax.random.fold_in(key, 701), (TOKENS, D), jnp.float32)


def place_ends(drawn, own_key, low, largest):
    longest = drawn.shape.index(max(drawn.shape))
    spots = []
    for shift in (0, 1):
        where = [jax.random.randint(jax.random.fold_in(own_key, axis), (), 0, length) for axis, length in enumerate(drawn.shape)]
        where[longest] = (where[longest] + shift) % drawn.shape[longest]
        spots.append(tuple(where))
    return drawn.at[spots[0]].set(low).at[spots[1]].set(largest)


def rank_bounds(count, lean):
    weights = [(1 << 20) // math.isqrt(standing ** lean) + 1 for standing in range(1, count + 1)]
    width = 1 + sum(weights) // (1 << 30)
    return np.cumsum(np.array([max(1, weight // width) for weight in weights]))


def skewed_ids(stream_key, dims, count, skew):
    listing = rank_bounds(count, skew)
    ticket = jax.random.randint(jax.random.fold_in(stream_key, 1), dims, 0, int(listing[count - 1]))
    grade = jnp.searchsorted(jnp.asarray(listing, jnp.int32), ticket, side="right")
    return jax.random.permutation(jax.random.fold_in(stream_key, 2), count)[grade].astype(jnp.int32)


def shared_out(own_key, own, number, rows, amount, top, reach, skew):
    order = jax.random.permutation(own_key, amount)
    crowded, ordinary = load_shares(amount, rows * top, reach, skew, True), load_shares(amount, rows * top, reach, skew, False)
    places = jnp.arange(amount)

    def named(sizes, rotation):
        used = int((sizes > 0).sum())
        fixed = max(1, used // 4)
        moved = fixed + (places - fixed + rotation * (used - fixed)) % max(1, amount - fixed)
        return jnp.zeros((amount,), jnp.int32).at[order[jnp.where(places < fixed, places, moved)]].set(jnp.asarray(sizes, jnp.int32))

    sizes = jnp.where(number % 4 == 0, named(crowded, number // 4), named(ordinary, number - number // 4 - 1))
    mixed = jax.random.permutation(jax.random.fold_in(own, 3), amount)
    giver, taker = mixed[0:amount // 2 * 2:2], mixed[1:amount // 2 * 2:2]
    margin = jnp.minimum(sizes[giver] - 1, reach - sizes[taker]) // 2
    margin = jnp.where((giver == order[0]) | (taker == order[0]) | (sizes[taker] == 0), 0, jnp.maximum(margin, 0))
    moved = jax.random.randint(jax.random.fold_in(own, 4), (amount // 2,), 0, 1 << 20) % (margin + 1)
    sizes = sizes.at[giver].add(-moved).at[taker].add(moved)
    items = jnp.searchsorted(jnp.cumsum(sizes), jnp.arange(rows * top), side="right").astype(jnp.int32)
    table = items.reshape(top, rows).T
    table = table[jax.random.permutation(jax.random.fold_in(own, 1), rows)]
    rotation = jax.random.randint(jax.random.fold_in(own, 2), (rows, 1), 0, top)
    return jnp.take_along_axis(table, (jnp.arange(top)[None, :] + rotation) % top, axis=1)


def load_shares(amount, total, most, slope, full):
    portions = [(1 << 20) // math.isqrt(rank ** slope) + 1 for rank in range(1, amount + 1)]
    largest = most if full else min(most, max(-(-total // amount), total * portions[0] // sum(portions)))
    least = 1 if total - largest >= amount - 1 else 0
    given, rest = [largest] + [least] * (amount - 1), total - largest - least * (amount - 1)
    while rest > 0:
        candidates = [i for i in range(1, amount) if given[i] < largest] or [i for i in range(1, amount) if given[i] < most]
        pool, left = sum([portions[i] for i in candidates]), rest
        for i in candidates:
            more = min(most - given[i], max(1, left * portions[i] // pool), rest)
            given[i] = given[i] + more
            rest = rest - more
    return np.array(given)


def setup_inputs(seed: int = 0) -> dict:
    key_of = jax.random.split(jax.random.key(seed), 7)
    encoded = draw_encoded(jax.random.fold_in(key_of[6], 71), 0)
    item_table = draw_item_table(jax.random.fold_in(key_of[6], 71), 0)
    target_owner_keys = jax.random.split(jax.random.fold_in(key_of[2], 1), TOKENS // TOK_DEV)
    target_owner_turns = jax.random.permutation(jax.random.fold_in(key_of[2], 3), TOKENS // TOK_DEV)
    target_owner = jax.vmap(lambda own, number: shared_out(jax.random.fold_in(key_of[2], 2), own, number, TOK_DEV, DEVICES, 1, CAP, 2))(target_owner_keys, target_owner_turns).reshape((TOKENS, 1))
    target_local = place_ends(skewed_ids(key_of[3], (TOKENS,), ROWS_DEV, 2), jax.random.fold_in(key_of[3], 3), 0, ROWS_DEV - 1).astype(jnp.int32)
    negative_ids = draw_negative_ids(jax.random.fold_in(key_of[6], 71), 0)
    valid = place_ends((jax.random.randint(key_of[5], (TOKENS,), 0, 4) < 3).astype(jnp.int32), jax.random.fold_in(key_of[5], 1), 0, 1)
    return dict(encoded=encoded, item_table=item_table, target_owner=target_owner, target_local=target_local, negative_ids=negative_ids, valid=valid)


def contract_rows(left, right):
    return lax.dot_general(left, right, (((1,), (1,)), ((), ())), precision=lax.Precision.HIGHEST, preferred_element_type=jnp.float32)


def reference(encoded, item_table, target_owner, target_local, negative_ids, valid):
    devices = N_GROUP * N_MEMBER
    target = target_owner[:, 0] * ROWS_DEV + target_local
    enc_blocks = encoded.reshape(devices, TOK_DEV, D)
    tgt_blocks = target.reshape(devices, TOK_DEV)
    weights = valid.astype(jnp.float32).reshape(devices, TOK_DEV)
    neg_blocks = negative_ids.reshape(N_GROUP, NEG)

    def step(table_acc, device):
        queries = enc_blocks[device]
        weight = weights[device]
        chosen = neg_blocks[device // N_MEMBER]
        tgt_rows = item_table[tgt_blocks[device]]
        neg_rows = item_table[chosen]
        positive = jnp.sum(queries * tgt_rows, axis=1)
        score = contract_rows(queries, neg_rows)
        top = jnp.maximum(jnp.max(score, axis=1), positive)
        expo = jnp.exp(score - top[:, None])
        own_exp = jnp.exp(positive - top)
        total = jnp.sum(expo, axis=1) + own_exp
        prob = expo / total[:, None]
        own = own_exp / total
        pulled = jnp.dot(prob, neg_rows, precision=lax.Precision.HIGHEST, preferred_element_type=jnp.float32)
        enc_grad = weight[:, None] * ((own - 1.0)[:, None] * tgt_rows + pulled)
        neg_grad = lax.dot_general(weight[:, None] * prob, queries, (((0,), (0,)), ((), ())), precision=lax.Precision.HIGHEST, preferred_element_type=jnp.float32)
        tgt_grad = (weight * (own - 1.0))[:, None] * queries
        table_acc = table_acc.at[chosen].add(neg_grad)
        return table_acc, (enc_grad, tgt_grad)

    table_acc, (enc_grads, tgt_grads) = lax.scan(step, jnp.zeros((ROWS, D), jnp.float32), jnp.arange(devices, dtype=jnp.int32))
    table_acc = table_acc.at[target].add(tgt_grads.reshape(TOKENS, D))
    return enc_grads.reshape(TOKENS, D), table_acc
```

```python
import functools

import jax
import jax.numpy as jnp
from jax import lax
from jax.experimental import pallas as pl
from jax.experimental.pallas import tpu as pltpu
from jax.sharding import PartitionSpec as P

F32 = jnp.float32
BF16 = jnp.bfloat16
I32 = jnp.int32
LANES = 128
VMEM = pl.BlockSpec(memory_space=pltpu.VMEM)
SMEM = pl.BlockSpec(memory_space=pltpu.SMEM)
MIB = 1 << 20

NN = (((1,), (0,)), ((), ()))
NT = (((1,), (1,)), ((), ()))
TN = (((0,), (0,)), ((), ()))


def call(kernel, out_shape, ins, outs, args, scratch=(), limit=20, flops=0, moved=0, name=None):
    return pl.pallas_call(
        kernel,
        out_shape=out_shape,
        in_specs=ins,
        out_specs=outs,
        scratch_shapes=list(scratch),
        compiler_params=pltpu.CompilerParams(vmem_limit_bytes=limit * MIB),
        cost_estimate=pl.CostEstimate(flops=flops, bytes_accessed=moved, transcendentals=0),
        name=name,
    )(*args)


def iota(shape, dim):
    return lax.broadcasted_iota(I32, shape, dim)


def as_bf16(flag):
    return flag.astype(F32).astype(BF16)


def dot1(a, b, dims):
    return lax.dot_general(a, b, dims, preferred_element_type=F32)


def split(x):
    hi = x.astype(BF16)
    return hi, (x - hi.astype(F32)).astype(BF16)


def dot3(a, b, dims):
    return dot1(a[0], b[0], dims) + (dot1(a[0], b[1], dims) + dot1(a[1], b[0], dims))


def row_to_col(row):
    return jnp.transpose(jnp.broadcast_to(row, (LANES, row.shape[1])))[:, 0:1]


def bucket_kernel(members, rows_dev, slots, own_ref, loc_ref, neg_ref, out_ref):
    devices = out_ref.shape[0]
    shift = rows_dev.bit_length() - 1

    def ranks(owner_row, count):
        hot = iota((devices, count), 0) == owner_row
        before = as_bf16(iota((count, count), 0) < iota((count, count), 1))
        seen = dot1(as_bf16(hot), before, NN)
        return hot, jnp.sum(jnp.where(hot, seen, 0.0), axis=0, keepdims=True).astype(I32)

    def table(hot, value, place):
        return dot1(jnp.where(hot, value, 0.0).astype(BF16), place, NT)

    def placed(lane_row, count):
        return as_bf16(iota((LANES, count), 0) == lane_row)

    tokens = own_ref.shape[0]
    own_col = jnp.broadcast_to(own_ref[...].astype(F32), (tokens, LANES))
    owner = jnp.transpose(own_col)[0:1].astype(I32)
    hot, rank = ranks(owner, tokens)
    place = placed(rank, tokens)
    local = loc_ref[...]
    high = table(hot, (local >> 6).astype(F32), place)
    low = table(hot, (local & 63).astype(F32), place)
    group = owner // members
    hot_member = (iota((devices, tokens), 0) & (members - 1)) == (owner & (members - 1))
    position = table(
        hot_member, (iota((1, tokens), 1) + 1).astype(F32), placed(group * slots + rank, tokens)
    )

    negatives = neg_ref.shape[1]
    ids = neg_ref[...]
    hot, rank = ranks(ids >> shift, negatives)
    place = placed(rank + slots, negatives)
    local = ids & (rows_dev - 1)
    high = high + table(hot, (local >> 6).astype(F32), place)
    low = low + table(hot, (local & 63).astype(F32), place)
    out_ref[:, 0:LANES] = high.astype(I32) * 64 + low.astype(I32)
    out_ref[:, LANES:] = position.astype(I32)


def gather_kernel(members, first, count, info, got, table, *outs):
    for d, out in enumerate(outs):
        source = (info[0] ^ d) * members

        def member(mr, carry, out=out, source=source):
            for k in range(count):
                row = got[source + mr, first + k]
                out[pl.ds(mr * count + k, 1), :] = table[pl.ds(row, 1), :]
            return carry

        lax.fori_loop(0, members, member, 0)


def score_kernel(members, info, neg_ref, *refs):
    encs = refs[:members]
    stats, prob_hi, prob_lo, pulled = refs[members:]
    tokens = encs[0].shape[0]
    neg = neg_ref[...]
    neg_t = split(jnp.transpose(neg))
    for e in range(members):
        lanes = pl.ds(pl.multiple_of((info[1] ^ e) * tokens, LANES), tokens)
        score = lax.dot_general(
            neg, encs[e][...], NT, precision=lax.Precision.HIGHEST, preferred_element_type=F32
        )
        top = jnp.max(score, axis=0, keepdims=True)
        prob = jnp.exp(score - top)
        stats[0:1, lanes] = top
        stats[1:2, lanes] = jnp.sum(prob, axis=0, keepdims=True)
        parts = split(prob)
        prob_hi[e] = parts[0]
        prob_lo[e] = parts[1]
        pulled[e] = dot3(neg_t, parts, NN)


def pick_kernel(members, slots, info, got, *refs):
    encs = refs[:members]
    outs = refs[members:]
    for e in range(members):
        mr = info[1] ^ e
        row = info[0] * members + mr
        enc = encs[e]
        for d, out in enumerate(outs):
            lane = LANES + (info[0] ^ d) * slots
            for k in range(slots):
                at = jnp.maximum(got[row, lane + k] - 1, 0)
                out[pl.ds(mr * slots + k, 1), :] = enc[pl.ds(at, 1), :]


def own_places(members, info, got):
    return got[pl.ds(pl.multiple_of(info[0] * members, members), members), LANES:]


def positive_kernel(members, groups, slots, tokens, info, got, stats, *refs):
    targets = refs[:groups]
    picked = refs[groups : 2 * groups]
    joined, own, row_t, column, place_rows = refs[2 * groups :]
    place_rows[...] = own_places(members, info, got)
    for e in range(members):
        mr = info[1] ^ e
        lanes = pl.ds(pl.multiple_of(mr * tokens, LANES), tokens)
        column[...] = row_to_col(place_rows[pl.ds(mr, 1), :])
        positive = jnp.zeros((1, tokens), F32)
        has = jnp.zeros((1, tokens), F32)
        rows, hots = [], []
        at = pl.ds(pl.multiple_of(mr * slots, slots), slots)
        for d in range(groups):
            place = column[pl.ds(pl.multiple_of((info[0] ^ d) * slots, slots), slots), :]
            hot = place == iota((slots, tokens), 1) + 1
            row = targets[d][at, :]
            value = jnp.sum(row * picked[d][at, :], axis=1, keepdims=True)
            positive += jnp.sum(jnp.where(hot, value, 0.0), axis=0, keepdims=True)
            has += jnp.sum(hot.astype(F32), axis=0, keepdims=True)
            rows.append(row)
            hots.append(hot.astype(F32))
        hot = jnp.concatenate(hots, axis=0).astype(BF16)
        high, low = split(jnp.concatenate(rows, axis=0))
        row_t[e] = dot1(high, hot, TN) + dot1(low, hot, TN)
        old = stats[0:1, lanes]
        top = jnp.where(has > 0, jnp.maximum(old, positive), old)
        joined[0:1, lanes] = top
        joined[1:2, lanes] = stats[1:2, lanes] * jnp.exp(old - top) + jnp.where(
            has > 0, jnp.exp(positive - top), 0.0
        )
        own[0:1, lanes] = positive
        own[1:2, lanes] = has


def join(first, second):
    top = jnp.maximum(first[0:1], second[0:1])
    total = first[1:2] * jnp.exp(first[0:1] - top) + second[1:2] * jnp.exp(second[0:1] - top)
    return top, total


def join_kernel(first, second, out):
    top, total = join(first[...], second[...])
    out[0:1, :] = top
    out[1:2, :] = total


def shares(info, e, tokens, final, stats, own):
    lanes = pl.ds(pl.multiple_of((info[1] ^ e) * tokens, LANES), tokens)
    top, total = final[0:1, lanes], final[1:2, lanes]
    scale = jnp.exp(stats[0:1, lanes] - top) / total
    extra = jnp.where(
        own[1:2, lanes] > 0, jnp.exp(own[0:1, lanes] - top) / total - 1.0, 0.0
    )
    return scale, extra


def pull_kernel(members, tokens, info, final, stats, own, pulled, row_t, *outs):
    for e in range(members):
        scale, extra = shares(info, e, tokens, final, stats, own)
        outs[e][...] = pulled[e] * scale + row_t[e] * extra


def grad_kernel(members, groups, slots, info, got, final, stats, own, prob_hi, prob_lo, *refs):
    encs = refs[:members]
    outs = refs[members : members + groups]
    total, coef, place_rows = refs[members + groups :]
    place_rows[...] = own_places(members, info, got)
    tokens, width = encs[0].shape
    for e in range(members):
        mr = info[1] ^ e
        scale, extra = shares(info, e, tokens, final, stats, own)
        enc = split(encs[e][...] * row_to_col(scale))
        part = dot3((prob_hi[e], prob_lo[e]), enc, NN)
        if e == 0:
            total[...] = part
        else:
            total[...] += part
        hot = place_rows[pl.ds(mr, 1), :] == iota((tokens, LANES), 0) + 1
        coef[pl.ds(mr, 1), :] = jnp.sum(
            jnp.where(hot, row_to_col(extra), 0.0), axis=0, keepdims=True
        )
    count = total.shape[0] // groups
    for d in range(groups):
        outs[d][0:count, :] = total[d * count : (d + 1) * count, :]
        outs[d][count:, 0:LANES] = coef[...]
        outs[d][count:, LANES:] = jnp.zeros((members, width - LANES), F32)


def scatter_kernel(members, groups, slots, count, info, got, *refs):
    grads = refs[:groups]
    picked = refs[groups : 2 * groups]
    out, column, rows = refs[2 * groups :]
    out[...] = jnp.zeros_like(out)
    for d in range(groups):
        source = (info[0] ^ d) * members
        grad = grads[d]
        negatives = members * count
        coef = grad[negatives:, 0:LANES]
        column[...] = jnp.transpose(jnp.concatenate([coef] * (LANES // members), axis=0))
        mine = column[pl.ds(pl.multiple_of(info[0] * slots, slots), slots), :]
        for mr in range(members):
            at = slice(mr * slots, (mr + 1) * slots)
            rows[at, :] = picked[d][at, :] * mine[:, mr : mr + 1]

        def member(mr, carry, source=source, grad=grad):
            for k in range(count):
                row = got[source + mr, slots + k]
                out[pl.ds(row, 1), :] += grad[pl.ds(mr * count + k, 1), :]
            for k in range(slots):
                row = got[source + mr, k]
                out[pl.ds(row, 1), :] += rows[pl.ds(mr * slots + k, 1), :]
            return carry

        lax.fori_loop(0, members, member, 0)


def add_kernel(*refs):
    total = refs[0][...]
    for ref in refs[1:-1]:
        total = total + ref[...]
    refs[-1][...] = total


def finish_kernel(valid, *refs):
    total = refs[0][...]
    for ref in refs[1:-1]:
        total = total + ref[...]
    refs[-1][...] = jnp.transpose(total) * row_to_col(valid[...].astype(F32))


def swap(value, axis, d):
    return lax.ppermute(value, axis, [(i, i ^ d) for i in range(lax.axis_size(axis))])


def shards(encoded, item_table, target_owner, target_local, negative_ids, valid):
    groups, members = lax.axis_size("group"), lax.axis_size("member")
    devices = groups * members
    tokens, width = encoded.shape
    rows_dev = item_table.shape[0]
    negatives = negative_ids.shape[0]
    slots = max(2, 4 * tokens // devices)
    count = negatives // devices
    near = max(1, members // 4)
    everyone = members * tokens
    shape = jax.ShapeDtypeStruct
    sds = lambda *s: shape(s, F32)

    info = jnp.stack([lax.axis_index("group"), lax.axis_index("member")]).astype(I32)
    masked = encoded * valid.astype(F32)[:, None]

    far = range(0, members, near)
    encs = [None] * members
    for z in far:
        encs[z] = swap(masked, "member", z) if z else masked
    for z in far:
        for x in range(1, near):
            encs[z ^ x] = swap(encs[z], "member", x)

    request = call(
        functools.partial(bucket_kernel, members, rows_dev, slots),
        shape((devices, 2 * LANES), I32),
        [VMEM] * 3,
        VMEM,
        (target_owner, target_local.reshape(1, -1), negative_ids.reshape(1, -1)),
        name="bucket",
    )
    got = lax.all_to_all(
        request, ("group", "member"), split_axis=0, concat_axis=0, tiled=True
    )

    negs = call(
        functools.partial(gather_kernel, members, slots, count),
        [sds(members * count, width)] * groups,
        [SMEM, SMEM, VMEM],
        [VMEM] * groups,
        (info, got, item_table),
        name="gather_negatives",
    )
    negs = [negs[0]] + [swap(negs[d], "group", d) for d in range(1, groups)]
    tgts = call(
        functools.partial(gather_kernel, members, 0, slots),
        [sds(members * slots, width)] * groups,
        [SMEM, SMEM, VMEM],
        [VMEM] * groups,
        (info, got, item_table),
        name="gather_targets",
    )
    tgts = [tgts[0]] + [swap(tgts[d], "group", d) for d in range(1, groups)]

    neg_all = jnp.concatenate(negs, axis=0)
    stats, prob_hi, prob_lo, pulled = call(
        functools.partial(score_kernel, members),
        [
            sds(2, everyone),
            shape((members, negatives, tokens), BF16),
            shape((members, negatives, tokens), BF16),
            sds(members, width, tokens),
        ],
        [SMEM] + [VMEM] * (1 + members),
        [VMEM] * 4,
        (info, neg_all, *encs),
        flops=18 * everyone * negatives * width,
        moved=8 * MIB,
        name="score",
    )
    picked = call(
        functools.partial(pick_kernel, members, slots),
        [sds(members * slots, width)] * groups,
        [SMEM, SMEM] + [VMEM] * members,
        [VMEM] * groups,
        (info, got, *encs),
        name="pick",
    )
    joined, own, row_t = call(
        functools.partial(positive_kernel, members, groups, slots, tokens),
        [sds(2, everyone), sds(2, everyone), sds(members, width, tokens)],
        [SMEM] + [VMEM] * (2 + 2 * groups),
        [VMEM] * 3,
        (info, got, stats, *tgts, *picked),
        scratch=[pltpu.VMEM((LANES, 1), I32), pltpu.VMEM((members, LANES), I32)],
        name="positive",
    )
    sent = [picked[0]] + [swap(picked[d], "group", d) for d in range(1, groups)]

    final = joined
    d = 1
    while d < members:
        final = call(
            join_kernel,
            sds(2, everyone),
            [VMEM] * 2,
            VMEM,
            (final, swap(final, "member", d)),
            name="join",
        )
        d *= 2

    pulls = call(
        functools.partial(pull_kernel, members, tokens),
        [sds(width, tokens)] * members,
        [SMEM] + [VMEM] * 5,
        [VMEM] * members,
        (info, final, stats, own, pulled, row_t),
        name="pull",
    )
    parts = []
    for z in reversed(far):
        arrived = [swap(pulls[z ^ x], "member", x) for x in range(1, near)]
        total = pulls[z]
        if arrived:
            total = call(
                add_kernel,
                sds(width, tokens),
                [VMEM] * (1 + len(arrived)),
                VMEM,
                (total, *arrived),
                name="add",
            )
        parts.append(swap(total, "member", z) if z else total)

    grads = call(
        functools.partial(grad_kernel, members, groups, slots),
        [sds(members * count + members, width)] * groups,
        [SMEM] + [VMEM] * (6 + members),
        [VMEM] * groups,
        (info, got, final, stats, own, prob_hi, prob_lo, *encs),
        scratch=[
            pltpu.VMEM((negatives, width), F32),
            pltpu.VMEM((members, LANES), F32),
            pltpu.VMEM((members, LANES), I32),
        ],
        flops=6 * everyone * negatives * width,
        moved=8 * MIB,
        name="grad",
    )
    grads = [grads[0]] + [swap(grads[d], "group", d) for d in range(1, groups)]
    table_grad = call(
        functools.partial(scatter_kernel, members, groups, slots, count),
        sds(rows_dev, width),
        [SMEM, SMEM] + [VMEM] * (2 * groups),
        VMEM,
        (info, got, *grads, *sent),
        scratch=[pltpu.VMEM((LANES, LANES), F32), pltpu.VMEM((members * slots, width), F32)],
        name="scatter",
    )
    encoded_grad = call(
        finish_kernel,
        sds(tokens, width),
        [VMEM] * (1 + len(parts)),
        VMEM,
        (valid.reshape(1, -1), *parts),
        name="finish",
    )
    return (encoded_grad, table_grad)


def solution(mesh):
    placed = (
        P(("group", "member"), None),
        P(("group", "member"), None),
        P(("group", "member"), None),
        P(("group", "member")),
        P(("group", "member")),
        P(("group", "member")),
    )
    return jax.shard_map(
        shards,
        mesh=mesh,
        in_specs=placed,
        out_specs=(P(("group", "member"), None), P(("group", "member"), None)),
        check_vma=False,
    )
```

```python
import functools

import jax
import jax.numpy as jnp
from jax import lax
from jax.experimental import pallas as pl
from jax.experimental.pallas import tpu as pltpu
from jax.sharding import PartitionSpec as P

F32 = jnp.float32
BF16 = jnp.bfloat16
I32 = jnp.int32
LANES = 128
VMEM = pl.BlockSpec(memory_space=pltpu.VMEM)
ANY = pl.BlockSpec(memory_space=pl.ANY)
SMEM = pl.BlockSpec(memory_space=pltpu.SMEM)
MIB = 1 << 20
BATCH = 8

NN = (((1,), (0,)), ((), ()))
NT = (((1,), (1,)), ((), ()))
TN = (((0,), (0,)), ((), ()))


def call(kernel, out_shape, ins, outs, args, scratch=(), limit=10, flops=0, moved=0, name=None):
    return pl.pallas_call(
        kernel,
        out_shape=out_shape,
        in_specs=ins,
        out_specs=outs,
        scratch_shapes=list(scratch),
        compiler_params=pltpu.CompilerParams(vmem_limit_bytes=limit * MIB),
        cost_estimate=pl.CostEstimate(flops=flops, bytes_accessed=moved, transcendentals=0),
        name=name,
    )(*args)


def iota(shape, dim):
    return lax.broadcasted_iota(I32, shape, dim)


def as_bf16(flag):
    return flag.astype(F32).astype(BF16)


def dot1(a, b, dims):
    return lax.dot_general(a, b, dims, preferred_element_type=F32)


def split(x):
    hi = x.astype(BF16)
    return hi, (x - hi.astype(F32)).astype(BF16)


def dot3(a, b, dims):
    return dot1(a[0], b[0], dims) + (dot1(a[0], b[1], dims) + dot1(a[1], b[0], dims))


def row_to_col(row):
    return jnp.transpose(jnp.broadcast_to(row, (LANES, row.shape[1])))[:, 0:1]


def split3(x):
    hi = x.astype(BF16)
    rest = x - hi.astype(F32)
    mid = rest.astype(BF16)
    return hi, mid, (rest - mid.astype(F32)).astype(BF16)


def dot6(a, b, dims):
    small = dot1(a[2], b[0], dims) + dot1(a[1], b[1], dims) + dot1(a[0], b[2], dims)
    return (small + (dot1(a[1], b[0], dims) + dot1(a[0], b[1], dims))) + dot1(a[0], b[0], dims)


def copy_rows(source, row_of, target, base, count):
    for b in range(0, count, BATCH):
        rows = [source[pl.ds(row_of(b + k), 1), :] for k in range(BATCH)] if count % BATCH == 0 else None
        if rows is None:
            for k in range(count):
                target[pl.ds(base + k, 1), :] = source[pl.ds(row_of(k), 1), :]
            return
        target[pl.ds(pl.multiple_of(base + b, BATCH), BATCH), :] = jnp.concatenate(rows, axis=0)


def front_kernel(members, rows_dev, slots, tokens, negatives, info, ints, enc_ref, out_ref, masked_ref):
    devices = out_ref.shape[0]
    shift = rows_dev.bit_length() - 1
    owner = ints[:, 0:tokens]
    local = ints[:, tokens : 2 * tokens]
    valid = ints[:, 2 * tokens : 3 * tokens]
    ids = ints[:, 3 * tokens :]
    masked_ref[...] = enc_ref[...] * row_to_col(valid.astype(F32))

    def ranks(owner_row, count):
        hot = iota((devices, count), 0) == owner_row
        before = as_bf16(iota((count, count), 0) < iota((count, count), 1))
        seen = dot1(as_bf16(hot), before, NN)
        return hot, jnp.sum(jnp.where(hot, seen, 0.0), axis=0, keepdims=True).astype(I32)

    def table(hot, value, place):
        return dot1(jnp.where(hot, value, 0.0).astype(BF16), place, NT)

    def placed(lane_row, count):
        return as_bf16(iota((LANES, count), 0) == lane_row)

    hot, rank = ranks(owner, tokens)
    place = placed(rank, tokens)
    high = table(hot, (local >> 6).astype(F32), place)
    low = table(hot, (local & 63).astype(F32), place)
    group = owner >> (members.bit_length() - 1)
    hot_member = (iota((devices, tokens), 0) & (members - 1)) == (owner & (members - 1))
    position = table(
        hot_member, (iota((1, tokens), 1) + 1).astype(F32), placed(group * slots + rank, tokens)
    )

    hot, rank = ranks(ids >> shift, negatives)
    place = placed(rank + slots, negatives)
    local = ids & (rows_dev - 1)
    high = high + table(hot, (local >> 6).astype(F32), place)
    low = low + table(hot, (local & 63).astype(F32), place)
    out_ref[:, 0, 0:LANES] = high.astype(I32) * 64 + low.astype(I32)
    out_ref[:, 0, LANES:] = position.astype(I32)


def gather_kernel(members, groups, slots, count, info, got, table, *refs):
    for d, out in enumerate(refs[-groups:]):
        first = (info[0] ^ d) * members

        def member(mr, carry, out=out, first=first):
            asked = got.at[first + mr, 0]
            copy_rows(table, lambda k: asked[slots + k], out, mr * count, count)
            copy_rows(table, lambda k: asked[k], out, members * count + mr * slots, slots)
            return carry

        lax.fori_loop(0, members, member, 0)


def score_kernel(members, groups, negatives, info, *refs):
    rows, refs = refs[:groups], refs[groups:]
    encs = refs[:members]
    stats, prob_hi, prob_lo, pulled = refs[members:]
    tokens = encs[0].shape[0]
    neg = jnp.concatenate([row[0 : negatives // groups, :] for row in rows], axis=0)
    neg3 = split3(neg)
    neg_t = split(jnp.transpose(neg))
    for e in range(members):
        lanes = pl.ds(pl.multiple_of((info[1] ^ e) * tokens, LANES), tokens)
        score = dot6(neg3, split3(encs[e][...]), NT)
        top = jnp.max(score, axis=0, keepdims=True)
        prob = jnp.exp(score - top)
        stats[0:1, lanes] = top
        stats[1:2, lanes] = jnp.sum(prob, axis=0, keepdims=True)
        parts = split(prob)
        prob_hi[e] = parts[0]
        prob_lo[e] = parts[1]
        pulled[e] = dot3(neg_t, parts, NN)


def own_places(members, info, got):
    return got[pl.ds(info[0] * members, members), 0, LANES:]


def slot_hot(members, groups, slots, info, place_rows, column, mr, tokens):
    column[...] = row_to_col(place_rows[pl.ds(mr, 1), :])
    place = [
        column[pl.ds(pl.multiple_of((info[0] ^ d) * slots, slots), slots), :]
        for d in range(groups)
    ]
    return jnp.concatenate(place, axis=0) == iota((groups * slots, tokens), 1) + 1


def pick_kernel(members, groups, slots, info, got, *refs):
    encs = refs[:members]
    outs = refs[members : members + groups]
    place_rows, column = refs[members + groups :]
    place_rows[...] = own_places(members, info, got)
    for e in range(members):
        mr = info[1] ^ e
        tokens = encs[e].shape[0]
        hot = as_bf16(slot_hot(members, groups, slots, info, place_rows, column, mr, tokens))
        hi, mid, low = split3(encs[e][...])
        found = (dot1(hot, hi, NN) + dot1(hot, mid, NN)) + dot1(hot, low, NN)
        at = pl.ds(pl.multiple_of(mr * slots, slots), slots)
        for d in range(groups):
            outs[d][at, :] = found[d * slots : (d + 1) * slots]


def positive_kernel(members, groups, slots, tokens, info, got, stats, *refs):
    rows, picked = refs[:groups], refs[groups : 2 * groups]
    joined, own, row_t, place_rows, column = refs[2 * groups :]
    place_rows[...] = own_places(members, info, got)
    first = rows[0].shape[0] - members * slots
    for e in range(members):
        mr = info[1] ^ e
        lanes = pl.ds(pl.multiple_of(mr * tokens, LANES), tokens)
        at = pl.ds(pl.multiple_of(mr * slots, slots), slots)
        after = pl.ds(pl.multiple_of(first + mr * slots, slots), slots)
        hot = slot_hot(members, groups, slots, info, place_rows, column, mr, tokens)
        row = jnp.concatenate([r[after, :] for r in rows], axis=0)
        enc = jnp.concatenate([p[at, :] for p in picked], axis=0)
        value = jnp.sum(row * enc, axis=1, keepdims=True)
        positive = jnp.sum(jnp.where(hot, value, 0.0), axis=0, keepdims=True)
        has = jnp.sum(hot.astype(F32), axis=0, keepdims=True)
        high, low = split(row)
        row_t[e] = dot1(high, as_bf16(hot), TN) + dot1(low, as_bf16(hot), TN)
        old = stats[0:1, lanes]
        top = jnp.where(has > 0, jnp.maximum(old, positive), old)
        joined[0:1, lanes] = top
        joined[1:2, lanes] = stats[1:2, lanes] * jnp.exp(old - top) + jnp.where(
            has > 0, jnp.exp(positive - top), 0.0
        )
        own[0:1, lanes] = positive
        own[1:2, lanes] = has


def join(first, second):
    top = jnp.maximum(first[0:1], second[0:1])
    total = first[1:2] * jnp.exp(first[0:1] - top) + second[1:2] * jnp.exp(second[0:1] - top)
    return top, total


def join_kernel(first, second, *refs):
    out = refs[-1]
    top, total = join(first[...], second[...])
    out[0:1, :] = top
    out[1:2, :] = total


def shares(info, e, tokens, final, stats, own):
    lanes = pl.ds(pl.multiple_of((info[1] ^ e) * tokens, LANES), tokens)
    top, total = final[0:1, lanes], final[1:2, lanes]
    scale = jnp.exp(stats[0:1, lanes] - top) / total
    extra = jnp.where(
        own[1:2, lanes] > 0, jnp.exp(own[0:1, lanes] - top) / total - 1.0, 0.0
    )
    return scale, extra


def pull_kernel(members, tokens, info, final, stats, own, pulled, row_t, *outs):
    for e in range(members):
        scale, extra = shares(info, e, tokens, final, stats, own)
        outs[e][...] = pulled[e] * scale + row_t[e] * extra


def flat(table, lane, slots):
    return jnp.concatenate(
        [table[m : m + 1, lane : lane + slots] for m in range(table.shape[0])], axis=1
    )


def grad_kernel(members, groups, slots, info, got, final, stats, own, prob_hi, prob_lo, *refs):
    encs = refs[:members]
    out, total, coef, place_rows = refs[members:]
    place_rows[...] = own_places(members, info, got)
    tokens, width = encs[0].shape
    for e in range(members):
        mr = info[1] ^ e
        scale, extra = shares(info, e, tokens, final, stats, own)
        enc = split(encs[e][...] * row_to_col(scale))
        part = dot3((prob_hi[e], prob_lo[e]), enc, NN)
        if e == 0:
            total[...] = part
        else:
            total[...] += part
        hot = place_rows[pl.ds(mr, 1), :] == iota((tokens, LANES), 0) + 1
        coef[pl.ds(mr, 1), :] = jnp.sum(
            jnp.where(hot, row_to_col(extra), 0.0), axis=0, keepdims=True
        )
    count = total.shape[0] // groups
    for g in range(groups):
        out[info[0] ^ g, 0:count, :] = total[g * count : (g + 1) * count, :]
        line = flat(coef[...], g * slots, slots)
        out[g, count:, 0 : line.shape[1]] = jnp.broadcast_to(line, (8, line.shape[1]))


def equal_in_batch(ids):
    size = ids.shape[1]
    across = jnp.broadcast_to(ids.astype(F32), (size, size))
    same = (jnp.transpose(across) == across) & (
        (iota((size, size), 0) // BATCH) == (iota((size, size), 1) // BATCH)
    )
    return same.astype(F32)


def scatter_kernel(members, groups, slots, count, info, got_v, got, grads, *refs):
    picked = refs[:groups]
    out, negs, tgts = refs[groups:]
    out[...] = jnp.zeros_like(out)

    def add_rows(asked, first, source, base, number):
        for b in range(0, number, BATCH):
            rows = [asked[first + b + k] for k in range(BATCH)]
            new = [
                out[pl.ds(rows[k], 1), :] + source[pl.ds(base + b + k, 1), :]
                for k in range(BATCH)
            ]
            for k in range(BATCH):
                out[pl.ds(rows[k], 1), :] = new[k]

    for d in range(groups):
        g = info[0] ^ d
        asked = got_v[pl.ds(g * members, members), 0, 0:LANES]
        number = members * count
        same = as_bf16(equal_in_batch(flat(asked, slots, count)) > 0)
        high, low = split(grads[g, 0:number, :])
        negs[...] = dot1(same, high, NN) + dot1(same, low, NN)
        weight = equal_in_batch(flat(asked, 0, slots)) * grads[g, number : number + 1, 0 : members * slots]
        tgts[...] = dot3(split(weight), split(picked[d][...]), NN)
        merged = BATCH // count if count < BATCH else 1

        def member(step, carry, g=g, merged=merged):
            if merged == 1:
                add_rows(got.at[g * members + step, 0], slots, negs, step * count, count)
                add_rows(got.at[g * members + step, 0], 0, tgts, step * slots, slots)
                return carry
            first = g * members + step * merged
            rows = [
                got[first + k // count, 0, slots + k % count] for k in range(BATCH)
            ]
            new = [
                out[pl.ds(rows[k], 1), :] + negs[pl.ds(step * BATCH + k, 1), :]
                for k in range(BATCH)
            ]
            for k in range(BATCH):
                out[pl.ds(rows[k], 1), :] = new[k]
            for m in range(merged):
                add_rows(got.at[first + m, 0], 0, tgts, (step * merged + m) * slots, slots)
            return carry

        lax.fori_loop(0, members // merged, member, 0)


def add_kernel(*refs):
    total = refs[0][...]
    for ref in refs[1:-1]:
        total = total + ref[...]
    refs[-1][...] = total


def finish_kernel(valid, *refs):
    total = refs[0][...]
    for ref in refs[1:-1]:
        total = total + ref[...]
    refs[-1][...] = jnp.transpose(total) * row_to_col(valid[...].astype(F32))


def swap(value, axis, d):
    return lax.ppermute(value, axis, [(i, i ^ d) for i in range(lax.axis_size(axis))])


def shards(encoded, item_table, target_owner, target_local, negative_ids, valid):
    groups, members = lax.axis_size("group"), lax.axis_size("member")
    devices = groups * members
    tokens, width = encoded.shape
    rows_dev = item_table.shape[0]
    negatives = negative_ids.shape[0]
    slots = max(2, 4 * tokens // devices)
    count = negatives // devices
    near = max(1, members // 4)
    everyone = members * tokens
    shape = jax.ShapeDtypeStruct
    sds = lambda *s: shape(s, F32)

    info = jnp.stack([lax.axis_index("group"), lax.axis_index("member")]).astype(I32)
    ints = jnp.concatenate([target_owner.reshape(-1), target_local, valid, negative_ids])
    request, masked = call(
        functools.partial(front_kernel, members, rows_dev, slots, tokens, negatives),
        [shape((devices, 1, 2 * LANES), I32), sds(tokens, width)],
        [SMEM] + [VMEM] * 2,
        [VMEM] * 2,
        (info, ints.reshape(1, -1), encoded),
        name="front",
    )
    got = lax.all_to_all(
        request, ("group", "member"), split_axis=0, concat_axis=0, tiled=True
    )

    encs = [masked] + [None] * (members - 1)
    direct = [d for d in range(1, members) if d < 2 * near or d % near == 0]
    for d in direct:
        encs[d] = swap(masked, "member", d)
    for d in range(1, members):
        if d not in direct:
            encs[d] = swap(encs[d // near * near], "member", d % near)

    early = [encs[d] for d in direct]
    rows = call(
        functools.partial(gather_kernel, members, groups, slots, count),
        [sds(members * (count + slots), width)] * groups,
        [SMEM, SMEM, VMEM] + [ANY] * len(early),
        [VMEM] * groups,
        (info, got, item_table, *early),
        name="gather",
    )
    rows = [rows[0]] + [swap(rows[d], "group", d) for d in range(1, groups)]

    picked = call(
        functools.partial(pick_kernel, members, groups, slots),
        [sds(members * slots, width)] * groups,
        [SMEM] + [VMEM] * (1 + members),
        [VMEM] * groups,
        (info, got, *encs),
        scratch=[pltpu.VMEM((members, LANES), I32), pltpu.VMEM((LANES, 1), I32)],
        name="pick",
    )
    sent = [picked[0]] + [swap(picked[d], "group", d) for d in range(1, groups)]
    stats, prob_hi, prob_lo, pulled = call(
        functools.partial(score_kernel, members, groups, negatives),
        [
            sds(2, everyone),
            shape((members, negatives, tokens), BF16),
            shape((members, negatives, tokens), BF16),
            sds(members, width, tokens),
        ],
        [SMEM] + [VMEM] * (groups + members),
        [VMEM] * 4,
        (info, *rows, *encs),
        flops=18 * everyone * negatives * width,
        moved=8 * MIB,
        name="score",
    )
    joined, own, row_t = call(
        functools.partial(positive_kernel, members, groups, slots, tokens),
        [sds(2, everyone), sds(2, everyone), sds(members, width, tokens)],
        [SMEM] + [VMEM] * (2 + 2 * groups),
        [VMEM] * 3,
        (info, got, stats, *rows, *picked),
        scratch=[pltpu.VMEM((members, LANES), I32), pltpu.VMEM((LANES, 1), I32)],
        name="positive",
    )

    final = joined
    d = 1
    while d < members:
        late = sent[1:] if 2 * d == members else []
        final = call(
            join_kernel,
            sds(2, everyone),
            [VMEM] * 2 + [ANY] * len(late),
            VMEM,
            (final, swap(final, "member", d), *late),
            name="join",
        )
        d *= 2

    pulls = call(
        functools.partial(pull_kernel, members, tokens),
        [sds(width, tokens)] * members,
        [SMEM] + [VMEM] * 5,
        [VMEM] * members,
        (info, final, stats, own, pulled, row_t),
        name="pull",
    )
    parts = []
    for z in [*range(members - near, near, -near), 0]:
        arrived = [swap(pulls[z ^ x], "member", x) for x in range(1, near)]
        total = call(
            add_kernel,
            sds(width, tokens),
            [VMEM] * near,
            VMEM,
            (pulls[z], *arrived),
            name="add",
        )
        parts.append(swap(total, "member", z) if z else total)
    parts += [swap(pulls[d], "member", d) for d in range(near, 2 * near)]

    grads = call(
        functools.partial(grad_kernel, members, groups, slots),
        sds(groups, members * count + 8, width),
        [SMEM] + [VMEM] * (6 + members),
        VMEM,
        (info, got, final, stats, own, prob_hi, prob_lo, *encs),
        scratch=[
            pltpu.VMEM((negatives, width), F32),
            pltpu.VMEM((members, LANES), F32),
            pltpu.VMEM((members, LANES), I32),
        ],
        flops=6 * everyone * negatives * width,
        moved=8 * MIB,
        name="grad",
    )
    grads = lax.all_to_all(grads, "group", split_axis=0, concat_axis=0, tiled=True)
    table_grad = call(
        functools.partial(scatter_kernel, members, groups, slots, count),
        sds(rows_dev, width),
        [SMEM, VMEM, SMEM, VMEM] + [VMEM] * groups,
        VMEM,
        (info, got, got, grads, *sent),
        scratch=[
            pltpu.VMEM((members * count, width), F32),
            pltpu.VMEM((members * slots, width), F32),
        ],
        name="scatter",
    )
    encoded_grad = call(
        finish_kernel,
        sds(tokens, width),
        [VMEM] * (1 + len(parts)),
        VMEM,
        (valid.reshape(1, -1), *parts),
        name="finish",
    )
    return (encoded_grad, table_grad)


def solution(mesh):
    placed = (
        P(("group", "member"), None),
        P(("group", "member"), None),
        P(("group", "member"), None),
        P(("group", "member")),
        P(("group", "member")),
        P(("group", "member")),
    )
    return jax.shard_map(
        shards,
        mesh=mesh,
        in_specs=placed,
        out_specs=(P(("group", "member"), None), P(("group", "member"), None)),
        check_vma=False,
    )
```

```python
import functools

import jax
import jax.numpy as jnp
from jax import lax
from jax.experimental import pallas as pl
from jax.experimental.pallas import tpu as pltpu
from jax.sharding import PartitionSpec as P

F32 = jnp.float32
BF16 = jnp.bfloat16
I32 = jnp.int32
LANES = 128
VMEM = pl.BlockSpec(memory_space=pltpu.VMEM)
ANY = pl.BlockSpec(memory_space=pl.ANY)
SMEM = pl.BlockSpec(memory_space=pltpu.SMEM)
MIB = 1 << 20
BATCH = 8

NN = (((1,), (0,)), ((), ()))
NT = (((1,), (1,)), ((), ()))
TN = (((0,), (0,)), ((), ()))


def call(kernel, out_shape, ins, outs, args, scratch=(), limit=10, flops=0, moved=0, name=None):
    return pl.pallas_call(
        kernel,
        out_shape=out_shape,
        in_specs=ins,
        out_specs=outs,
        scratch_shapes=list(scratch),
        compiler_params=pltpu.CompilerParams(vmem_limit_bytes=limit * MIB),
        cost_estimate=pl.CostEstimate(flops=flops, bytes_accessed=moved, transcendentals=0),
        name=name,
    )(*args)


def iota(shape, dim):
    return lax.broadcasted_iota(I32, shape, dim)


def as_bf16(flag):
    return flag.astype(F32).astype(BF16)


def dot1(a, b, dims):
    return lax.dot_general(a, b, dims, preferred_element_type=F32)


def split(x):
    hi = x.astype(BF16)
    return hi, (x - hi.astype(F32)).astype(BF16)


def dot3(a, b, dims):
    return dot1(a[0], b[0], dims) + (dot1(a[0], b[1], dims) + dot1(a[1], b[0], dims))


def row_to_col(row):
    return jnp.transpose(jnp.broadcast_to(row, (LANES, row.shape[1])))[:, 0:1]


def split3(x):
    hi = x.astype(BF16)
    rest = x - hi.astype(F32)
    mid = rest.astype(BF16)
    return hi, mid, (rest - mid.astype(F32)).astype(BF16)


def dot6(a, b, dims):
    small = dot1(a[2], b[0], dims) + dot1(a[1], b[1], dims) + dot1(a[0], b[2], dims)
    return (small + (dot1(a[1], b[0], dims) + dot1(a[0], b[1], dims))) + dot1(a[0], b[0], dims)


def copy_rows(source, row_of, target, base, count):
    for b in range(0, count, BATCH):
        rows = [source[pl.ds(row_of(b + k), 1), :] for k in range(BATCH)] if count % BATCH == 0 else None
        if rows is None:
            for k in range(count):
                target[pl.ds(base + k, 1), :] = source[pl.ds(row_of(k), 1), :]
            return
        target[pl.ds(pl.multiple_of(base + b, BATCH), BATCH), :] = jnp.concatenate(rows, axis=0)


def front_kernel(members, rows_dev, slots, tokens, negatives, info, ints, enc_ref, out_ref, masked_ref):
    devices = out_ref.shape[0]
    shift = rows_dev.bit_length() - 1
    owner = ints[:, 0:tokens]
    local = ints[:, tokens : 2 * tokens]
    valid = ints[:, 2 * tokens : 3 * tokens]
    ids = ints[:, 3 * tokens :]
    masked_ref[...] = enc_ref[...] * row_to_col(valid.astype(F32))

    def ranks(owner_row, count):
        hot = iota((devices, count), 0) == owner_row
        before = as_bf16(iota((count, count), 0) < iota((count, count), 1))
        seen = dot1(as_bf16(hot), before, NN)
        return hot, jnp.sum(jnp.where(hot, seen, 0.0), axis=0, keepdims=True).astype(I32)

    def table(hot, value, place):
        return dot1(jnp.where(hot, value, 0.0).astype(BF16), place, NT)

    def placed(lane_row, count):
        return as_bf16(iota((LANES, count), 0) == lane_row)

    hot, rank = ranks(owner, tokens)
    place = placed(rank, tokens)
    high = table(hot, (local >> 6).astype(F32), place)
    low = table(hot, (local & 63).astype(F32), place)
    group = owner >> (members.bit_length() - 1)
    hot_member = (iota((devices, tokens), 0) & (members - 1)) == (owner & (members - 1))
    position = table(
        hot_member, (iota((1, tokens), 1) + 1).astype(F32), placed(group * slots + rank, tokens)
    )

    hot, rank = ranks(ids >> shift, negatives)
    place = placed(rank + slots, negatives)
    local = ids & (rows_dev - 1)
    high = high + table(hot, (local >> 6).astype(F32), place)
    low = low + table(hot, (local & 63).astype(F32), place)
    out_ref[:, 0, 0:LANES] = high.astype(I32) * 64 + low.astype(I32)
    out_ref[:, 0, LANES:] = position.astype(I32)


def gather_kernel(members, groups, part, count, info, got, table, *refs):
    for d, out in enumerate(refs[-groups:]):
        first = (info[0] ^ d) * members

        def member(mr, carry, out=out, first=first):
            asked = got.at[first + mr, 0]
            copy_rows(table, lambda k: asked[part + k], out, mr * count, count)
            return carry

        lax.fori_loop(0, members, member, 0)


def score_kernel(blocks, groups, info, *refs):
    rows, refs = refs[:groups], refs[groups:]
    encs, refs = refs[: len(blocks)], refs[len(blocks) :]
    stats, prob_hi, prob_lo = refs[-3:]
    if len(refs) > 3:
        stats[...] = refs[0][...]
    tokens = encs[0].shape[0]
    neg = split3(jnp.concatenate([row[...] for row in rows], axis=0))
    for i, e in enumerate(blocks):
        lanes = pl.ds(pl.multiple_of((info[1] ^ e) * tokens, LANES), tokens)
        score = dot6(neg, split3(encs[i][...]), NT)
        top = jnp.max(score, axis=0, keepdims=True)
        prob = jnp.exp(score - top)
        stats[0:1, lanes] = top
        stats[1:2, lanes] = jnp.sum(prob, axis=0, keepdims=True)
        parts = split(prob)
        prob_hi[i] = parts[0]
        prob_lo[i] = parts[1]


def own_places(members, info, got):
    return got[pl.ds(info[0] * members, members), 0, LANES:]


def slot_hot(members, groups, slots, info, place_rows, column, mr, tokens):
    column[...] = row_to_col(place_rows[pl.ds(mr, 1), :])
    place = [
        column[pl.ds(pl.multiple_of((info[0] ^ d) * slots, slots), slots), :]
        for d in range(groups)
    ]
    return jnp.concatenate(place, axis=0) == iota((groups * slots, tokens), 1) + 1


def pick_kernel(members, groups, slots, info, got, *refs):
    encs = refs[:members]
    outs = refs[members : members + groups]
    place_rows, column = refs[members + groups :]
    place_rows[...] = own_places(members, info, got)
    for e in range(members):
        mr = info[1] ^ e
        tokens = encs[e].shape[0]
        hot = as_bf16(slot_hot(members, groups, slots, info, place_rows, column, mr, tokens))
        hi, mid, low = split3(encs[e][...])
        found = (dot1(hot, hi, NN) + dot1(hot, mid, NN)) + dot1(hot, low, NN)
        at = pl.ds(pl.multiple_of(mr * slots, slots), slots)
        for d in range(groups):
            outs[d][at, :] = found[d * slots : (d + 1) * slots]


def positive_kernel(members, groups, slots, tokens, info, got, stats, *refs):
    rows, picked = refs[:groups], refs[groups : 2 * groups]
    joined, own, place_rows, column = refs[2 * groups :]
    place_rows[...] = own_places(members, info, got)
    for e in range(members):
        mr = info[1] ^ e
        lanes = pl.ds(pl.multiple_of(mr * tokens, LANES), tokens)
        at = pl.ds(pl.multiple_of(mr * slots, slots), slots)
        hot = slot_hot(members, groups, slots, info, place_rows, column, mr, tokens)
        row = jnp.concatenate([r[at, :] for r in rows], axis=0)
        enc = jnp.concatenate([p[at, :] for p in picked], axis=0)
        value = jnp.sum(row * enc, axis=1, keepdims=True)
        positive = jnp.sum(jnp.where(hot, value, 0.0), axis=0, keepdims=True)
        has = jnp.sum(hot.astype(F32), axis=0, keepdims=True)
        old = stats[0:1, lanes]
        top = jnp.where(has > 0, jnp.maximum(old, positive), old)
        joined[0:1, lanes] = top
        joined[1:2, lanes] = stats[1:2, lanes] * jnp.exp(old - top) + jnp.where(
            has > 0, jnp.exp(positive - top), 0.0
        )
        own[0:1, lanes] = positive
        own[1:2, lanes] = has


def pulled_kernel(members, groups, slots, halves, info, got, *refs):
    negs, refs = refs[:groups], refs[groups:]
    rows, refs = refs[:groups], refs[groups:]
    probs, (pulled, row_t, place_rows, column) = refs[:-4], refs[-4:]
    place_rows[...] = own_places(members, info, got)
    neg = jnp.concatenate([row[...] for row in negs], axis=0)
    neg_t = split(jnp.transpose(neg))
    tokens = pulled.shape[2]
    for h, blocks in enumerate(halves):
        for i, e in enumerate(blocks):
            mr = info[1] ^ e
            pulled[e] = dot3(neg_t, (probs[2 * h][i], probs[2 * h + 1][i]), NN)
            at = pl.ds(pl.multiple_of(mr * slots, slots), slots)
            hot = slot_hot(members, groups, slots, info, place_rows, column, mr, tokens)
            high, low = split(jnp.concatenate([r[at, :] for r in rows], axis=0))
            row_t[e] = dot1(high, as_bf16(hot), TN) + dot1(low, as_bf16(hot), TN)


def join(first, second):
    top = jnp.maximum(first[0:1], second[0:1])
    total = first[1:2] * jnp.exp(first[0:1] - top) + second[1:2] * jnp.exp(second[0:1] - top)
    return top, total


def join_kernel(first, second, *refs):
    out = refs[-1]
    top, total = join(first[...], second[...])
    out[0:1, :] = top
    out[1:2, :] = total


def shares(info, e, tokens, final, stats, own):
    lanes = pl.ds(pl.multiple_of((info[1] ^ e) * tokens, LANES), tokens)
    top, total = final[0:1, lanes], final[1:2, lanes]
    scale = jnp.exp(stats[0:1, lanes] - top) / total
    extra = jnp.where(
        own[1:2, lanes] > 0, jnp.exp(own[0:1, lanes] - top) / total - 1.0, 0.0
    )
    return scale, extra


def pull_kernel(members, tokens, info, final, stats, own, pulled, row_t, *outs):
    for e in range(members):
        scale, extra = shares(info, e, tokens, final, stats, own)
        outs[e][...] = pulled[e] * scale + row_t[e] * extra


def flat(table, lane, slots):
    return jnp.concatenate(
        [table[m : m + 1, lane : lane + slots] for m in range(table.shape[0])], axis=1
    )


def grad_kernel(members, groups, slots, halves, info, got, final, stats, own, *refs):
    probs, refs = refs[: 2 * len(halves)], refs[2 * len(halves) :]
    encs = refs[:members]
    out, total, coef, place_rows = refs[members:]
    place_rows[...] = own_places(members, info, got)
    tokens, width = encs[0].shape
    for h, i, e in [(h, i, e) for h, blocks in enumerate(halves) for i, e in enumerate(blocks)]:
        mr = info[1] ^ e
        scale, extra = shares(info, e, tokens, final, stats, own)
        enc = split(encs[e][...] * row_to_col(scale))
        part = dot3((probs[2 * h][i], probs[2 * h + 1][i]), enc, NN)
        if h == 0 and i == 0:
            total[...] = part
        else:
            total[...] += part
        hot = place_rows[pl.ds(mr, 1), :] == iota((tokens, LANES), 0) + 1
        coef[pl.ds(mr, 1), :] = jnp.sum(
            jnp.where(hot, row_to_col(extra), 0.0), axis=0, keepdims=True
        )
    count = total.shape[0] // groups
    for g in range(groups):
        out[info[0] ^ g, 0:count, :] = total[g * count : (g + 1) * count, :]
        line = flat(coef[...], g * slots, slots)
        out[g, count:, 0 : line.shape[1]] = jnp.broadcast_to(line, (8, line.shape[1]))


def equal_in_batch(ids):
    size = ids.shape[1]
    across = jnp.broadcast_to(ids.astype(F32), (size, size))
    same = (jnp.transpose(across) == across) & (
        (iota((size, size), 0) // BATCH) == (iota((size, size), 1) // BATCH)
    )
    return same.astype(F32)


def scatter_kernel(members, groups, slots, count, info, got_v, got, grads, *refs):
    picked = refs[:groups]
    out, negs, tgts = refs[groups:]
    out[...] = jnp.zeros_like(out)

    def add_rows(asked, first, source, base, number):
        for b in range(0, number, BATCH):
            rows = [asked[first + b + k] for k in range(BATCH)]
            new = [
                out[pl.ds(rows[k], 1), :] + source[pl.ds(base + b + k, 1), :]
                for k in range(BATCH)
            ]
            for k in range(BATCH):
                out[pl.ds(rows[k], 1), :] = new[k]

    for d in range(groups):
        g = info[0] ^ d
        asked = got_v[pl.ds(g * members, members), 0, 0:LANES]
        number = members * count
        same = as_bf16(equal_in_batch(flat(asked, slots, count)) > 0)
        high, low = split(grads[g, 0:number, :])
        negs[...] = dot1(same, high, NN) + dot1(same, low, NN)
        weight = equal_in_batch(flat(asked, 0, slots)) * grads[g, number : number + 1, 0 : members * slots]
        tgts[...] = dot3(split(weight), split(picked[d][...]), NN)
        merged = BATCH // count if count < BATCH else 1

        def member(step, carry, g=g, merged=merged):
            if merged == 1:
                add_rows(got.at[g * members + step, 0], slots, negs, step * count, count)
                add_rows(got.at[g * members + step, 0], 0, tgts, step * slots, slots)
                return carry
            first = g * members + step * merged
            rows = [
                got[first + k // count, 0, slots + k % count] for k in range(BATCH)
            ]
            new = [
                out[pl.ds(rows[k], 1), :] + negs[pl.ds(step * BATCH + k, 1), :]
                for k in range(BATCH)
            ]
            for k in range(BATCH):
                out[pl.ds(rows[k], 1), :] = new[k]
            for m in range(merged):
                add_rows(got.at[first + m, 0], 0, tgts, (step * merged + m) * slots, slots)
            return carry

        lax.fori_loop(0, members // merged, member, 0)


def add_kernel(*refs):
    total = refs[0][...]
    for ref in refs[1:-1]:
        total = total + ref[...]
    refs[-1][...] = total


def finish_kernel(valid, *refs):
    total = refs[0][...]
    for ref in refs[1:-1]:
        total = total + ref[...]
    refs[-1][...] = jnp.transpose(total) * row_to_col(valid[...].astype(F32))


def swap(value, axis, d):
    return lax.ppermute(value, axis, [(i, i ^ d) for i in range(lax.axis_size(axis))])


def shards(encoded, item_table, target_owner, target_local, negative_ids, valid):
    groups, members = lax.axis_size("group"), lax.axis_size("member")
    devices = groups * members
    tokens, width = encoded.shape
    rows_dev = item_table.shape[0]
    negatives = negative_ids.shape[0]
    slots = max(2, 4 * tokens // devices)
    count = negatives // devices
    near = max(1, members // 4)
    everyone = members * tokens
    shape = jax.ShapeDtypeStruct
    sds = lambda *s: shape(s, F32)

    info = jnp.stack([lax.axis_index("group"), lax.axis_index("member")]).astype(I32)
    ints = jnp.concatenate([target_owner.reshape(-1), target_local, valid, negative_ids])
    request, masked = call(
        functools.partial(front_kernel, members, rows_dev, slots, tokens, negatives),
        [shape((devices, 1, 2 * LANES), I32), sds(tokens, width)],
        [SMEM] + [VMEM] * 2,
        [VMEM] * 2,
        (info, ints.reshape(1, -1), encoded),
        name="front",
    )
    got = lax.all_to_all(
        request, ("group", "member"), split_axis=0, concat_axis=0, tiled=True
    )

    encs = [masked] + [None] * (members - 1)
    for z in range(near, members, near):
        known = 2 * near if z == 3 * near else 0
        encs[z] = swap(encs[known], "member", z ^ known)
    for z in range(0, members, near):
        for x in range(1, near):
            encs[z ^ x] = swap(encs[z], "member", x)
    halves = [[d for d in range(members) if (d < near) or d in (near, 2 * near)], []]
    halves[1] = [d for d in range(members) if d not in halves[0]]

    early = [encs[d] for d in halves[0] if d]
    gather = lambda part, many, deps, name: call(
        functools.partial(gather_kernel, members, groups, part, many),
        [sds(members * many, width)] * groups,
        [SMEM, SMEM, VMEM] + [ANY] * len(deps),
        [VMEM] * groups,
        (info, got, item_table, *deps),
        name=name,
    )
    negs = gather(slots, count, early, "gather_negatives")
    negs = [negs[0]] + [swap(negs[d], "group", d) for d in range(1, groups)]
    rows = gather(0, slots, [], "gather_targets")
    rows = [rows[0]] + [swap(rows[d], "group", d) for d in range(1, groups)]

    stats, probs = [], []
    for blocks in halves:
        many = len(blocks)
        *stats, hi, lo = call(
            functools.partial(score_kernel, blocks, groups),
            [sds(2, everyone)] + [shape((many, negatives, tokens), BF16)] * 2,
            [SMEM] + [VMEM] * (groups + many + len(stats)),
            [VMEM] * 3,
            (info, *negs, *[encs[e] for e in blocks], *stats),
            flops=12 * many * tokens * negatives * width,
            moved=MIB,
            name="score",
        )
        probs += [hi, lo]
    stats = stats[0]
    picked = call(
        functools.partial(pick_kernel, members, groups, slots),
        [sds(members * slots, width)] * groups,
        [SMEM] + [VMEM] * (1 + members),
        [VMEM] * groups,
        (info, got, *encs),
        scratch=[pltpu.VMEM((members, LANES), I32), pltpu.VMEM((LANES, 1), I32)],
        name="pick",
    )
    sent = [picked[0]] + [swap(picked[d], "group", d) for d in range(1, groups)]
    joined, own = call(
        functools.partial(positive_kernel, members, groups, slots, tokens),
        [sds(2, everyone)] * 2,
        [SMEM] + [VMEM] * (2 + 2 * groups),
        [VMEM] * 2,
        (info, got, stats, *rows, *picked),
        scratch=[pltpu.VMEM((members, LANES), I32), pltpu.VMEM((LANES, 1), I32)],
        name="positive",
    )
    pulled, row_t = call(
        functools.partial(pulled_kernel, members, groups, slots, halves),
        [sds(members, width, tokens)] * 2,
        [SMEM] + [VMEM] * (1 + 2 * groups + len(probs)),
        [VMEM] * 2,
        (info, got, *negs, *rows, *probs),
        scratch=[pltpu.VMEM((members, LANES), I32), pltpu.VMEM((LANES, 1), I32)],
        flops=6 * everyone * negatives * width,
        moved=MIB,
        name="pulled",
    )

    final = joined
    d = 1
    while d < members:
        late = sent[1:] if 2 * d == members else []
        final = call(
            join_kernel,
            sds(2, everyone),
            [VMEM] * 2 + [ANY] * len(late),
            VMEM,
            (final, swap(final, "member", d), *late),
            name="join",
        )
        d *= 2

    pulls = call(
        functools.partial(pull_kernel, members, tokens),
        [sds(width, tokens)] * members,
        [SMEM] + [VMEM] * 5,
        [VMEM] * members,
        (info, final, stats, own, pulled, row_t),
        name="pull",
    )
    def added(*terms):
        if len(terms) == 1:
            return terms[0]
        return call(
            add_kernel, sds(width, tokens), [VMEM] * len(terms), VMEM, terms, name="add"
        )

    sums = {}
    for z in [*range(members - near, 0, -near), 0]:
        arrived = [swap(pulls[z ^ x], "member", x) for x in range(1, near)]
        if z == 2 * near and 3 * near in sums:
            arrived.append(swap(sums.pop(3 * near), "member", near))
        sums[z] = added(pulls[z], *arrived)
    parts = [swap(total, "member", z) if z else total for z, total in sums.items()]

    grads = call(
        functools.partial(grad_kernel, members, groups, slots, halves),
        sds(groups, members * count + 8, width),
        [SMEM] + [VMEM] * (4 + len(probs) + members),
        VMEM,
        (info, got, final, stats, own, *probs, *encs),
        scratch=[
            pltpu.VMEM((negatives, width), F32),
            pltpu.VMEM((members, LANES), F32),
            pltpu.VMEM((members, LANES), I32),
        ],
        flops=6 * everyone * negatives * width,
        moved=8 * MIB,
        name="grad",
    )
    grads = lax.all_to_all(grads, "group", split_axis=0, concat_axis=0, tiled=True)
    table_grad = call(
        functools.partial(scatter_kernel, members, groups, slots, count),
        sds(rows_dev, width),
        [SMEM, VMEM, SMEM, VMEM] + [VMEM] * groups,
        VMEM,
        (info, got, got, grads, *sent),
        scratch=[
            pltpu.VMEM((members * count, width), F32),
            pltpu.VMEM((members * slots, width), F32),
        ],
        name="scatter",
    )
    encoded_grad = call(
        finish_kernel,
        sds(tokens, width),
        [VMEM] * (1 + len(parts)),
        VMEM,
        (valid.reshape(1, -1), *parts),
        name="finish",
    )
    return (encoded_grad, table_grad)


def solution(mesh):
    placed = (
        P(("group", "member"), None),
        P(("group", "member"), None),
        P(("group", "member"), None),
        P(("group", "member")),
        P(("group", "member")),
        P(("group", "member")),
    )
    return jax.shard_map(
        shards,
        mesh=mesh,
        in_specs=placed,
        out_specs=(P(("group", "member"), None), P(("group", "member"), None)),
        check_vma=False,
    )
```

```python
import functools

import jax
import jax.numpy as jnp
from jax import lax
from jax.experimental import pallas as pl
from jax.experimental.pallas import tpu as pltpu
from jax.sharding import PartitionSpec as P

F32 = jnp.float32
BF16 = jnp.bfloat16
I32 = jnp.int32
LANES = 128
VMEM = pl.BlockSpec(memory_space=pltpu.VMEM)
ANY = pl.BlockSpec(memory_space=pl.ANY)
SMEM = pl.BlockSpec(memory_space=pltpu.SMEM)
MIB = 1 << 20
BATCH = 8

NN = (((1,), (0,)), ((), ()))
NT = (((1,), (1,)), ((), ()))
TN = (((0,), (0,)), ((), ()))


def call(kernel, out_shape, ins, outs, args, scratch=(), limit=10, flops=0, moved=0, name=None):
    return pl.pallas_call(
        kernel,
        out_shape=out_shape,
        in_specs=ins,
        out_specs=outs,
        scratch_shapes=list(scratch),
        compiler_params=pltpu.CompilerParams(vmem_limit_bytes=limit * MIB),
        cost_estimate=pl.CostEstimate(flops=flops, bytes_accessed=moved, transcendentals=0),
        name=name,
    )(*args)


def iota(shape, dim):
    return lax.broadcasted_iota(I32, shape, dim)


def as_bf16(flag):
    return flag.astype(F32).astype(BF16)


def dot1(a, b, dims):
    return lax.dot_general(a, b, dims, preferred_element_type=F32)


def split(x):
    hi = x.astype(BF16)
    return hi, (x - hi.astype(F32)).astype(BF16)


def dot3(a, b, dims):
    return dot1(a[0], b[0], dims) + (dot1(a[0], b[1], dims) + dot1(a[1], b[0], dims))


def row_to_col(row):
    return jnp.transpose(jnp.broadcast_to(row, (LANES, row.shape[1])))[:, 0:1]


def split3(x):
    hi = x.astype(BF16)
    rest = x - hi.astype(F32)
    mid = rest.astype(BF16)
    return hi, mid, (rest - mid.astype(F32)).astype(BF16)


def dot6(a, b, dims):
    small = dot1(a[2], b[0], dims) + dot1(a[1], b[1], dims) + dot1(a[0], b[2], dims)
    return (small + (dot1(a[1], b[0], dims) + dot1(a[0], b[1], dims))) + dot1(a[0], b[0], dims)


def copy_rows(source, row_of, target, base, count):
    for b in range(0, count, BATCH):
        rows = [source[pl.ds(row_of(b + k), 1), :] for k in range(BATCH)] if count % BATCH == 0 else None
        if rows is None:
            for k in range(count):
                target[pl.ds(base + k, 1), :] = source[pl.ds(row_of(k), 1), :]
            return
        target[pl.ds(pl.multiple_of(base + b, BATCH), BATCH), :] = jnp.concatenate(rows, axis=0)


def front_kernel(members, rows_dev, slots, tokens, negatives, info, ints, enc_ref, out_ref, masked_ref):
    devices = out_ref.shape[0]
    shift = rows_dev.bit_length() - 1
    owner = ints[:, 0:tokens]
    local = ints[:, tokens : 2 * tokens]
    valid = ints[:, 2 * tokens : 3 * tokens]
    ids = ints[:, 3 * tokens :]
    masked_ref[...] = enc_ref[...] * row_to_col(valid.astype(F32))

    def ranks(owner_row, count):
        hot = iota((devices, count), 0) == owner_row
        before = as_bf16(iota((count, count), 0) < iota((count, count), 1))
        seen = dot1(as_bf16(hot), before, NN)
        return hot, jnp.sum(jnp.where(hot, seen, 0.0), axis=0, keepdims=True).astype(I32)

    def table(hot, value, place):
        return dot1(jnp.where(hot, value, 0.0).astype(BF16), place, NT)

    def placed(lane_row, count):
        return as_bf16(iota((LANES, count), 0) == lane_row)

    hot, rank = ranks(owner, tokens)
    place = placed(rank, tokens)
    high = table(hot, (local >> 6).astype(F32), place)
    low = table(hot, (local & 63).astype(F32), place)
    group = owner >> (members.bit_length() - 1)
    hot_member = (iota((devices, tokens), 0) & (members - 1)) == (owner & (members - 1))
    position = table(
        hot_member, (iota((1, tokens), 1) + 1).astype(F32), placed(group * slots + rank, tokens)
    )

    hot, rank = ranks(ids >> shift, negatives)
    place = placed(rank + slots, negatives)
    local = ids & (rows_dev - 1)
    high = high + table(hot, (local >> 6).astype(F32), place)
    low = low + table(hot, (local & 63).astype(F32), place)
    out_ref[:, 0, 0:LANES] = high.astype(I32) * 64 + low.astype(I32)
    out_ref[:, 0, LANES:] = position.astype(I32)


def gather_kernel(members, groups, part, count, info, got, table, *refs):
    for d, out in enumerate(refs[-groups:]):
        first = (info[0] ^ d) * members

        def member(mr, carry, out=out, first=first):
            asked = got.at[first + mr, 0]
            copy_rows(table, lambda k: asked[part + k], out, mr * count, count)
            return carry

        lax.fori_loop(0, members, member, 0)


def score_kernel(blocks, groups, info, *refs):
    rows, refs = refs[:groups], refs[groups:]
    encs, refs = refs[: len(blocks)], refs[len(blocks) :]
    stats, prob_hi, prob_lo = refs[-3:]
    if len(refs) > 3:
        stats[...] = refs[0][...]
    tokens = encs[0].shape[0]
    neg = split3(jnp.concatenate([row[...] for row in rows], axis=0))
    for i, e in enumerate(blocks):
        lanes = pl.ds(pl.multiple_of((info[1] ^ e) * tokens, LANES), tokens)
        score = dot6(neg, split3(encs[i][...]), NT)
        top = jnp.max(score, axis=0, keepdims=True)
        prob = jnp.exp(score - top)
        stats[0:1, lanes] = top
        stats[1:2, lanes] = jnp.sum(prob, axis=0, keepdims=True)
        parts = split(prob)
        prob_hi[i] = parts[0]
        prob_lo[i] = parts[1]


def own_places(members, info, got):
    return got[pl.ds(info[0] * members, members), 0, LANES:]


def slot_hot(members, groups, slots, info, place_rows, column, mr, tokens):
    column[...] = row_to_col(place_rows[pl.ds(mr, 1), :])
    place = [
        column[pl.ds(pl.multiple_of((info[0] ^ d) * slots, slots), slots), :]
        for d in range(groups)
    ]
    return jnp.concatenate(place, axis=0) == iota((groups * slots, tokens), 1) + 1


def pick_kernel(members, groups, slots, info, got, *refs):
    encs = refs[:members]
    outs = refs[members : members + groups]
    place_rows, column = refs[members + groups :]
    place_rows[...] = own_places(members, info, got)
    for e in range(members):
        mr = info[1] ^ e
        tokens = encs[e].shape[0]
        hot = as_bf16(slot_hot(members, groups, slots, info, place_rows, column, mr, tokens))
        hi, mid, low = split3(encs[e][...])
        found = (dot1(hot, hi, NN) + dot1(hot, mid, NN)) + dot1(hot, low, NN)
        at = pl.ds(pl.multiple_of(mr * slots, slots), slots)
        for d in range(groups):
            outs[d][at, :] = found[d * slots : (d + 1) * slots]


def positive_kernel(members, groups, slots, tokens, info, got, stats, *refs):
    rows, picked = refs[:groups], refs[groups : 2 * groups]
    joined, own, place_rows, column = refs[2 * groups :]
    place_rows[...] = own_places(members, info, got)
    for e in range(members):
        mr = info[1] ^ e
        lanes = pl.ds(pl.multiple_of(mr * tokens, LANES), tokens)
        at = pl.ds(pl.multiple_of(mr * slots, slots), slots)
        hot = slot_hot(members, groups, slots, info, place_rows, column, mr, tokens)
        row = jnp.concatenate([r[at, :] for r in rows], axis=0)
        enc = jnp.concatenate([p[at, :] for p in picked], axis=0)
        value = jnp.sum(row * enc, axis=1, keepdims=True)
        positive = jnp.sum(jnp.where(hot, value, 0.0), axis=0, keepdims=True)
        has = jnp.sum(hot.astype(F32), axis=0, keepdims=True)
        old = stats[0:1, lanes]
        top = jnp.where(has > 0, jnp.maximum(old, positive), old)
        joined[0:1, lanes] = top
        joined[1:2, lanes] = stats[1:2, lanes] * jnp.exp(old - top) + jnp.where(
            has > 0, jnp.exp(positive - top), 0.0
        )
        own[0:1, lanes] = positive
        own[1:2, lanes] = has


def pulled_kernel(members, groups, slots, halves, info, got, *refs):
    negs, refs = refs[:groups], refs[groups:]
    rows, refs = refs[:groups], refs[groups:]
    probs, (pulled, row_t, place_rows, column) = refs[:-4], refs[-4:]
    place_rows[...] = own_places(members, info, got)
    neg = jnp.concatenate([row[...] for row in negs], axis=0)
    neg_t = split(jnp.transpose(neg))
    tokens = pulled.shape[2]
    for h, blocks in enumerate(halves):
        for i, e in enumerate(blocks):
            mr = info[1] ^ e
            pulled[e] = dot3(neg_t, (probs[2 * h][i], probs[2 * h + 1][i]), NN)
            at = pl.ds(pl.multiple_of(mr * slots, slots), slots)
            hot = slot_hot(members, groups, slots, info, place_rows, column, mr, tokens)
            high, low = split(jnp.concatenate([r[at, :] for r in rows], axis=0))
            row_t[e] = dot1(high, as_bf16(hot), TN) + dot1(low, as_bf16(hot), TN)


def join(first, second):
    top = jnp.maximum(first[0:1], second[0:1])
    total = first[1:2] * jnp.exp(first[0:1] - top) + second[1:2] * jnp.exp(second[0:1] - top)
    return top, total


def join_kernel(first, second, *refs):
    out = refs[-1]
    top, total = join(first[...], second[...])
    out[0:1, :] = top
    out[1:2, :] = total


def shares(info, e, tokens, final, stats, own):
    lanes = pl.ds(pl.multiple_of((info[1] ^ e) * tokens, LANES), tokens)
    top, total = final[0:1, lanes], final[1:2, lanes]
    scale = jnp.exp(stats[0:1, lanes] - top) / total
    extra = jnp.where(
        own[1:2, lanes] > 0, jnp.exp(own[0:1, lanes] - top) / total - 1.0, 0.0
    )
    return scale, extra


def pull_kernel(blocks, tokens, info, final, stats, own, pulled, row_t, *refs):
    for e, out in zip(blocks, refs[-len(blocks) :]):
        scale, extra = shares(info, e, tokens, final, stats, own)
        out[...] = pulled[e] * scale + row_t[e] * extra


def flat(table, lane, slots):
    return jnp.concatenate(
        [table[m : m + 1, lane : lane + slots] for m in range(table.shape[0])], axis=1
    )


def grad_kernel(members, groups, slots, halves, info, got, final, stats, own, *refs):
    probs, refs = refs[: 2 * len(halves)], refs[2 * len(halves) :]
    encs = refs[:members]
    outs = refs[members : members + groups]
    total, coef, place_rows = refs[members + groups :]
    place_rows[...] = own_places(members, info, got)
    tokens, width = encs[0].shape
    for h, i, e in [(h, i, e) for h, blocks in enumerate(halves) for i, e in enumerate(blocks)]:
        mr = info[1] ^ e
        scale, extra = shares(info, e, tokens, final, stats, own)
        enc = split(encs[e][...] * row_to_col(scale))
        part = dot3((probs[2 * h][i], probs[2 * h + 1][i]), enc, NN)
        if h == 0 and i == 0:
            total[...] = part
        else:
            total[...] += part
        hot = place_rows[pl.ds(mr, 1), :] == iota((tokens, LANES), 0) + 1
        coef[pl.ds(mr, 1), :] = jnp.sum(
            jnp.where(hot, row_to_col(extra), 0.0), axis=0, keepdims=True
        )
    count = total.shape[0] // groups
    lines = [flat(coef[...], g * slots, slots) for g in range(groups)]
    for d, out in enumerate(outs):
        out[0:count, :] = total[d * count : (d + 1) * count, :]
        line = lines[0]
        for g in range(1, groups):
            line = jnp.where((info[0] ^ d) == g, lines[g], line)
        out[count:, 0 : line.shape[1]] = jnp.broadcast_to(line, (8, line.shape[1]))


def equal_in_batch(ids):
    size = ids.shape[1]
    across = jnp.broadcast_to(ids.astype(F32), (size, size))
    same = (jnp.transpose(across) == across) & (
        (iota((size, size), 0) // BATCH) == (iota((size, size), 1) // BATCH)
    )
    return same.astype(F32)


def scatter_kernel(members, groups, slots, count, info, got_v, got, *refs):
    grads, picked = refs[:groups], refs[groups : 2 * groups]
    out, negs, tgts = refs[2 * groups :]
    out[...] = jnp.zeros_like(out)

    def add_rows(asked, first, source, base, number):
        for b in range(0, number, BATCH):
            rows = [asked[first + b + k] for k in range(BATCH)]
            new = [
                out[pl.ds(rows[k], 1), :] + source[pl.ds(base + b + k, 1), :]
                for k in range(BATCH)
            ]
            for k in range(BATCH):
                out[pl.ds(rows[k], 1), :] = new[k]

    for d in range(groups):
        g = info[0] ^ d
        asked = got_v[pl.ds(g * members, members), 0, 0:LANES]
        number = members * count
        same = as_bf16(equal_in_batch(flat(asked, slots, count)) > 0)
        high, low = split(grads[d][0:number, :])
        negs[...] = dot1(same, high, NN) + dot1(same, low, NN)
        weight = equal_in_batch(flat(asked, 0, slots))
        weight = weight * grads[d][number : number + 1, 0 : members * slots]
        tgts[...] = dot3(split(weight), split(picked[d][...]), NN)
        merged = BATCH // count if count < BATCH else 1

        def member(step, carry, g=g, merged=merged):
            if merged == 1:
                add_rows(got.at[g * members + step, 0], slots, negs, step * count, count)
                add_rows(got.at[g * members + step, 0], 0, tgts, step * slots, slots)
                return carry
            first = g * members + step * merged
            rows = [
                got[first + k // count, 0, slots + k % count] for k in range(BATCH)
            ]
            new = [
                out[pl.ds(rows[k], 1), :] + negs[pl.ds(step * BATCH + k, 1), :]
                for k in range(BATCH)
            ]
            for k in range(BATCH):
                out[pl.ds(rows[k], 1), :] = new[k]
            for m in range(merged):
                add_rows(got.at[first + m, 0], 0, tgts, (step * merged + m) * slots, slots)
            return carry

        lax.fori_loop(0, members // merged, member, 0)


def add_kernel(terms, *refs):
    total = refs[0][...]
    for ref in refs[1:terms]:
        total = total + ref[...]
    refs[-1][...] = total


def finish_kernel(valid, *refs):
    total = refs[0][...]
    for ref in refs[1:-1]:
        total = total + ref[...]
    refs[-1][...] = jnp.transpose(total) * row_to_col(valid[...].astype(F32))


def swap(value, axis, d):
    return lax.ppermute(value, axis, [(i, i ^ d) for i in range(lax.axis_size(axis))])


def shards(encoded, item_table, target_owner, target_local, negative_ids, valid):
    groups, members = lax.axis_size("group"), lax.axis_size("member")
    devices = groups * members
    tokens, width = encoded.shape
    rows_dev = item_table.shape[0]
    negatives = negative_ids.shape[0]
    slots = max(2, 4 * tokens // devices)
    count = negatives // devices
    near = max(1, members // 4)
    everyone = members * tokens
    shape = jax.ShapeDtypeStruct
    sds = lambda *s: shape(s, F32)

    info = jnp.stack([lax.axis_index("group"), lax.axis_index("member")]).astype(I32)
    ints = jnp.concatenate([target_owner.reshape(-1), target_local, valid, negative_ids])
    request, masked = call(
        functools.partial(front_kernel, members, rows_dev, slots, tokens, negatives),
        [shape((devices, 1, 2 * LANES), I32), sds(tokens, width)],
        [SMEM] + [VMEM] * 2,
        [VMEM] * 2,
        (info, ints.reshape(1, -1), encoded),
        name="front",
    )
    got = lax.all_to_all(
        request, ("group", "member"), split_axis=0, concat_axis=0, tiled=True
    )

    encs = [masked] + [None] * (members - 1)
    for z in (near, 2 * near):
        encs[z] = swap(masked, "member", z)
    onward, got = lax.optimization_barrier((encs[2 * near], got))
    encs[3 * near] = swap(onward, "member", near)
    for z in range(0, members, near):
        for x in range(1, near):
            encs[z ^ x] = swap(onward if z == 2 * near else encs[z], "member", x)
    halves = [[d for d in range(members) if (d < near) or d in (near, 2 * near)], []]
    halves[1] = [d for d in range(members) if d not in halves[0]]

    early = [encs[d] for d in halves[0] if d]
    gather = lambda part, many, deps, name: call(
        functools.partial(gather_kernel, members, groups, part, many),
        [sds(members * many, width)] * groups,
        [SMEM, SMEM, VMEM] + [ANY] * len(deps),
        [VMEM] * groups,
        (info, got, item_table, *deps),
        name=name,
    )
    negs = gather(slots, count, early, "gather_negatives")
    negs = [negs[0]] + [swap(negs[d], "group", d) for d in range(1, groups)]
    rows = gather(0, slots, [], "gather_targets")
    rows = [rows[0]] + [swap(rows[d], "group", d) for d in range(1, groups)]

    stats, probs = [], []
    for blocks in halves:
        many = len(blocks)
        *stats, hi, lo = call(
            functools.partial(score_kernel, blocks, groups),
            [sds(2, everyone)] + [shape((many, negatives, tokens), BF16)] * 2,
            [SMEM] + [VMEM] * (groups + many + len(stats)),
            [VMEM] * 3,
            (info, *negs, *[encs[e] for e in blocks], *stats),
            flops=12 * many * tokens * negatives * width,
            moved=MIB,
            name="score",
        )
        probs += [hi, lo]
    stats = stats[0]
    picked = call(
        functools.partial(pick_kernel, members, groups, slots),
        [sds(members * slots, width)] * groups,
        [SMEM] + [VMEM] * (1 + members),
        [VMEM] * groups,
        (info, got, *encs),
        scratch=[pltpu.VMEM((members, LANES), I32), pltpu.VMEM((LANES, 1), I32)],
        name="pick",
    )
    sent = [picked[0]] + [swap(picked[d], "group", d) for d in range(1, groups)]
    joined, own = call(
        functools.partial(positive_kernel, members, groups, slots, tokens),
        [sds(2, everyone)] * 2,
        [SMEM] + [VMEM] * (2 + 2 * groups),
        [VMEM] * 2,
        (info, got, stats, *rows, *picked),
        scratch=[pltpu.VMEM((members, LANES), I32), pltpu.VMEM((LANES, 1), I32)],
        name="positive",
    )
    pulled, row_t = call(
        functools.partial(pulled_kernel, members, groups, slots, halves),
        [sds(members, width, tokens)] * 2,
        [SMEM] + [VMEM] * (1 + 2 * groups + len(probs)),
        [VMEM] * 2,
        (info, got, *negs, *rows, *probs),
        scratch=[pltpu.VMEM((members, LANES), I32), pltpu.VMEM((LANES, 1), I32)],
        flops=6 * everyone * negatives * width,
        moved=MIB,
        name="pulled",
    )

    final = joined
    d = 1
    while d < members:
        late = sent[1:] if 2 * d == members else []
        final = call(
            join_kernel,
            sds(2, everyone),
            [VMEM] * 2 + [ANY] * len(late),
            VMEM,
            (final, swap(final, "member", d), *late),
            name="join",
        )
        d *= 2

    grads = call(
        functools.partial(grad_kernel, members, groups, slots, halves),
        [sds(members * count + 8, width)] * groups,
        [SMEM] + [VMEM] * (4 + len(probs) + members),
        [VMEM] * groups,
        (info, got, final, stats, own, *probs, *encs),
        scratch=[
            pltpu.VMEM((negatives, width), F32),
            pltpu.VMEM((members, LANES), F32),
            pltpu.VMEM((members, LANES), I32),
        ],
        flops=6 * everyone * negatives * width,
        moved=8 * MIB,
        name="grad",
    )
    def added(terms, deps):
        return call(
            functools.partial(add_kernel, len(terms)),
            sds(width, tokens),
            [VMEM] * len(terms) + [ANY] * len(deps),
            VMEM,
            (*terms, *deps),
            name="add",
        )

    graded = [grads[0]]
    grads = graded + [swap(grads[d], "group", d) for d in range(1, groups)]
    def scaled(first, many, deps):
        blocks = list(range(first, first + many))
        return call(
            functools.partial(pull_kernel, blocks, tokens),
            [sds(width, tokens)] * many,
            [SMEM] + [VMEM] * 5 + [ANY] * len(deps),
            [VMEM] * many,
            (info, final, stats, own, pulled, row_t, *deps),
            name="pull",
        )

    def beside(blocks):
        return [swap(blocks[x], "member", x) for x in range(1, near)]

    farthest = scaled(3 * near, near, [])
    arrived = beside(farthest)
    far = scaled(2 * near, near, arrived)
    total = added([farthest[0], *arrived], graded)
    total = added([far[0], *beside(far), swap(total, "member", near)], grads[1:])
    close = scaled(0, 2 * near, [total])
    parts = [swap(total, "member", 2 * near), close[0]]
    parts += [swap(close[d], "member", d) for d in range(1, 2 * near)]

    table_grad = call(
        functools.partial(scatter_kernel, members, groups, slots, count),
        sds(rows_dev, width),
        [SMEM, VMEM, SMEM] + [VMEM] * (2 * groups),
        VMEM,
        (info, got, got, *grads, *sent),
        scratch=[
            pltpu.VMEM((members * count, width), F32),
            pltpu.VMEM((members * slots, width), F32),
        ],
        name="scatter",
    )
    encoded_grad = call(
        finish_kernel,
        sds(tokens, width),
        [VMEM] * (1 + len(parts)),
        VMEM,
        (valid.reshape(1, -1), *parts),
        name="finish",
    )
    return (encoded_grad, table_grad)


def solution(mesh):
    placed = (
        P(("group", "member"), None),
        P(("group", "member"), None),
        P(("group", "member"), None),
        P(("group", "member")),
        P(("group", "member")),
        P(("group", "member")),
    )
    return jax.shard_map(
        shards,
        mesh=mesh,
        in_specs=placed,
        out_specs=(P(("group", "member"), None), P(("group", "member"), None)),
        check_vma=False,
    )
```

```python
import functools

import jax
import jax.numpy as jnp
from jax import lax
from jax.experimental import pallas as pl
from jax.experimental.pallas import tpu as pltpu
from jax.sharding import PartitionSpec as P

F32 = jnp.float32
BF16 = jnp.bfloat16
I32 = jnp.int32
LANES = 128
VMEM = pl.BlockSpec(memory_space=pltpu.VMEM)
ANY = pl.BlockSpec(memory_space=pl.ANY)
SMEM = pl.BlockSpec(memory_space=pltpu.SMEM)
MIB = 1 << 20
BATCH = 8

NN = (((1,), (0,)), ((), ()))
NT = (((1,), (1,)), ((), ()))
TN = (((0,), (0,)), ((), ()))


def call(kernel, out_shape, ins, outs, args, scratch=(), limit=10, flops=0, moved=0, name=None):
    return pl.pallas_call(
        kernel,
        out_shape=out_shape,
        in_specs=ins,
        out_specs=outs,
        scratch_shapes=list(scratch),
        compiler_params=pltpu.CompilerParams(vmem_limit_bytes=limit * MIB),
        cost_estimate=pl.CostEstimate(flops=flops, bytes_accessed=moved, transcendentals=0),
        name=name,
    )(*args)


def iota(shape, dim):
    return lax.broadcasted_iota(I32, shape, dim)


def as_bf16(flag):
    return flag.astype(F32).astype(BF16)


def dot1(a, b, dims):
    return lax.dot_general(a, b, dims, preferred_element_type=F32)


def split(x):
    hi = x.astype(BF16)
    return hi, (x - hi.astype(F32)).astype(BF16)


def dot3(a, b, dims):
    return dot1(a[0], b[0], dims) + (dot1(a[0], b[1], dims) + dot1(a[1], b[0], dims))


def row_to_col(row):
    return jnp.transpose(jnp.broadcast_to(row, (LANES, row.shape[1])))[:, 0:1]


def split3(x):
    hi = x.astype(BF16)
    rest = x - hi.astype(F32)
    mid = rest.astype(BF16)
    return hi, mid, (rest - mid.astype(F32)).astype(BF16)


def dot6(a, b, dims):
    small = dot1(a[2], b[0], dims) + dot1(a[1], b[1], dims) + dot1(a[0], b[2], dims)
    return (small + (dot1(a[1], b[0], dims) + dot1(a[0], b[1], dims))) + dot1(a[0], b[0], dims)


def copy_rows(source, row_of, target, base, count):
    for b in range(0, count, BATCH):
        rows = [source[pl.ds(row_of(b + k), 1), :] for k in range(BATCH)] if count % BATCH == 0 else None
        if rows is None:
            for k in range(count):
                target[pl.ds(base + k, 1), :] = source[pl.ds(row_of(k), 1), :]
            return
        target[pl.ds(pl.multiple_of(base + b, BATCH), BATCH), :] = jnp.concatenate(rows, axis=0)


def front_kernel(members, rows_dev, slots, tokens, negatives, info, ints, enc_ref, out_ref, masked_ref):
    devices = out_ref.shape[0]
    shift = rows_dev.bit_length() - 1
    owner = ints[:, 0:tokens]
    local = ints[:, tokens : 2 * tokens]
    valid = ints[:, 2 * tokens : 3 * tokens]
    ids = ints[:, 3 * tokens :]
    masked_ref[...] = enc_ref[...] * row_to_col(valid.astype(F32))

    def ranks(owner_row, count):
        hot = iota((devices, count), 0) == owner_row
        before = as_bf16(iota((count, count), 0) < iota((count, count), 1))
        seen = dot1(as_bf16(hot), before, NN)
        return hot, jnp.sum(jnp.where(hot, seen, 0.0), axis=0, keepdims=True).astype(I32)

    def table(hot, value, place):
        return dot1(jnp.where(hot, value, 0.0).astype(BF16), place, NT)

    def placed(lane_row, count):
        return as_bf16(iota((LANES, count), 0) == lane_row)

    hot, rank = ranks(owner, tokens)
    place = placed(rank, tokens)
    high = table(hot, (local >> 6).astype(F32), place)
    low = table(hot, (local & 63).astype(F32), place)
    group = owner >> (members.bit_length() - 1)
    hot_member = (iota((devices, tokens), 0) & (members - 1)) == (owner & (members - 1))
    position = table(
        hot_member, (iota((1, tokens), 1) + 1).astype(F32), placed(group * slots + rank, tokens)
    )

    hot, rank = ranks(ids >> shift, negatives)
    place = placed(rank + slots, negatives)
    local = ids & (rows_dev - 1)
    high = high + table(hot, (local >> 6).astype(F32), place)
    low = low + table(hot, (local & 63).astype(F32), place)
    out_ref[:, 0, 0:LANES] = high.astype(I32) * 64 + low.astype(I32)
    out_ref[:, 0, LANES : 2 * LANES] = position.astype(I32)
    if out_ref.shape[2] > 2 * LANES:
        rest = out_ref.shape[2] - 2 * LANES
        out_ref[:, 0, 2 * LANES :] = jnp.zeros((devices, rest), I32)


def gather_kernel(members, groups, part, count, info, got, table, *refs):
    for d, out in enumerate(refs[-groups:]):
        first = (info[0] ^ d) * members

        def member(mr, carry, out=out, first=first):
            asked = got.at[first + mr, 0]
            copy_rows(table, lambda k: asked[part + k], out, mr * count, count)
            return carry

        lax.fori_loop(0, members, member, 0)


def score_kernel(blocks, groups, info, *refs):
    rows, refs = refs[:groups], refs[groups:]
    encs, refs = refs[: len(blocks)], refs[len(blocks) :]
    stats, prob_hi, prob_lo = refs[-3:]
    if len(refs) > 3:
        stats[...] = refs[0][...]
    tokens = encs[0].shape[0]
    neg = split3(jnp.concatenate([row[...] for row in rows], axis=0))
    for i, e in enumerate(blocks):
        lanes = pl.ds(pl.multiple_of((info[1] ^ e) * tokens, LANES), tokens)
        score = dot6(neg, split3(encs[i][...]), NT)
        top = jnp.max(score, axis=0, keepdims=True)
        prob = jnp.exp(score - top)
        stats[0:1, lanes] = top
        stats[1:2, lanes] = jnp.sum(prob, axis=0, keepdims=True)
        parts = split(prob)
        prob_hi[i] = parts[0]
        prob_lo[i] = parts[1]


def own_places(members, info, got):
    return got[pl.ds(info[0] * members, members), 0, LANES : 2 * LANES]


def slot_hot(members, groups, slots, info, place_rows, column, mr, tokens):
    column[...] = row_to_col(place_rows[pl.ds(mr, 1), :])
    place = [
        column[pl.ds(pl.multiple_of((info[0] ^ d) * slots, slots), slots), :]
        for d in range(groups)
    ]
    return jnp.concatenate(place, axis=0) == iota((groups * slots, tokens), 1) + 1


def pick_kernel(members, groups, slots, info, got, *refs):
    encs = refs[:members]
    outs = refs[members : members + groups]
    place_rows, column = refs[members + groups :]
    place_rows[...] = own_places(members, info, got)
    for e in range(members):
        mr = info[1] ^ e
        tokens = encs[e].shape[0]
        hot = as_bf16(slot_hot(members, groups, slots, info, place_rows, column, mr, tokens))
        hi, mid, low = split3(encs[e][...])
        found = (dot1(hot, hi, NN) + dot1(hot, mid, NN)) + dot1(hot, low, NN)
        at = pl.ds(pl.multiple_of(mr * slots, slots), slots)
        for d in range(groups):
            outs[d][at, :] = found[d * slots : (d + 1) * slots]


def positive_kernel(members, groups, slots, tokens, info, got, stats, *refs):
    rows, picked = refs[:groups], refs[groups : 2 * groups]
    joined, own, place_rows, column = refs[2 * groups :]
    place_rows[...] = own_places(members, info, got)
    for e in range(members):
        mr = info[1] ^ e
        lanes = pl.ds(pl.multiple_of(mr * tokens, LANES), tokens)
        at = pl.ds(pl.multiple_of(mr * slots, slots), slots)
        hot = slot_hot(members, groups, slots, info, place_rows, column, mr, tokens)
        row = jnp.concatenate([r[at, :] for r in rows], axis=0)
        enc = jnp.concatenate([p[at, :] for p in picked], axis=0)
        value = jnp.sum(row * enc, axis=1, keepdims=True)
        positive = jnp.sum(jnp.where(hot, value, 0.0), axis=0, keepdims=True)
        has = jnp.sum(hot.astype(F32), axis=0, keepdims=True)
        old = stats[0:1, lanes]
        top = jnp.where(has > 0, jnp.maximum(old, positive), old)
        joined[0:1, lanes] = top
        joined[1:2, lanes] = stats[1:2, lanes] * jnp.exp(old - top) + jnp.where(
            has > 0, jnp.exp(positive - top), 0.0
        )
        own[0:1, lanes] = positive
        own[1:2, lanes] = has


def pulled_kernel(members, groups, slots, blocks, info, got, *refs):
    negs, refs = refs[:groups], refs[groups:]
    rows, refs = refs[:groups], refs[groups:]
    prob_hi, prob_lo, pulled, row_t, place_rows, column = refs
    place_rows[...] = own_places(members, info, got)
    neg = jnp.concatenate([row[...] for row in negs], axis=0)
    neg_t = split(jnp.transpose(neg))
    tokens = pulled.shape[2]
    for i, e in enumerate(blocks):
        mr = info[1] ^ e
        pulled[i] = dot3(neg_t, (prob_hi[i], prob_lo[i]), NN)
        at = pl.ds(pl.multiple_of(mr * slots, slots), slots)
        hot = slot_hot(members, groups, slots, info, place_rows, column, mr, tokens)
        high, low = split(jnp.concatenate([r[at, :] for r in rows], axis=0))
        row_t[i] = dot1(high, as_bf16(hot), TN) + dot1(low, as_bf16(hot), TN)


def join(first, second):
    top = jnp.maximum(first[0:1], second[0:1])
    total = first[1:2] * jnp.exp(first[0:1] - top) + second[1:2] * jnp.exp(second[0:1] - top)
    return top, total


def join_kernel(first, second, *refs):
    out = refs[-1]
    top, total = join(first[...], second[...])
    out[0:1, :] = top
    out[1:2, :] = total


def shares(info, e, tokens, final, stats, own):
    lanes = pl.ds(pl.multiple_of((info[1] ^ e) * tokens, LANES), tokens)
    top, total = final[0:1, lanes], final[1:2, lanes]
    scale = jnp.exp(stats[0:1, lanes] - top) / total
    extra = jnp.where(
        own[1:2, lanes] > 0, jnp.exp(own[0:1, lanes] - top) / total - 1.0, 0.0
    )
    return scale, extra


def pull_kernel(halves, blocks, tokens, info, final, stats, own, *refs):
    for e, out in zip(blocks, refs[-len(blocks) :]):
        h = 0 if e in halves[0] else 1
        pulled, row_t = (ref[halves[h].index(e)] for ref in refs[2 * h : 2 * h + 2])
        scale, extra = shares(info, e, tokens, final, stats, own)
        out[...] = pulled * scale + row_t * extra


def flat(table, lane, slots):
    return jnp.concatenate(
        [table[m : m + 1, lane : lane + slots] for m in range(table.shape[0])], axis=1
    )


def grad_kernel(members, groups, slots, halves, info, got, final, stats, own, *refs):
    probs, refs = refs[: 2 * len(halves)], refs[2 * len(halves) :]
    encs = refs[:members]
    *outs, total, coef, place_rows = refs[-groups - 3 :]
    place_rows[...] = own_places(members, info, got)
    tokens, width = encs[0].shape
    for h, i, e in [(h, i, e) for h, blocks in enumerate(halves) for i, e in enumerate(blocks)]:
        mr = info[1] ^ e
        scale, extra = shares(info, e, tokens, final, stats, own)
        enc = split(encs[e][...] * row_to_col(scale))
        part = dot3((probs[2 * h][i], probs[2 * h + 1][i]), enc, NN)
        if h == 0 and i == 0:
            total[...] = part
        else:
            total[...] += part
        hot = place_rows[pl.ds(mr, 1), :] == iota((tokens, LANES), 0) + 1
        coef[pl.ds(mr, 1), :] = jnp.sum(
            jnp.where(hot, row_to_col(extra), 0.0), axis=0, keepdims=True
        )
    count = total.shape[0] // groups
    lines = [flat(coef[...], g * slots, slots) for g in range(groups)]
    for d, out in enumerate(outs):
        out[0:count, :] = total[d * count : (d + 1) * count, :]
        line = lines[0]
        for g in range(1, groups):
            line = jnp.where((info[0] ^ d) == g, lines[g], line)
        out[count:, 0 : line.shape[1]] = jnp.broadcast_to(line, (8, line.shape[1]))


def equal_in_batch(ids):
    size = ids.shape[1]
    across = jnp.broadcast_to(ids.astype(F32), (size, size))
    same = (jnp.transpose(across) == across) & (
        (iota((size, size), 0) // BATCH) == (iota((size, size), 1) // BATCH)
    )
    return same.astype(F32)


def scatter_kernel(members, groups, slots, count, info, got_v, got, *refs):
    grads, picked = refs[:groups], refs[groups : 2 * groups]
    out, negs, tgts = refs[2 * groups :]
    out[...] = jnp.zeros_like(out)

    def add_rows(asked, first, source, base, number):
        for b in range(0, number, BATCH):
            rows = [asked[first + b + k] for k in range(BATCH)]
            new = [
                out[pl.ds(rows[k], 1), :] + source[pl.ds(base + b + k, 1), :]
                for k in range(BATCH)
            ]
            for k in range(BATCH):
                out[pl.ds(rows[k], 1), :] = new[k]

    for d in range(groups):
        g = info[0] ^ d
        asked = got_v[pl.ds(g * members, members), 0, 0:LANES]
        number = members * count
        same = as_bf16(equal_in_batch(flat(asked, slots, count)) > 0)
        high, low = split(grads[d][0:number, :])
        negs[...] = dot1(same, high, NN) + dot1(same, low, NN)
        weight = equal_in_batch(flat(asked, 0, slots))
        weight = weight * grads[d][number : number + 1, 0 : members * slots]
        tgts[...] = dot3(split(weight), split(picked[d][...]), NN)
        merged = BATCH // count if count < BATCH else 1

        def member(step, carry, g=g, merged=merged):
            if merged == 1:
                add_rows(got.at[g * members + step, 0], slots, negs, step * count, count)
                add_rows(got.at[g * members + step, 0], 0, tgts, step * slots, slots)
                return carry
            first = g * members + step * merged
            rows = [
                got[first + k // count, 0, slots + k % count] for k in range(BATCH)
            ]
            new = [
                out[pl.ds(rows[k], 1), :] + negs[pl.ds(step * BATCH + k, 1), :]
                for k in range(BATCH)
            ]
            for k in range(BATCH):
                out[pl.ds(rows[k], 1), :] = new[k]
            for m in range(merged):
                add_rows(got.at[first + m, 0], 0, tgts, (step * merged + m) * slots, slots)
            return carry

        lax.fori_loop(0, members // merged, member, 0)


def add_kernel(terms, *refs):
    total = refs[0][...]
    for ref in refs[1:terms]:
        total = total + ref[...]
    refs[-1][...] = total


def finish_kernel(valid, *refs):
    total = refs[0][...]
    for ref in refs[1:-1]:
        total = total + ref[...]
    refs[-1][...] = jnp.transpose(total) * row_to_col(valid[...].astype(F32))


def swap(value, axis, d):
    return lax.ppermute(value, axis, [(i, i ^ d) for i in range(lax.axis_size(axis))])


def shards(encoded, item_table, target_owner, target_local, negative_ids, valid):
    groups, members = lax.axis_size("group"), lax.axis_size("member")
    devices = groups * members
    tokens, width = encoded.shape
    rows_dev = item_table.shape[0]
    negatives = negative_ids.shape[0]
    slots = max(2, 4 * tokens // devices)
    count = negatives // devices
    near = max(1, members // 4)
    everyone = members * tokens
    shape = jax.ShapeDtypeStruct
    sds = lambda *s: shape(s, F32)

    info = jnp.stack([lax.axis_index("group"), lax.axis_index("member")]).astype(I32)
    ints = jnp.concatenate([target_owner.reshape(-1), target_local, valid, negative_ids])
    request, masked = call(
        functools.partial(front_kernel, members, rows_dev, slots, tokens, negatives),
        [shape((devices, 1, max(2 * LANES, (1 << 15) // devices)), I32), sds(tokens, width)],
        [SMEM] + [VMEM] * 2,
        [VMEM] * 2,
        (info, ints.reshape(1, -1), encoded),
        name="front",
    )
    got = lax.all_to_all(
        request, ("group", "member"), split_axis=0, concat_axis=0, tiled=True
    )

    encs = [masked] + [None] * (members - 1)
    for z in (near, 2 * near):
        encs[z] = swap(masked, "member", z)
    onward, got = lax.optimization_barrier((encs[2 * near], got))
    encs[3 * near] = swap(onward, "member", near)
    for z in range(0, members, near):
        for x in range(1, near):
            encs[z ^ x] = swap(onward if z == 2 * near else encs[z], "member", x)
    halves = [[d for d in range(members) if (d < near) or d in (near, 2 * near)], []]
    halves[1] = [d for d in range(members) if d not in halves[0]]

    early = [encs[d] for d in halves[0] if d]
    gather = lambda part, many, deps, name: call(
        functools.partial(gather_kernel, members, groups, part, many),
        [sds(members * many, width)] * groups,
        [SMEM, SMEM, VMEM] + [ANY] * len(deps),
        [VMEM] * groups,
        (info, got, item_table, *deps),
        name=name,
    )
    negs = gather(slots, count, early, "gather_negatives")
    negs = [negs[0]] + [swap(negs[d], "group", d) for d in range(1, groups)]
    rows = gather(0, slots, [], "gather_targets")
    rows = [rows[0]] + [swap(rows[d], "group", d) for d in range(1, groups)]

    stats, probs = [], []
    for blocks in halves:
        many = len(blocks)
        *stats, hi, lo = call(
            functools.partial(score_kernel, blocks, groups),
            [sds(2, everyone)] + [shape((many, negatives, tokens), BF16)] * 2,
            [SMEM] + [VMEM] * (groups + many + len(stats)),
            [VMEM] * 3,
            (info, *negs, *[encs[e] for e in blocks], *stats),
            flops=12 * many * tokens * negatives * width,
            moved=MIB,
            name="score",
        )
        probs += [hi, lo]
    stats = stats[0]
    picked = call(
        functools.partial(pick_kernel, members, groups, slots),
        [sds(members * slots, width)] * groups,
        [SMEM] + [VMEM] * (1 + members),
        [VMEM] * groups,
        (info, got, *encs),
        scratch=[pltpu.VMEM((members, LANES), I32), pltpu.VMEM((LANES, 1), I32)],
        name="pick",
    )
    sent = [picked[0]] + [swap(picked[d], "group", d) for d in range(1, groups)]
    joined, own = call(
        functools.partial(positive_kernel, members, groups, slots, tokens),
        [sds(2, everyone)] * 2,
        [SMEM] + [VMEM] * (2 + 2 * groups),
        [VMEM] * 2,
        (info, got, stats, *rows, *picked),
        scratch=[pltpu.VMEM((members, LANES), I32), pltpu.VMEM((LANES, 1), I32)],
        name="positive",
    )
    pulled = []
    for h, blocks in enumerate(halves):
        pulled += call(
            functools.partial(pulled_kernel, members, groups, slots, blocks),
            [sds(len(blocks), width, tokens)] * 2,
            [SMEM] + [VMEM] * (3 + 2 * groups),
            [VMEM] * 2,
            (info, got, *negs, *rows, *probs[2 * h : 2 * h + 2]),
            scratch=[pltpu.VMEM((members, LANES), I32), pltpu.VMEM((LANES, 1), I32)],
            flops=6 * len(blocks) * tokens * negatives * width,
            moved=MIB,
            name="pulled",
        )

    final = joined
    d, hops = 1, 0
    while d < members:
        late = pulled[2 * hops : 2 * hops + 2]
        hops += 1
        final = call(
            join_kernel,
            sds(2, everyone),
            [VMEM] * 2 + [ANY] * len(late),
            VMEM,
            (final, swap(final, "member", d), *late),
            name="join",
        )
        d *= 2

    grads = call(
        functools.partial(grad_kernel, members, groups, slots, halves),
        [sds(members * count + 8, width)] * groups,
        [SMEM] + [VMEM] * (4 + len(probs) + members) + [ANY] * (groups - 1),
        [VMEM] * groups,
        (info, got, final, stats, own, *probs, *encs, *sent[1:]),
        scratch=[
            pltpu.VMEM((negatives, width), F32),
            pltpu.VMEM((members, LANES), F32),
            pltpu.VMEM((members, LANES), I32),
        ],
        flops=6 * everyone * negatives * width,
        moved=8 * MIB,
        name="grad",
    )
    def added(terms, deps):
        return call(
            functools.partial(add_kernel, len(terms)),
            sds(width, tokens),
            [VMEM] * len(terms) + [ANY] * len(deps),
            VMEM,
            (*terms, *deps),
            name="add",
        )

    graded = [grads[0]]
    grads = graded + [swap(grads[d], "group", d) for d in range(1, groups)]
    def scaled(blocks, deps):
        return call(
            functools.partial(pull_kernel, halves, blocks, tokens),
            [sds(width, tokens)] * len(blocks),
            [SMEM] + [VMEM] * 7 + [ANY] * len(deps),
            [VMEM] * len(blocks),
            (info, final, stats, own, *pulled, *deps),
            name="pull",
        )

    def beside(blocks):
        return [swap(block, "member", x) for x, block in enumerate(blocks, 1)]

    along = list(range(near))
    farthest, *rest, nearest = scaled([3 * near + x for x in along] + [near], [])
    arrived = beside(rest)
    nearest = swap(nearest, "member", near)
    far, *others = scaled([2 * near + x for x in along], [*arrived, nearest, *graded])
    total = swap(added([farthest, *arrived], graded), "member", near)
    half = added([far, *beside(others)], grads[1:])
    close = [*along[1:], *[near + x for x in along[1:]]]
    kept, *sends = scaled([0, *close], [half])
    parts = [swap(block, "member", d) for d, block in zip(close, sends)]
    parts += [nearest, kept, swap(added([half, total], []), "member", 2 * near)]

    table_grad = call(
        functools.partial(scatter_kernel, members, groups, slots, count),
        sds(rows_dev, width),
        [SMEM, VMEM, SMEM] + [VMEM] * (2 * groups),
        VMEM,
        (info, got, got, *grads, *sent),
        scratch=[
            pltpu.VMEM((members * count, width), F32),
            pltpu.VMEM((members * slots, width), F32),
        ],
        name="scatter",
    )
    encoded_grad = call(
        finish_kernel,
        sds(tokens, width),
        [VMEM] * (1 + len(parts)),
        VMEM,
        (valid.reshape(1, -1), *parts),
        name="finish",
    )
    return (encoded_grad, table_grad)


def solution(mesh):
    placed = (
        P(("group", "member"), None),
        P(("group", "member"), None),
        P(("group", "member"), None),
        P(("group", "member")),
        P(("group", "member")),
        P(("group", "member")),
    )
    return jax.shard_map(
        shards,
        mesh=mesh,
        in_specs=placed,
        out_specs=(P(("group", "member"), None), P(("group", "member"), None)),
        check_vma=False,
    )
```

```python
import functools

import jax
import jax.numpy as jnp
from jax import lax
from jax.experimental import pallas as pl
from jax.experimental.pallas import tpu as pltpu
from jax.sharding import PartitionSpec as P

F32 = jnp.float32
BF16 = jnp.bfloat16
I32 = jnp.int32
LANES = 128
VMEM = pl.BlockSpec(memory_space=pltpu.VMEM)
ANY = pl.BlockSpec(memory_space=pl.ANY)
SMEM = pl.BlockSpec(memory_space=pltpu.SMEM)
MIB = 1 << 20
BATCH = 8

NN = (((1,), (0,)), ((), ()))
NT = (((1,), (1,)), ((), ()))
TN = (((0,), (0,)), ((), ()))


def call(kernel, out_shape, ins, outs, args, scratch=(), limit=10, flops=0, moved=0, name=None):
    return pl.pallas_call(
        kernel,
        out_shape=out_shape,
        in_specs=ins,
        out_specs=outs,
        scratch_shapes=list(scratch),
        compiler_params=pltpu.CompilerParams(vmem_limit_bytes=limit * MIB),
        cost_estimate=pl.CostEstimate(flops=flops, bytes_accessed=moved, transcendentals=0),
        name=name,
    )(*args)


def iota(shape, dim):
    return lax.broadcasted_iota(I32, shape, dim)


def as_bf16(flag):
    return flag.astype(F32).astype(BF16)


def dot1(a, b, dims):
    return lax.dot_general(a, b, dims, preferred_element_type=F32)


def split(x):
    hi = x.astype(BF16)
    return hi, (x - hi.astype(F32)).astype(BF16)


def dot3(a, b, dims):
    return dot1(a[0], b[0], dims) + (dot1(a[0], b[1], dims) + dot1(a[1], b[0], dims))


def row_to_col(row):
    return jnp.transpose(jnp.broadcast_to(row, (LANES, row.shape[1])))[:, 0:1]


def split3(x):
    hi = x.astype(BF16)
    rest = x - hi.astype(F32)
    mid = rest.astype(BF16)
    return hi, mid, (rest - mid.astype(F32)).astype(BF16)


def dot6(a, b, dims):
    small = dot1(a[2], b[0], dims) + dot1(a[1], b[1], dims) + dot1(a[0], b[2], dims)
    return (small + (dot1(a[1], b[0], dims) + dot1(a[0], b[1], dims))) + dot1(a[0], b[0], dims)


def copy_rows(source, row_of, target, base, count):
    for b in range(0, count, BATCH):
        rows = [source[pl.ds(row_of(b + k), 1), :] for k in range(BATCH)] if count % BATCH == 0 else None
        if rows is None:
            for k in range(count):
                target[pl.ds(base + k, 1), :] = source[pl.ds(row_of(k), 1), :]
            return
        target[pl.ds(pl.multiple_of(base + b, BATCH), BATCH), :] = jnp.concatenate(rows, axis=0)


def front_kernel(members, rows_dev, slots, tokens, negatives, info, ints, enc_ref, out_ref, masked_ref):
    devices = out_ref.shape[0]
    shift = rows_dev.bit_length() - 1
    owner = ints[:, 0:tokens]
    local = ints[:, tokens : 2 * tokens]
    valid = ints[:, 2 * tokens : 3 * tokens]
    ids = ints[:, 3 * tokens :]
    masked_ref[...] = enc_ref[...] * row_to_col(valid.astype(F32))

    def ranks(owner_row, count):
        hot = iota((devices, count), 0) == owner_row
        before = as_bf16(iota((count, count), 0) < iota((count, count), 1))
        seen = dot1(as_bf16(hot), before, NN)
        return hot, jnp.sum(jnp.where(hot, seen, 0.0), axis=0, keepdims=True).astype(I32)

    def table(hot, value, place):
        return dot1(jnp.where(hot, value, 0.0).astype(BF16), place, NT)

    def placed(lane_row, count):
        return as_bf16(iota((LANES, count), 0) == lane_row)

    hot, rank = ranks(owner, tokens)
    place = placed(rank, tokens)
    high = table(hot, (local >> 6).astype(F32), place)
    low = table(hot, (local & 63).astype(F32), place)
    group = owner >> (members.bit_length() - 1)
    hot_member = (iota((devices, tokens), 0) & (members - 1)) == (owner & (members - 1))
    position = table(
        hot_member, (iota((1, tokens), 1) + 1).astype(F32), placed(group * slots + rank, tokens)
    )

    hot, rank = ranks(ids >> shift, negatives)
    place = placed(rank + slots, negatives)
    local = ids & (rows_dev - 1)
    high = high + table(hot, (local >> 6).astype(F32), place)
    low = low + table(hot, (local & 63).astype(F32), place)
    out_ref[:, 0, 0:LANES] = high.astype(I32) * 64 + low.astype(I32)
    out_ref[:, 0, LANES : 2 * LANES] = position.astype(I32)


def gather_kernel(members, groups, part, count, info, got, table, *refs):
    for d, out in enumerate(refs[-groups:]):
        first = (info[0] ^ d) * members

        def member(mr, carry, out=out, first=first):
            asked = got.at[first + mr, 0]
            copy_rows(table, lambda k: asked[part + k], out, mr * count, count)
            return carry

        lax.fori_loop(0, members, member, 0)


def score_kernel(blocks, groups, info, *refs):
    rows, refs = refs[:groups], refs[groups:]
    encs, refs = refs[: len(blocks)], refs[len(blocks) :]
    stats, prob_hi, prob_lo = refs[-3:]
    if len(refs) > 3:
        stats[...] = refs[0][...]
    tokens = encs[0].shape[0]
    neg = split3(jnp.concatenate([row[...] for row in rows], axis=0))
    for i, e in enumerate(blocks):
        lanes = pl.ds(pl.multiple_of((info[1] ^ e) * tokens, LANES), tokens)
        score = dot6(neg, split3(encs[i][...]), NT)
        top = jnp.max(score, axis=0, keepdims=True)
        prob = jnp.exp(score - top)
        stats[0:1, lanes] = top
        stats[1:2, lanes] = jnp.sum(prob, axis=0, keepdims=True)
        parts = split(prob)
        prob_hi[i] = parts[0]
        prob_lo[i] = parts[1]


def own_places(members, info, got):
    return got[pl.ds(info[0] * members, members), 0, LANES : 2 * LANES]


def slot_hot(members, groups, slots, info, place_rows, column, mr, tokens):
    column[...] = row_to_col(place_rows[pl.ds(mr, 1), :])
    place = [
        column[pl.ds(pl.multiple_of((info[0] ^ d) * slots, slots), slots), :]
        for d in range(groups)
    ]
    return jnp.concatenate(place, axis=0) == iota((groups * slots, tokens), 1) + 1


def pick_kernel(members, groups, slots, info, got, *refs):
    encs = refs[:members]
    outs = refs[members : members + groups]
    place_rows, column = refs[members + groups :]
    place_rows[...] = own_places(members, info, got)
    for e in range(members):
        mr = info[1] ^ e
        tokens = encs[e].shape[0]
        hot = as_bf16(slot_hot(members, groups, slots, info, place_rows, column, mr, tokens))
        hi, mid, low = split3(encs[e][...])
        found = (dot1(hot, hi, NN) + dot1(hot, mid, NN)) + dot1(hot, low, NN)
        at = pl.ds(pl.multiple_of(mr * slots, slots), slots)
        for d in range(groups):
            outs[d][at, :] = found[d * slots : (d + 1) * slots]


def positive_kernel(members, groups, slots, tokens, info, got, stats, *refs):
    rows, picked = refs[:groups], refs[groups : 2 * groups]
    joined, own, place_rows, column = refs[2 * groups :]
    place_rows[...] = own_places(members, info, got)
    for e in range(members):
        mr = info[1] ^ e
        lanes = pl.ds(pl.multiple_of(mr * tokens, LANES), tokens)
        at = pl.ds(pl.multiple_of(mr * slots, slots), slots)
        hot = slot_hot(members, groups, slots, info, place_rows, column, mr, tokens)
        row = jnp.concatenate([r[at, :] for r in rows], axis=0)
        enc = jnp.concatenate([p[at, :] for p in picked], axis=0)
        value = jnp.sum(row * enc, axis=1, keepdims=True)
        positive = jnp.sum(jnp.where(hot, value, 0.0), axis=0, keepdims=True)
        has = jnp.sum(hot.astype(F32), axis=0, keepdims=True)
        old = stats[0:1, lanes]
        top = jnp.where(has > 0, jnp.maximum(old, positive), old)
        joined[0:1, lanes] = top
        joined[1:2, lanes] = stats[1:2, lanes] * jnp.exp(old - top) + jnp.where(
            has > 0, jnp.exp(positive - top), 0.0
        )
        own[0:1, lanes] = positive
        own[1:2, lanes] = has


def pulled_kernel(members, groups, slots, blocks, info, got, *refs):
    negs, refs = refs[:groups], refs[groups:]
    rows, refs = refs[:groups], refs[groups:]
    prob_hi, prob_lo, pulled, row_t, place_rows, column = refs
    place_rows[...] = own_places(members, info, got)
    neg = jnp.concatenate([row[...] for row in negs], axis=0)
    neg_t = split(jnp.transpose(neg))
    tokens = pulled.shape[2]
    for i, e in enumerate(blocks):
        mr = info[1] ^ e
        pulled[i] = dot3(neg_t, (prob_hi[i], prob_lo[i]), NN)
        at = pl.ds(pl.multiple_of(mr * slots, slots), slots)
        hot = slot_hot(members, groups, slots, info, place_rows, column, mr, tokens)
        high, low = split(jnp.concatenate([r[at, :] for r in rows], axis=0))
        row_t[i] = dot1(high, as_bf16(hot), TN) + dot1(low, as_bf16(hot), TN)


def join(first, second):
    top = jnp.maximum(first[0:1], second[0:1])
    total = first[1:2] * jnp.exp(first[0:1] - top) + second[1:2] * jnp.exp(second[0:1] - top)
    return top, total


def join_kernel(first, second, *refs):
    out = refs[-1]
    top, total = join(first[...], second[...])
    out[0:1, :] = top
    out[1:2, :] = total


def shares(info, e, tokens, final, stats, own):
    lanes = pl.ds(pl.multiple_of((info[1] ^ e) * tokens, LANES), tokens)
    top, total = final[0:1, lanes], final[1:2, lanes]
    scale = jnp.exp(stats[0:1, lanes] - top) / total
    extra = jnp.where(
        own[1:2, lanes] > 0, jnp.exp(own[0:1, lanes] - top) / total - 1.0, 0.0
    )
    return scale, extra


def pull_kernel(halves, blocks, tokens, info, final, stats, own, *refs):
    for e, out in zip(blocks, refs[-len(blocks) :]):
        h = 0 if e in halves[0] else 1
        pulled, row_t = (ref[halves[h].index(e)] for ref in refs[2 * h : 2 * h + 2])
        scale, extra = shares(info, e, tokens, final, stats, own)
        out[...] = pulled * scale + row_t * extra


def flat(table, lane, slots):
    return jnp.concatenate(
        [table[m : m + 1, lane : lane + slots] for m in range(table.shape[0])], axis=1
    )


def grad_kernel(members, groups, slots, halves, info, got, final, stats, own, *refs):
    probs, refs = refs[: 2 * len(halves)], refs[2 * len(halves) :]
    encs = refs[:members]
    *outs, total, coef, place_rows = refs[-groups - 3 :]
    place_rows[...] = own_places(members, info, got)
    tokens, width = encs[0].shape
    for h, i, e in [(h, i, e) for h, blocks in enumerate(halves) for i, e in enumerate(blocks)]:
        mr = info[1] ^ e
        scale, extra = shares(info, e, tokens, final, stats, own)
        enc = split(encs[e][...] * row_to_col(scale))
        part = dot3((probs[2 * h][i], probs[2 * h + 1][i]), enc, NN)
        if h == 0 and i == 0:
            total[...] = part
        else:
            total[...] += part
        hot = place_rows[pl.ds(mr, 1), :] == iota((tokens, LANES), 0) + 1
        coef[pl.ds(mr, 1), :] = jnp.sum(
            jnp.where(hot, row_to_col(extra), 0.0), axis=0, keepdims=True
        )
    count = total.shape[0] // groups
    lines = [flat(coef[...], g * slots, slots) for g in range(groups)]
    for d, out in enumerate(outs):
        out[0:count, :] = total[d * count : (d + 1) * count, :]
        line = lines[0]
        for g in range(1, groups):
            line = jnp.where((info[0] ^ d) == g, lines[g], line)
        out[count:, 0 : line.shape[1]] = jnp.broadcast_to(line, (8, line.shape[1]))


def equal_in_batch(ids):
    size = ids.shape[1]
    across = jnp.broadcast_to(ids.astype(F32), (size, size))
    same = (jnp.transpose(across) == across) & (
        (iota((size, size), 0) // BATCH) == (iota((size, size), 1) // BATCH)
    )
    return same.astype(F32)


def scatter_kernel(members, groups, own, slots, count, info, got_v, got, *refs):
    size = len(own)
    grads, picked = refs[:size], refs[size : 2 * size]
    out, negs, tgts = refs[-3:]
    out[...] = refs[2 * size][...] if own[0] else jnp.zeros_like(out)

    def add_rows(asked, first, source, base, number):
        for b in range(0, number, BATCH):
            rows = [asked[first + b + k] for k in range(BATCH)]
            new = [
                out[pl.ds(rows[k], 1), :] + source[pl.ds(base + b + k, 1), :]
                for k in range(BATCH)
            ]
            for k in range(BATCH):
                out[pl.ds(rows[k], 1), :] = new[k]

    for i, d in enumerate(own):
        g = info[0] ^ d
        asked = got_v[pl.ds(g * members, members), 0, 0:LANES]
        number = members * count
        same = as_bf16(equal_in_batch(flat(asked, slots, count)) > 0)
        high, low = split(grads[i][0:number, :])
        negs[...] = dot1(same, high, NN) + dot1(same, low, NN)
        weight = equal_in_batch(flat(asked, 0, slots))
        weight = weight * grads[i][number : number + 1, 0 : members * slots]
        tgts[...] = dot3(split(weight), split(picked[i][...]), NN)
        merged = BATCH // count if count < BATCH else 1

        def member(step, carry, g=g, merged=merged):
            if merged == 1:
                add_rows(got.at[g * members + step, 0], slots, negs, step * count, count)
                add_rows(got.at[g * members + step, 0], 0, tgts, step * slots, slots)
                return carry
            first = g * members + step * merged
            rows = [
                got[first + k // count, 0, slots + k % count] for k in range(BATCH)
            ]
            new = [
                out[pl.ds(rows[k], 1), :] + negs[pl.ds(step * BATCH + k, 1), :]
                for k in range(BATCH)
            ]
            for k in range(BATCH):
                out[pl.ds(rows[k], 1), :] = new[k]
            for m in range(merged):
                add_rows(got.at[first + m, 0], 0, tgts, (step * merged + m) * slots, slots)
            return carry

        lax.fori_loop(0, members // merged, member, 0)


def add_kernel(terms, *refs):
    total = refs[0][...]
    for ref in refs[1:terms]:
        total = total + ref[...]
    refs[-1][...] = total


def finish_kernel(valid, *refs):
    total = refs[0][...]
    for ref in refs[1:-1]:
        total = total + ref[...]
    refs[-1][...] = jnp.transpose(total) * row_to_col(valid[...].astype(F32))


def swap(value, axis, d):
    return lax.ppermute(value, axis, [(i, i ^ d) for i in range(lax.axis_size(axis))])


def shards(encoded, item_table, target_owner, target_local, negative_ids, valid):
    groups, members = lax.axis_size("group"), lax.axis_size("member")
    devices = groups * members
    tokens, width = encoded.shape
    rows_dev = item_table.shape[0]
    negatives = negative_ids.shape[0]
    slots = max(2, 4 * tokens // devices)
    count = negatives // devices
    near = max(1, members // 4)
    everyone = members * tokens
    shape = jax.ShapeDtypeStruct
    sds = lambda *s: shape(s, F32)

    info = jnp.stack([lax.axis_index("group"), lax.axis_index("member")]).astype(I32)
    ints = jnp.concatenate([target_owner.reshape(-1), target_local, valid, negative_ids])
    request, masked = call(
        functools.partial(front_kernel, members, rows_dev, slots, tokens, negatives),
        [shape((devices, 1, 2 * LANES), I32), sds(tokens, width)],
        [SMEM] + [VMEM] * 2,
        [VMEM] * 2,
        (info, ints.reshape(1, -1), encoded),
        name="front",
    )
    got = lax.all_to_all(
        request, ("group", "member"), split_axis=0, concat_axis=0, tiled=True
    )

    encs = [masked] + [None] * (members - 1)
    for z in (near, 2 * near):
        encs[z] = swap(masked, "member", z)
    onward, got = lax.optimization_barrier((encs[2 * near], got))
    encs[3 * near] = swap(onward, "member", near)
    for z in range(0, members, near):
        for x in range(1, near):
            encs[z ^ x] = swap(onward if z == 2 * near else encs[z], "member", x)
    halves = [[d for d in range(members) if (d < near) or d in (near, 2 * near)], []]
    halves[1] = [d for d in range(members) if d not in halves[0]]

    early = [encs[d] for d in halves[0] if d]
    gather = lambda part, many, deps, name: call(
        functools.partial(gather_kernel, members, groups, part, many),
        [sds(members * many, width)] * groups,
        [SMEM, SMEM, VMEM] + [ANY] * len(deps),
        [VMEM] * groups,
        (info, got, item_table, *deps),
        name=name,
    )
    negs = gather(slots, count, early, "gather_negatives")
    negs = [negs[0]] + [swap(negs[d], "group", d) for d in range(1, groups)]
    rows = gather(0, slots, [], "gather_targets")
    rows = [rows[0]] + [swap(rows[d], "group", d) for d in range(1, groups)]

    stats, probs = [], []
    for blocks in halves:
        many = len(blocks)
        *stats, hi, lo = call(
            functools.partial(score_kernel, blocks, groups),
            [sds(2, everyone)] + [shape((many, negatives, tokens), BF16)] * 2,
            [SMEM] + [VMEM] * (groups + many + len(stats)),
            [VMEM] * 3,
            (info, *negs, *[encs[e] for e in blocks], *stats),
            flops=12 * many * tokens * negatives * width,
            moved=MIB,
            name="score",
        )
        probs += [hi, lo]
    stats = stats[0]
    picked = call(
        functools.partial(pick_kernel, members, groups, slots),
        [sds(members * slots, width)] * groups,
        [SMEM] + [VMEM] * (1 + members),
        [VMEM] * groups,
        (info, got, *encs),
        scratch=[pltpu.VMEM((members, LANES), I32), pltpu.VMEM((LANES, 1), I32)],
        name="pick",
    )
    sent = [picked[0]] + [swap(picked[d], "group", d) for d in range(1, groups)]
    joined, own = call(
        functools.partial(positive_kernel, members, groups, slots, tokens),
        [sds(2, everyone)] * 2,
        [SMEM] + [VMEM] * (2 + 2 * groups),
        [VMEM] * 2,
        (info, got, stats, *rows, *picked),
        scratch=[pltpu.VMEM((members, LANES), I32), pltpu.VMEM((LANES, 1), I32)],
        name="positive",
    )
    pulled = []
    for h, blocks in enumerate(halves):
        pulled += call(
            functools.partial(pulled_kernel, members, groups, slots, blocks),
            [sds(len(blocks), width, tokens)] * 2,
            [SMEM] + [VMEM] * (3 + 2 * groups),
            [VMEM] * 2,
            (info, got, *negs, *rows, *probs[2 * h : 2 * h + 2]),
            scratch=[pltpu.VMEM((members, LANES), I32), pltpu.VMEM((LANES, 1), I32)],
            flops=6 * len(blocks) * tokens * negatives * width,
            moved=MIB,
            name="pulled",
        )

    final = joined
    d, hops = 1, 0
    while d < members:
        late = pulled[2 * hops : 2 * hops + 2]
        hops += 1
        final = call(
            join_kernel,
            sds(2, everyone),
            [VMEM] * 2 + [ANY] * len(late),
            VMEM,
            (final, swap(final, "member", d), *late),
            name="join",
        )
        d *= 2

    grads = call(
        functools.partial(grad_kernel, members, groups, slots, halves),
        [sds(members * count + 8, width)] * groups,
        [SMEM] + [VMEM] * (4 + len(probs) + members) + [ANY] * (groups - 1),
        [VMEM] * groups,
        (info, got, final, stats, own, *probs, *encs, *sent[1:]),
        scratch=[
            pltpu.VMEM((negatives, width), F32),
            pltpu.VMEM((members, LANES), F32),
            pltpu.VMEM((members, LANES), I32),
        ],
        flops=6 * everyone * negatives * width,
        moved=8 * MIB,
        name="grad",
    )
    def added(terms, deps):
        return call(
            functools.partial(add_kernel, len(terms)),
            sds(width, tokens),
            [VMEM] * len(terms) + [ANY] * len(deps),
            VMEM,
            (*terms, *deps),
            name="add",
        )

    graded = [grads[0]]
    grads = graded + [swap(grads[d], "group", d) for d in range(1, groups)]
    def scaled(blocks, deps):
        return call(
            functools.partial(pull_kernel, halves, blocks, tokens),
            [sds(width, tokens)] * len(blocks),
            [SMEM] + [VMEM] * 7 + [ANY] * len(deps),
            [VMEM] * len(blocks),
            (info, final, stats, own, *pulled, *deps),
            name="pull",
        )

    def beside(blocks):
        return [swap(block, "member", x) for x, block in enumerate(blocks, 1)]

    along = list(range(near))
    def scatter(own, base, deps, flops):
        return call(
            functools.partial(scatter_kernel, members, groups, own, slots, count),
            sds(rows_dev, width),
            [SMEM, VMEM, SMEM] + [VMEM] * (2 * len(own) + len(base)) + [ANY] * len(deps),
            VMEM,
            (info, got, got, *[grads[d] for d in own], *[sent[d] for d in own], *base, *deps),
            scratch=[
                pltpu.VMEM((members * count, width), F32),
                pltpu.VMEM((members * slots, width), F32),
            ],
            flops=flops,
            name="scatter",
        )

    table_own = scatter([0], [], grads[1:], 1 << 33)
    farthest, *rest, nearest = scaled([3 * near + x for x in along] + [near], [])
    arrived = beside(rest)
    nearest = swap(nearest, "member", near)
    far, *others = scaled([2 * near + x for x in along], [*arrived, nearest, *graded])
    total = swap(added([farthest, *arrived], graded), "member", near)
    half = added([far, *beside(others)], [table_own])
    close = [*along[1:], *[near + x for x in along[1:]]]
    kept, *sends = scaled([0, *close], [half])
    parts = [swap(block, "member", d) for d, block in zip(close, sends)]
    parts += [nearest, kept, swap(added([half, total], []), "member", 2 * near)]

    table_grad = scatter(list(range(1, groups)), [table_own], [], 0)
    encoded_grad = call(
        finish_kernel,
        sds(tokens, width),
        [VMEM] * (1 + len(parts)),
        VMEM,
        (valid.reshape(1, -1), *parts),
        name="finish",
    )
    return (encoded_grad, table_grad)


def solution(mesh):
    placed = (
        P(("group", "member"), None),
        P(("group", "member"), None),
        P(("group", "member"), None),
        P(("group", "member")),
        P(("group", "member")),
        P(("group", "member")),
    )
    return jax.shard_map(
        shards,
        mesh=mesh,
        in_specs=placed,
        out_specs=(P(("group", "member"), None), P(("group", "member"), None)),
        check_vma=False,
    )
```

```python
import functools

import jax
import jax.numpy as jnp
from jax import lax
from jax.experimental import pallas as pl
from jax.experimental.pallas import tpu as pltpu
from jax.sharding import PartitionSpec as P

F32 = jnp.float32
BF16 = jnp.bfloat16
I32 = jnp.int32
LANES = 128
VMEM = pl.BlockSpec(memory_space=pltpu.VMEM)
ANY = pl.BlockSpec(memory_space=pl.ANY)
SMEM = pl.BlockSpec(memory_space=pltpu.SMEM)
MIB = 1 << 20
BATCH = 8

NN = (((1,), (0,)), ((), ()))
NT = (((1,), (1,)), ((), ()))
TN = (((0,), (0,)), ((), ()))


def call(kernel, out_shape, ins, outs, args, scratch=(), limit=10, flops=0, moved=0, name=None):
    return pl.pallas_call(
        kernel,
        out_shape=out_shape,
        in_specs=ins,
        out_specs=outs,
        scratch_shapes=list(scratch),
        compiler_params=pltpu.CompilerParams(vmem_limit_bytes=limit * MIB),
        cost_estimate=pl.CostEstimate(flops=flops, bytes_accessed=moved, transcendentals=0),
        name=name,
    )(*args)


def iota(shape, dim):
    return lax.broadcasted_iota(I32, shape, dim)


def as_bf16(flag):
    return flag.astype(F32).astype(BF16)


def dot1(a, b, dims):
    return lax.dot_general(a, b, dims, preferred_element_type=F32)


def split(x):
    hi = x.astype(BF16)
    return hi, (x - hi.astype(F32)).astype(BF16)


def dot3(a, b, dims):
    return dot1(a[0], b[0], dims) + (dot1(a[0], b[1], dims) + dot1(a[1], b[0], dims))


def row_to_col(row):
    return jnp.transpose(jnp.broadcast_to(row, (LANES, row.shape[1])))[:, 0:1]


def split3(x):
    hi = x.astype(BF16)
    rest = x - hi.astype(F32)
    mid = rest.astype(BF16)
    return hi, mid, (rest - mid.astype(F32)).astype(BF16)


def dot6(a, b, dims):
    small = dot1(a[2], b[0], dims) + dot1(a[1], b[1], dims) + dot1(a[0], b[2], dims)
    return (small + (dot1(a[1], b[0], dims) + dot1(a[0], b[1], dims))) + dot1(a[0], b[0], dims)


def copy_rows(source, row_of, target, base, count):
    for b in range(0, count, BATCH):
        rows = [source[pl.ds(row_of(b + k), 1), :] for k in range(BATCH)] if count % BATCH == 0 else None
        if rows is None:
            for k in range(count):
                target[pl.ds(base + k, 1), :] = source[pl.ds(row_of(k), 1), :]
            return
        target[pl.ds(pl.multiple_of(base + b, BATCH), BATCH), :] = jnp.concatenate(rows, axis=0)


def front_kernel(members, rows_dev, slots, tokens, negatives, info, ints, enc_ref, out_ref, masked_ref):
    devices = out_ref.shape[0]
    shift = rows_dev.bit_length() - 1
    owner = ints[:, 0:tokens]
    local = ints[:, tokens : 2 * tokens]
    valid = ints[:, 2 * tokens : 3 * tokens]
    ids = ints[:, 3 * tokens :]
    masked_ref[...] = enc_ref[...] * row_to_col(valid.astype(F32))

    def ranks(owner_row, count):
        hot = iota((devices, count), 0) == owner_row
        before = as_bf16(iota((count, count), 0) < iota((count, count), 1))
        seen = dot1(as_bf16(hot), before, NN)
        return hot, jnp.sum(jnp.where(hot, seen, 0.0), axis=0, keepdims=True).astype(I32)

    def table(hot, value, place):
        return dot1(jnp.where(hot, value, 0.0).astype(BF16), place, NT)

    def placed(lane_row, count):
        return as_bf16(iota((LANES, count), 0) == lane_row)

    hot, rank = ranks(owner, tokens)
    place = placed(rank, tokens)
    high = table(hot, (local >> 6).astype(F32), place)
    low = table(hot, (local & 63).astype(F32), place)
    group = owner >> (members.bit_length() - 1)
    hot_member = (iota((devices, tokens), 0) & (members - 1)) == (owner & (members - 1))
    position = table(
        hot_member, (iota((1, tokens), 1) + 1).astype(F32), placed(group * slots + rank, tokens)
    )

    hot, rank = ranks(ids >> shift, negatives)
    place = placed(rank + slots, negatives)
    local = ids & (rows_dev - 1)
    high = high + table(hot, (local >> 6).astype(F32), place)
    low = low + table(hot, (local & 63).astype(F32), place)
    out_ref[:, 0, 0:LANES] = high.astype(I32) * 64 + low.astype(I32)
    out_ref[:, 0, LANES : 2 * LANES] = position.astype(I32)


def gather_kernel(members, groups, part, count, info, got, table, *refs):
    for d, out in enumerate(refs[-groups:]):
        first = (info[0] ^ d) * members

        def member(mr, carry, out=out, first=first):
            asked = got.at[first + mr, 0]
            copy_rows(table, lambda k: asked[part + k], out, mr * count, count)
            return carry

        lax.fori_loop(0, members, member, 0)


def score_kernel(blocks, groups, info, *refs):
    rows, refs = refs[:groups], refs[groups:]
    encs, refs = refs[: len(blocks)], refs[len(blocks) :]
    stats, prob_hi, prob_lo = refs[-3:]
    if len(refs) > 3:
        stats[...] = refs[0][...]
    tokens = encs[0].shape[0]
    neg = split3(jnp.concatenate([row[...] for row in rows], axis=0))
    for i, e in enumerate(blocks):
        lanes = pl.ds(pl.multiple_of((info[1] ^ e) * tokens, LANES), tokens)
        score = dot6(neg, split3(encs[i][...]), NT)
        top = jnp.max(score, axis=0, keepdims=True)
        prob = jnp.exp(score - top)
        stats[0:1, lanes] = top
        stats[1:2, lanes] = jnp.sum(prob, axis=0, keepdims=True)
        parts = split(prob)
        prob_hi[i] = parts[0]
        prob_lo[i] = parts[1]


def own_places(members, info, got):
    return got[pl.ds(info[0] * members, members), 0, LANES : 2 * LANES]


def slot_hot(members, groups, slots, info, place_rows, column, mr, tokens):
    column[...] = row_to_col(place_rows[pl.ds(mr, 1), :])
    place = [
        column[pl.ds(pl.multiple_of((info[0] ^ d) * slots, slots), slots), :]
        for d in range(groups)
    ]
    return jnp.concatenate(place, axis=0) == iota((groups * slots, tokens), 1) + 1


def pick_kernel(members, groups, slots, info, got, *refs):
    encs = refs[:members]
    outs = refs[members : members + groups]
    place_rows, column = refs[members + groups :]
    place_rows[...] = own_places(members, info, got)
    for e in range(members):
        mr = info[1] ^ e
        tokens = encs[e].shape[0]
        hot = as_bf16(slot_hot(members, groups, slots, info, place_rows, column, mr, tokens))
        hi, mid, low = split3(encs[e][...])
        found = (dot1(hot, hi, NN) + dot1(hot, mid, NN)) + dot1(hot, low, NN)
        at = pl.ds(pl.multiple_of(mr * slots, slots), slots)
        for d in range(groups):
            outs[d][at, :] = found[d * slots : (d + 1) * slots]


def positive_kernel(members, groups, slots, tokens, info, got, stats, *refs):
    rows, picked = refs[:groups], refs[groups : 2 * groups]
    joined, own, place_rows, column = refs[2 * groups :]
    place_rows[...] = own_places(members, info, got)
    for e in range(members):
        mr = info[1] ^ e
        lanes = pl.ds(pl.multiple_of(mr * tokens, LANES), tokens)
        at = pl.ds(pl.multiple_of(mr * slots, slots), slots)
        hot = slot_hot(members, groups, slots, info, place_rows, column, mr, tokens)
        row = jnp.concatenate([r[at, :] for r in rows], axis=0)
        enc = jnp.concatenate([p[at, :] for p in picked], axis=0)
        value = jnp.sum(row * enc, axis=1, keepdims=True)
        positive = jnp.sum(jnp.where(hot, value, 0.0), axis=0, keepdims=True)
        has = jnp.sum(hot.astype(F32), axis=0, keepdims=True)
        old = stats[0:1, lanes]
        top = jnp.where(has > 0, jnp.maximum(old, positive), old)
        joined[0:1, lanes] = top
        joined[1:2, lanes] = stats[1:2, lanes] * jnp.exp(old - top) + jnp.where(
            has > 0, jnp.exp(positive - top), 0.0
        )
        own[0:1, lanes] = positive
        own[1:2, lanes] = has


def pulled_kernel(members, groups, slots, blocks, info, got, *refs):
    negs, refs = refs[:groups], refs[groups:]
    rows, refs = refs[:groups], refs[groups:]
    prob_hi, prob_lo, pulled, row_t, place_rows, column = refs
    place_rows[...] = own_places(members, info, got)
    neg = jnp.concatenate([row[...] for row in negs], axis=0)
    neg_t = split(jnp.transpose(neg))
    tokens = pulled.shape[2]
    for i, e in enumerate(blocks):
        mr = info[1] ^ e
        pulled[i] = dot3(neg_t, (prob_hi[i], prob_lo[i]), NN)
        at = pl.ds(pl.multiple_of(mr * slots, slots), slots)
        hot = slot_hot(members, groups, slots, info, place_rows, column, mr, tokens)
        high, low = split(jnp.concatenate([r[at, :] for r in rows], axis=0))
        row_t[i] = dot1(high, as_bf16(hot), TN) + dot1(low, as_bf16(hot), TN)


def join(first, second):
    top = jnp.maximum(first[0:1], second[0:1])
    total = first[1:2] * jnp.exp(first[0:1] - top) + second[1:2] * jnp.exp(second[0:1] - top)
    return top, total


def join_kernel(first, second, *refs):
    out = refs[-1]
    top, total = join(first[...], second[...])
    out[0:1, :] = top
    out[1:2, :] = total


def shares(info, e, tokens, final, stats, own):
    lanes = pl.ds(pl.multiple_of((info[1] ^ e) * tokens, LANES), tokens)
    top, total = final[0:1, lanes], final[1:2, lanes]
    scale = jnp.exp(stats[0:1, lanes] - top) / total
    extra = jnp.where(
        own[1:2, lanes] > 0, jnp.exp(own[0:1, lanes] - top) / total - 1.0, 0.0
    )
    return scale, extra


def pull_kernel(halves, blocks, tokens, info, final, stats, own, *refs):
    for e, out in zip(blocks, refs[-len(blocks) :]):
        h = 0 if e in halves[0] else 1
        pulled, row_t = (ref[halves[h].index(e)] for ref in refs[2 * h : 2 * h + 2])
        scale, extra = shares(info, e, tokens, final, stats, own)
        out[...] = pulled * scale + row_t * extra


def flat(table, lane, slots):
    return jnp.concatenate(
        [table[m : m + 1, lane : lane + slots] for m in range(table.shape[0])], axis=1
    )


def grad_kernel(members, groups, slots, halves, info, got, final, stats, own, *refs):
    probs, refs = refs[: 2 * len(halves)], refs[2 * len(halves) :]
    encs = refs[:members]
    *outs, total, coef, place_rows = refs[-groups - 3 :]
    place_rows[...] = own_places(members, info, got)
    tokens, width = encs[0].shape
    for h, i, e in [(h, i, e) for h, blocks in enumerate(halves) for i, e in enumerate(blocks)]:
        mr = info[1] ^ e
        scale, extra = shares(info, e, tokens, final, stats, own)
        enc = split(encs[e][...] * row_to_col(scale))
        part = dot3((probs[2 * h][i], probs[2 * h + 1][i]), enc, NN)
        if h == 0 and i == 0:
            total[...] = part
        else:
            total[...] += part
        hot = place_rows[pl.ds(mr, 1), :] == iota((tokens, LANES), 0) + 1
        coef[pl.ds(mr, 1), :] = jnp.sum(
            jnp.where(hot, row_to_col(extra), 0.0), axis=0, keepdims=True
        )
    count = total.shape[0] // groups
    lines = [flat(coef[...], g * slots, slots) for g in range(groups)]
    for d, out in enumerate(outs):
        out[0:count, :] = total[d * count : (d + 1) * count, :]
        line = lines[0]
        for g in range(1, groups):
            line = jnp.where((info[0] ^ d) == g, lines[g], line)
        out[count:, 0 : line.shape[1]] = jnp.broadcast_to(line, (8, line.shape[1]))


def equal_in_batch(ids):
    size = ids.shape[1]
    across = jnp.broadcast_to(ids.astype(F32), (size, size))
    same = (jnp.transpose(across) == across) & (
        (iota((size, size), 0) // BATCH) == (iota((size, size), 1) // BATCH)
    )
    return same.astype(F32)


def scatter_kernel(members, groups, own, slots, count, info, got_v, got, *refs):
    size = len(own)
    grads, picked = refs[:size], refs[size : 2 * size]
    out, negs, tgts = refs[-3:]
    out[...] = refs[2 * size][...] if own[0] else jnp.zeros_like(out)

    def add_rows(asked, first, source, base, number):
        for b in range(0, number, BATCH):
            rows = [asked[first + b + k] for k in range(BATCH)]
            new = [
                out[pl.ds(rows[k], 1), :] + source[pl.ds(base + b + k, 1), :]
                for k in range(BATCH)
            ]
            for k in range(BATCH):
                out[pl.ds(rows[k], 1), :] = new[k]

    for i, d in enumerate(own):
        g = info[0] ^ d
        asked = got_v[pl.ds(g * members, members), 0, 0:LANES]
        number = members * count
        same = as_bf16(equal_in_batch(flat(asked, slots, count)) > 0)
        high, low = split(grads[i][0:number, :])
        negs[...] = dot1(same, high, NN) + dot1(same, low, NN)
        weight = equal_in_batch(flat(asked, 0, slots))
        weight = weight * grads[i][number : number + 1, 0 : members * slots]
        tgts[...] = dot3(split(weight), split(picked[i][...]), NN)
        merged = BATCH // count if count < BATCH else 1

        def member(step, carry, g=g, merged=merged):
            if merged == 1:
                add_rows(got.at[g * members + step, 0], slots, negs, step * count, count)
                add_rows(got.at[g * members + step, 0], 0, tgts, step * slots, slots)
                return carry
            first = g * members + step * merged
            rows = [
                got[first + k // count, 0, slots + k % count] for k in range(BATCH)
            ]
            new = [
                out[pl.ds(rows[k], 1), :] + negs[pl.ds(step * BATCH + k, 1), :]
                for k in range(BATCH)
            ]
            for k in range(BATCH):
                out[pl.ds(rows[k], 1), :] = new[k]
            for m in range(merged):
                add_rows(got.at[first + m, 0], 0, tgts, (step * merged + m) * slots, slots)
            return carry

        lax.fori_loop(0, members // merged, member, 0)


def add_kernel(terms, *refs):
    total = refs[0][...]
    for ref in refs[1:terms]:
        total = total + ref[...]
    refs[-1][...] = total


def finish_kernel(valid, *refs):
    total = refs[0][...]
    for ref in refs[1:-1]:
        total = total + ref[...]
    refs[-1][...] = jnp.transpose(total) * row_to_col(valid[...].astype(F32))


def swap(value, axis, d):
    return lax.ppermute(value, axis, [(i, i ^ d) for i in range(lax.axis_size(axis))])


def shards(encoded, item_table, target_owner, target_local, negative_ids, valid):
    groups, members = lax.axis_size("group"), lax.axis_size("member")
    devices = groups * members
    tokens, width = encoded.shape
    rows_dev = item_table.shape[0]
    negatives = negative_ids.shape[0]
    slots = max(2, 4 * tokens // devices)
    count = negatives // devices
    near = max(1, members // 4)
    everyone = members * tokens
    shape = jax.ShapeDtypeStruct
    sds = lambda *s: shape(s, F32)

    info = jnp.stack([lax.axis_index("group"), lax.axis_index("member")]).astype(I32)
    ints = jnp.concatenate([target_owner.reshape(-1), target_local, valid, negative_ids])
    request, masked = call(
        functools.partial(front_kernel, members, rows_dev, slots, tokens, negatives),
        [shape((devices, 1, 2 * LANES), I32), sds(tokens, width)],
        [SMEM] + [VMEM] * 2,
        [VMEM] * 2,
        (info, ints.reshape(1, -1), encoded),
        name="front",
    )
    got = lax.all_to_all(
        request, ("group", "member"), split_axis=0, concat_axis=0, tiled=True
    )

    encs = [masked] + [None] * (members - 1)
    for z in (near, 2 * near):
        encs[z] = swap(masked, "member", z)
    onward, got = lax.optimization_barrier((encs[2 * near], got))
    encs[3 * near] = swap(onward, "member", near)
    for z in (0, 2 * near, 3 * near):
        for x in range(1, near):
            encs[z ^ x] = swap(onward if z == 2 * near else encs[z], "member", x)
    halves = [[d for d in range(members) if (d < near) or d in (near, 2 * near)], []]
    halves[1] = [d for d in range(members) if d not in halves[0]]

    early = [encs[d] for d in halves[0] if d]
    gather = lambda part, many, deps, name: call(
        functools.partial(gather_kernel, members, groups, part, many),
        [sds(members * many, width)] * groups,
        [SMEM, SMEM, VMEM] + [ANY] * len(deps),
        [VMEM] * groups,
        (info, got, item_table, *deps),
        name=name,
    )
    negs = gather(slots, count, early, "gather_negatives")
    for x in range(1, near):
        encs[near + x] = swap(lax.optimization_barrier((encs[x], negs[0]))[0], "member", near)
    negs = [negs[0]] + [swap(negs[d], "group", d) for d in range(1, groups)]
    rows = gather(0, slots, [encs[2 * near + x] for x in range(1, near)], "gather_targets")
    rows = [rows[0]] + [swap(rows[d], "group", d) for d in range(1, groups)]

    stats, probs = [], []
    for blocks in halves:
        many = len(blocks)
        *stats, hi, lo = call(
            functools.partial(score_kernel, blocks, groups),
            [sds(2, everyone)] + [shape((many, negatives, tokens), BF16)] * 2,
            [SMEM] + [VMEM] * (groups + many + len(stats)),
            [VMEM] * 3,
            (info, *negs, *[encs[e] for e in blocks], *stats),
            flops=12 * many * tokens * negatives * width,
            moved=MIB,
            name="score",
        )
        probs += [hi, lo]
    stats = stats[0]
    picked = call(
        functools.partial(pick_kernel, members, groups, slots),
        [sds(members * slots, width)] * groups,
        [SMEM] + [VMEM] * (1 + members),
        [VMEM] * groups,
        (info, got, *encs),
        scratch=[pltpu.VMEM((members, LANES), I32), pltpu.VMEM((LANES, 1), I32)],
        name="pick",
    )
    sent = [picked[0]] + [swap(picked[d], "group", d) for d in range(1, groups)]
    joined, own = call(
        functools.partial(positive_kernel, members, groups, slots, tokens),
        [sds(2, everyone)] * 2,
        [SMEM] + [VMEM] * (2 + 2 * groups),
        [VMEM] * 2,
        (info, got, stats, *rows, *picked),
        scratch=[pltpu.VMEM((members, LANES), I32), pltpu.VMEM((LANES, 1), I32)],
        name="positive",
    )
    pulled = []
    for h, blocks in enumerate(halves):
        pulled += call(
            functools.partial(pulled_kernel, members, groups, slots, blocks),
            [sds(len(blocks), width, tokens)] * 2,
            [SMEM] + [VMEM] * (3 + 2 * groups),
            [VMEM] * 2,
            (info, got, *negs, *rows, *probs[2 * h : 2 * h + 2]),
            scratch=[pltpu.VMEM((members, LANES), I32), pltpu.VMEM((LANES, 1), I32)],
            flops=6 * len(blocks) * tokens * negatives * width,
            moved=MIB,
            name="pulled",
        )

    final = joined
    d, hops = 1, 0
    while d < members:
        late = pulled[2 * hops : 2 * hops + 2]
        hops += 1
        final = call(
            join_kernel,
            sds(2, everyone),
            [VMEM] * 2 + [ANY] * len(late),
            VMEM,
            (final, swap(final, "member", d), *late),
            name="join",
        )
        d *= 2

    grads = call(
        functools.partial(grad_kernel, members, groups, slots, halves),
        [sds(members * count + 8, width)] * groups,
        [SMEM] + [VMEM] * (4 + len(probs) + members) + [ANY] * (groups - 1),
        [VMEM] * groups,
        (info, got, final, stats, own, *probs, *encs, *sent[1:]),
        scratch=[
            pltpu.VMEM((negatives, width), F32),
            pltpu.VMEM((members, LANES), F32),
            pltpu.VMEM((members, LANES), I32),
        ],
        flops=6 * everyone * negatives * width,
        moved=8 * MIB,
        name="grad",
    )
    def added(terms, deps, flops=0):
        return call(
            functools.partial(add_kernel, len(terms)),
            sds(width, tokens),
            [VMEM] * len(terms) + [ANY] * len(deps),
            VMEM,
            (*terms, *deps),
            flops=flops,
            name="add",
        )

    graded = [grads[0]]
    grads = graded + [swap(grads[d], "group", d) for d in range(1, groups)]
    def scaled(blocks, deps):
        return call(
            functools.partial(pull_kernel, halves, blocks, tokens),
            [sds(width, tokens)] * len(blocks),
            [SMEM] + [VMEM] * 7 + [ANY] * len(deps),
            [VMEM] * len(blocks),
            (info, final, stats, own, *pulled, *deps),
            name="pull",
        )

    def beside(blocks):
        return [swap(block, "member", x) for x, block in enumerate(blocks, 1)]

    along = list(range(near))
    def scatter(own, base, deps, flops):
        return call(
            functools.partial(scatter_kernel, members, groups, own, slots, count),
            sds(rows_dev, width),
            [SMEM, VMEM, SMEM] + [VMEM] * (2 * len(own) + len(base)) + [ANY] * len(deps),
            VMEM,
            (info, got, got, *[grads[d] for d in own], *[sent[d] for d in own], *base, *deps),
            scratch=[
                pltpu.VMEM((members * count, width), F32),
                pltpu.VMEM((members * slots, width), F32),
            ],
            flops=flops,
            name="scatter",
        )

    farthest, *rest, nearest = scaled([3 * near + x for x in along] + [near], [])
    arrived = beside(rest)
    nearest = swap(nearest, "member", near)
    far, *others = scaled([2 * near + x for x in along], [*arrived, nearest, *graded])
    total = added([farthest, *arrived], graded)
    table_own = scatter([0], [], [total], 1 << 33)
    total = swap(total, "member", near)
    far = added([far], [table_own, *grads[1:]])
    half = added([far, *beside(others), total], [])
    close = [*along[1:], *[near + x for x in along[1:]]]
    kept, *sends = scaled([0, *close], [half])
    parts = [swap(block, "member", d) for d, block in zip(close, sends)]
    parts.append(added([nearest, kept, swap(half, "member", 2 * near)], []))

    table_grad = scatter(list(range(1, groups)), [table_own], [], 0)
    encoded_grad = call(
        finish_kernel,
        sds(tokens, width),
        [VMEM] * (1 + len(parts)),
        VMEM,
        (valid.reshape(1, -1), *parts),
        name="finish",
    )
    return (encoded_grad, table_grad)


def solution(mesh):
    placed = (
        P(("group", "member"), None),
        P(("group", "member"), None),
        P(("group", "member"), None),
        P(("group", "member")),
        P(("group", "member")),
        P(("group", "member")),
    )
    return jax.shard_map(
        shards,
        mesh=mesh,
        in_specs=placed,
        out_specs=(P(("group", "member"), None), P(("group", "member"), None)),
        check_vma=False,
    )
```

```python
import functools

import jax
import jax.numpy as jnp
from jax import lax
from jax.experimental import pallas as pl
from jax.experimental.pallas import tpu as pltpu
from jax.sharding import PartitionSpec as P

F32 = jnp.float32
BF16 = jnp.bfloat16
I32 = jnp.int32
LANES = 128
VMEM = pl.BlockSpec(memory_space=pltpu.VMEM)
ANY = pl.BlockSpec(memory_space=pl.ANY)
SMEM = pl.BlockSpec(memory_space=pltpu.SMEM)
MIB = 1 << 20
BATCH = 8

NN = (((1,), (0,)), ((), ()))
NT = (((1,), (1,)), ((), ()))
TN = (((0,), (0,)), ((), ()))


def call(kernel, out_shape, ins, outs, args, scratch=(), limit=10, flops=0, moved=0, name=None):
    return pl.pallas_call(
        kernel,
        out_shape=out_shape,
        in_specs=ins,
        out_specs=outs,
        scratch_shapes=list(scratch),
        compiler_params=pltpu.CompilerParams(vmem_limit_bytes=limit * MIB),
        cost_estimate=pl.CostEstimate(flops=flops, bytes_accessed=moved, transcendentals=0),
        name=name,
    )(*args)


def iota(shape, dim):
    return lax.broadcasted_iota(I32, shape, dim)


def as_bf16(flag):
    return flag.astype(F32).astype(BF16)


def dot1(a, b, dims):
    return lax.dot_general(a, b, dims, preferred_element_type=F32)


def split(x):
    hi = x.astype(BF16)
    return hi, (x - hi.astype(F32)).astype(BF16)


def dot3(a, b, dims):
    return dot1(a[0], b[0], dims) + (dot1(a[0], b[1], dims) + dot1(a[1], b[0], dims))


def row_to_col(row):
    return jnp.transpose(jnp.broadcast_to(row, (LANES, row.shape[1])))[:, 0:1]


def split3(x):
    hi = x.astype(BF16)
    rest = x - hi.astype(F32)
    mid = rest.astype(BF16)
    return hi, mid, (rest - mid.astype(F32)).astype(BF16)


def dot6(a, b, dims):
    small = dot1(a[2], b[0], dims) + dot1(a[1], b[1], dims) + dot1(a[0], b[2], dims)
    return (small + (dot1(a[1], b[0], dims) + dot1(a[0], b[1], dims))) + dot1(a[0], b[0], dims)


def copy_rows(source, row_of, target, base, count):
    for b in range(0, count, BATCH):
        rows = [source[pl.ds(row_of(b + k), 1), :] for k in range(BATCH)] if count % BATCH == 0 else None
        if rows is None:
            for k in range(count):
                target[pl.ds(base + k, 1), :] = source[pl.ds(row_of(k), 1), :]
            return
        target[pl.ds(pl.multiple_of(base + b, BATCH), BATCH), :] = jnp.concatenate(rows, axis=0)


def front_kernel(members, rows_dev, slots, tokens, negatives, info, ints, enc_ref, out_ref, masked_ref):
    devices = out_ref.shape[0]
    shift = rows_dev.bit_length() - 1
    owner = ints[:, 0:tokens]
    local = ints[:, tokens : 2 * tokens]
    valid = ints[:, 2 * tokens : 3 * tokens]
    ids = ints[:, 3 * tokens :]
    masked_ref[...] = enc_ref[...] * row_to_col(valid.astype(F32))

    def ranks(owner_row, count):
        hot = iota((devices, count), 0) == owner_row
        before = as_bf16(iota((count, count), 0) < iota((count, count), 1))
        seen = dot1(as_bf16(hot), before, NN)
        return hot, jnp.sum(jnp.where(hot, seen, 0.0), axis=0, keepdims=True).astype(I32)

    def table(hot, value, place):
        return dot1(jnp.where(hot, value, 0.0).astype(BF16), place, NT)

    def placed(lane_row, count):
        return as_bf16(iota((LANES, count), 0) == lane_row)

    hot, rank = ranks(owner, tokens)
    place = placed(rank, tokens)
    high = table(hot, (local >> 6).astype(F32), place)
    low = table(hot, (local & 63).astype(F32), place)
    group = owner >> (members.bit_length() - 1)
    hot_member = (iota((devices, tokens), 0) & (members - 1)) == (owner & (members - 1))
    position = table(
        hot_member, (iota((1, tokens), 1) + 1).astype(F32), placed(group * slots + rank, tokens)
    )

    hot, rank = ranks(ids >> shift, negatives)
    place = placed(rank + slots, negatives)
    local = ids & (rows_dev - 1)
    high = high + table(hot, (local >> 6).astype(F32), place)
    low = low + table(hot, (local & 63).astype(F32), place)
    out_ref[:, 0, 0:LANES] = high.astype(I32) * 64 + low.astype(I32)
    out_ref[:, 0, LANES : 2 * LANES] = position.astype(I32)


def gather_kernel(members, groups, part, count, info, got, table, *refs):
    for d, out in enumerate(refs[-groups:]):
        first = (info[0] ^ d) * members

        def member(mr, carry, out=out, first=first):
            asked = got.at[first + mr, 0]
            copy_rows(table, lambda k: asked[part + k], out, mr * count, count)
            return carry

        lax.fori_loop(0, members, member, 0)


def score_kernel(blocks, groups, info, *refs):
    rows, refs = refs[:groups], refs[groups:]
    encs, refs = refs[: len(blocks)], refs[len(blocks) :]
    stats, prob_hi, prob_lo = refs[-3:]
    if len(refs) > 3:
        stats[...] = refs[0][...]
    tokens = encs[0].shape[0]
    neg = split3(jnp.concatenate([row[...] for row in rows], axis=0))
    for i, e in enumerate(blocks):
        lanes = pl.ds(pl.multiple_of((info[1] ^ e) * tokens, LANES), tokens)
        score = dot6(neg, split3(encs[i][...]), NT)
        top = jnp.max(score, axis=0, keepdims=True)
        prob = jnp.exp(score - top)
        stats[0:1, lanes] = top
        stats[1:2, lanes] = jnp.sum(prob, axis=0, keepdims=True)
        parts = split(prob)
        prob_hi[i] = parts[0]
        prob_lo[i] = parts[1]


def own_places(members, info, got):
    return got[pl.ds(info[0] * members, members), 0, LANES : 2 * LANES]


def slot_hot(members, groups, slots, info, place_rows, column, mr, tokens):
    column[...] = row_to_col(place_rows[pl.ds(mr, 1), :])
    place = [
        column[pl.ds(pl.multiple_of((info[0] ^ d) * slots, slots), slots), :]
        for d in range(groups)
    ]
    return jnp.concatenate(place, axis=0) == iota((groups * slots, tokens), 1) + 1


def pick_kernel(members, groups, slots, info, got, *refs):
    encs = refs[:members]
    outs = refs[members : members + groups]
    place_rows, column = refs[members + groups :]
    place_rows[...] = own_places(members, info, got)
    for e in range(members):
        mr = info[1] ^ e
        tokens = encs[e].shape[0]
        hot = as_bf16(slot_hot(members, groups, slots, info, place_rows, column, mr, tokens))
        hi, mid, low = split3(encs[e][...])
        found = (dot1(hot, hi, NN) + dot1(hot, mid, NN)) + dot1(hot, low, NN)
        at = pl.ds(pl.multiple_of(mr * slots, slots), slots)
        for d in range(groups):
            outs[d][at, :] = found[d * slots : (d + 1) * slots]


def positive_kernel(members, groups, slots, tokens, info, got, stats, *refs):
    rows, picked = refs[:groups], refs[groups : 2 * groups]
    joined, own, place_rows, column = refs[2 * groups :]
    place_rows[...] = own_places(members, info, got)
    for e in range(members):
        mr = info[1] ^ e
        lanes = pl.ds(pl.multiple_of(mr * tokens, LANES), tokens)
        at = pl.ds(pl.multiple_of(mr * slots, slots), slots)
        hot = slot_hot(members, groups, slots, info, place_rows, column, mr, tokens)
        row = jnp.concatenate([r[at, :] for r in rows], axis=0)
        enc = jnp.concatenate([p[at, :] for p in picked], axis=0)
        value = jnp.sum(row * enc, axis=1, keepdims=True)
        positive = jnp.sum(jnp.where(hot, value, 0.0), axis=0, keepdims=True)
        has = jnp.sum(hot.astype(F32), axis=0, keepdims=True)
        old = stats[0:1, lanes]
        top = jnp.where(has > 0, jnp.maximum(old, positive), old)
        joined[0:1, lanes] = top
        joined[1:2, lanes] = stats[1:2, lanes] * jnp.exp(old - top) + jnp.where(
            has > 0, jnp.exp(positive - top), 0.0
        )
        own[0:1, lanes] = positive
        own[1:2, lanes] = has


def pulled_kernel(members, groups, slots, blocks, info, got, *refs):
    negs, refs = refs[:groups], refs[groups:]
    rows, refs = refs[:groups], refs[groups:]
    prob_hi, prob_lo, pulled, row_t, place_rows, column = refs
    place_rows[...] = own_places(members, info, got)
    neg = jnp.concatenate([row[...] for row in negs], axis=0)
    neg_t = split(jnp.transpose(neg))
    tokens = pulled.shape[2]
    for i, e in enumerate(blocks):
        mr = info[1] ^ e
        pulled[i] = dot3(neg_t, (prob_hi[i], prob_lo[i]), NN)
        at = pl.ds(pl.multiple_of(mr * slots, slots), slots)
        hot = slot_hot(members, groups, slots, info, place_rows, column, mr, tokens)
        high, low = split(jnp.concatenate([r[at, :] for r in rows], axis=0))
        row_t[i] = dot1(high, as_bf16(hot), TN) + dot1(low, as_bf16(hot), TN)


def join(first, second):
    top = jnp.maximum(first[0:1], second[0:1])
    total = first[1:2] * jnp.exp(first[0:1] - top) + second[1:2] * jnp.exp(second[0:1] - top)
    return top, total


def join_kernel(first, second, *refs):
    out = refs[-1]
    top, total = join(first[...], second[...])
    out[0:1, :] = top
    out[1:2, :] = total


def shares(info, e, tokens, final, stats, own):
    lanes = pl.ds(pl.multiple_of((info[1] ^ e) * tokens, LANES), tokens)
    top, total = final[0:1, lanes], final[1:2, lanes]
    scale = jnp.exp(stats[0:1, lanes] - top) / total
    extra = jnp.where(
        own[1:2, lanes] > 0, jnp.exp(own[0:1, lanes] - top) / total - 1.0, 0.0
    )
    return scale, extra


def pull_kernel(halves, blocks, tokens, info, final, stats, own, *refs):
    for e, out in zip(blocks, refs[-len(blocks) :]):
        h = 0 if e in halves[0] else 1
        pulled, row_t = (ref[halves[h].index(e)] for ref in refs[2 * h : 2 * h + 2])
        scale, extra = shares(info, e, tokens, final, stats, own)
        out[...] = pulled * scale + row_t * extra


def flat(table, lane, slots):
    return jnp.concatenate(
        [table[m : m + 1, lane : lane + slots] for m in range(table.shape[0])], axis=1
    )


def grad_kernel(members, groups, slots, halves, info, got, final, stats, own, *refs):
    probs, refs = refs[: 2 * len(halves)], refs[2 * len(halves) :]
    encs = refs[:members]
    *outs, total, coef, place_rows = refs[-groups - 3 :]
    place_rows[...] = own_places(members, info, got)
    tokens, width = encs[0].shape
    for h, i, e in [(h, i, e) for h, blocks in enumerate(halves) for i, e in enumerate(blocks)]:
        mr = info[1] ^ e
        scale, extra = shares(info, e, tokens, final, stats, own)
        enc = split(encs[e][...] * row_to_col(scale))
        part = dot3((probs[2 * h][i], probs[2 * h + 1][i]), enc, NN)
        if h == 0 and i == 0:
            total[...] = part
        else:
            total[...] += part
        hot = place_rows[pl.ds(mr, 1), :] == iota((tokens, LANES), 0) + 1
        coef[pl.ds(mr, 1), :] = jnp.sum(
            jnp.where(hot, row_to_col(extra), 0.0), axis=0, keepdims=True
        )
    count = total.shape[0] // groups
    lines = [flat(coef[...], g * slots, slots) for g in range(groups)]
    for d, out in enumerate(outs):
        out[0:count, :] = total[d * count : (d + 1) * count, :]
        line = lines[0]
        for g in range(1, groups):
            line = jnp.where((info[0] ^ d) == g, lines[g], line)
        out[count:, 0 : line.shape[1]] = jnp.broadcast_to(line, (8, line.shape[1]))


def equal_in_batch(ids):
    size = ids.shape[1]
    across = jnp.broadcast_to(ids.astype(F32), (size, size))
    same = (jnp.transpose(across) == across) & (
        (iota((size, size), 0) // BATCH) == (iota((size, size), 1) // BATCH)
    )
    return same.astype(F32)


def scatter_kernel(members, groups, own, slots, count, info, got_v, got, *refs):
    size = len(own)
    grads, picked = refs[:size], refs[size : 2 * size]
    out, negs, tgts = refs[-3:]
    out[...] = refs[2 * size][...] if own[0] else jnp.zeros_like(out)

    def add_rows(asked, first, source, base, number):
        for b in range(0, number, BATCH):
            rows = [asked[first + b + k] for k in range(BATCH)]
            new = [
                out[pl.ds(rows[k], 1), :] + source[pl.ds(base + b + k, 1), :]
                for k in range(BATCH)
            ]
            for k in range(BATCH):
                out[pl.ds(rows[k], 1), :] = new[k]

    for i, d in enumerate(own):
        g = info[0] ^ d
        asked = got_v[pl.ds(g * members, members), 0, 0:LANES]
        number = members * count
        same = as_bf16(equal_in_batch(flat(asked, slots, count)) > 0)
        high, low = split(grads[i][0:number, :])
        negs[...] = dot1(same, high, NN) + dot1(same, low, NN)
        weight = equal_in_batch(flat(asked, 0, slots))
        weight = weight * grads[i][number : number + 1, 0 : members * slots]
        tgts[...] = dot3(split(weight), split(picked[i][...]), NN)
        merged = BATCH // count if count < BATCH else 1

        def member(step, carry, g=g, merged=merged):
            if merged == 1:
                add_rows(got.at[g * members + step, 0], slots, negs, step * count, count)
                add_rows(got.at[g * members + step, 0], 0, tgts, step * slots, slots)
                return carry
            first = g * members + step * merged
            rows = [
                got[first + k // count, 0, slots + k % count] for k in range(BATCH)
            ]
            new = [
                out[pl.ds(rows[k], 1), :] + negs[pl.ds(step * BATCH + k, 1), :]
                for k in range(BATCH)
            ]
            for k in range(BATCH):
                out[pl.ds(rows[k], 1), :] = new[k]
            for m in range(merged):
                add_rows(got.at[first + m, 0], 0, tgts, (step * merged + m) * slots, slots)
            return carry

        lax.fori_loop(0, members // merged, member, 0)


def add_kernel(terms, *refs):
    total = refs[0][...]
    for ref in refs[1:terms]:
        total = total + ref[...]
    refs[-1][...] = total


def finish_kernel(valid, *refs):
    total = refs[0][...]
    for ref in refs[1:-1]:
        total = total + ref[...]
    refs[-1][...] = jnp.transpose(total) * row_to_col(valid[...].astype(F32))


def swap(value, axis, d):
    return lax.ppermute(value, axis, [(i, i ^ d) for i in range(lax.axis_size(axis))])


def shards(encoded, item_table, target_owner, target_local, negative_ids, valid):
    groups, members = lax.axis_size("group"), lax.axis_size("member")
    devices = groups * members
    tokens, width = encoded.shape
    rows_dev = item_table.shape[0]
    negatives = negative_ids.shape[0]
    slots = max(2, 4 * tokens // devices)
    count = negatives // devices
    near = max(1, members // 4)
    everyone = members * tokens
    shape = jax.ShapeDtypeStruct
    sds = lambda *s: shape(s, F32)

    info = jnp.stack([lax.axis_index("group"), lax.axis_index("member")]).astype(I32)
    ints = jnp.concatenate([target_owner.reshape(-1), target_local, valid, negative_ids])
    request, masked = call(
        functools.partial(front_kernel, members, rows_dev, slots, tokens, negatives),
        [shape((devices, 1, 2 * LANES), I32), sds(tokens, width)],
        [SMEM] + [VMEM] * 2,
        [VMEM] * 2,
        (info, ints.reshape(1, -1), encoded),
        name="front",
    )
    got = lax.all_to_all(
        request, ("group", "member"), split_axis=0, concat_axis=0, tiled=True
    )

    encs = [masked] + [None] * (members - 1)
    for z in (near, 2 * near):
        encs[z] = swap(masked, "member", z)
    onward, got = lax.optimization_barrier((encs[2 * near], got))
    encs[3 * near] = swap(onward, "member", near)
    for z in (0, 2 * near, 3 * near):
        for x in range(1, near):
            encs[z ^ x] = swap(onward if z == 2 * near else encs[z], "member", x)
    halves = [[d for d in range(members) if (d < near) or d in (near, 2 * near)], []]
    halves[1] = [d for d in range(members) if d not in halves[0]]

    early = [encs[d] for d in halves[0] if d and d != near]
    gather = lambda part, many, deps, name: call(
        functools.partial(gather_kernel, members, groups, part, many),
        [sds(members * many, width)] * groups,
        [SMEM, SMEM, VMEM] + [ANY] * len(deps),
        [VMEM] * groups,
        (info, got, item_table, *deps),
        name=name,
    )
    negs = gather(slots, count, early, "gather_negatives")
    for x in range(1, near):
        encs[near + x] = swap(lax.optimization_barrier((encs[x], negs[0]))[0], "member", near)
    negs = [negs[0]] + [swap(negs[d], "group", d) for d in range(1, groups)]
    rows = gather(0, slots, [encs[near], *encs[2 * near + 1 : 3 * near]], "gather_targets")
    rows = [rows[0]] + [swap(rows[d], "group", d) for d in range(1, groups)]

    stats, probs = [], []
    for blocks in halves:
        many = len(blocks)
        *stats, hi, lo = call(
            functools.partial(score_kernel, blocks, groups),
            [sds(2, everyone)] + [shape((many, negatives, tokens), BF16)] * 2,
            [SMEM] + [VMEM] * (groups + many + len(stats)),
            [VMEM] * 3,
            (info, *negs, *[encs[e] for e in blocks], *stats),
            flops=12 * many * tokens * negatives * width,
            moved=MIB,
            name="score",
        )
        probs += [hi, lo]
    stats = stats[0]
    picked = call(
        functools.partial(pick_kernel, members, groups, slots),
        [sds(members * slots, width)] * groups,
        [SMEM] + [VMEM] * (1 + members),
        [VMEM] * groups,
        (info, got, *encs),
        scratch=[pltpu.VMEM((members, LANES), I32), pltpu.VMEM((LANES, 1), I32)],
        name="pick",
    )
    sent = [picked[0]] + [swap(picked[d], "group", d) for d in range(1, groups)]
    joined, own = call(
        functools.partial(positive_kernel, members, groups, slots, tokens),
        [sds(2, everyone)] * 2,
        [SMEM] + [VMEM] * (2 + 2 * groups),
        [VMEM] * 2,
        (info, got, stats, *rows, *picked),
        scratch=[pltpu.VMEM((members, LANES), I32), pltpu.VMEM((LANES, 1), I32)],
        name="positive",
    )
    pulled = []
    for h, blocks in enumerate(halves):
        pulled += call(
            functools.partial(pulled_kernel, members, groups, slots, blocks),
            [sds(len(blocks), width, tokens)] * 2,
            [SMEM] + [VMEM] * (3 + 2 * groups),
            [VMEM] * 2,
            (info, got, *negs, *rows, *probs[2 * h : 2 * h + 2]),
            scratch=[pltpu.VMEM((members, LANES), I32), pltpu.VMEM((LANES, 1), I32)],
            flops=6 * len(blocks) * tokens * negatives * width,
            moved=MIB,
            name="pulled",
        )

    final = joined
    d, hops = 1, 0
    while d < members:
        late = pulled[2 * hops : 2 * hops + 2]
        hops += 1
        final = call(
            join_kernel,
            sds(2, everyone),
            [VMEM] * 2 + [ANY] * len(late),
            VMEM,
            (final, swap(final, "member", d), *late),
            name="join",
        )
        d *= 2

    grads = call(
        functools.partial(grad_kernel, members, groups, slots, halves),
        [sds(members * count + 8, width)] * groups,
        [SMEM] + [VMEM] * (4 + len(probs) + members) + [ANY] * (groups - 1),
        [VMEM] * groups,
        (info, got, final, stats, own, *probs, *encs, *sent[1:]),
        scratch=[
            pltpu.VMEM((negatives, width), F32),
            pltpu.VMEM((members, LANES), F32),
            pltpu.VMEM((members, LANES), I32),
        ],
        flops=6 * everyone * negatives * width,
        moved=8 * MIB,
        name="grad",
    )
    def added(terms, deps, flops=0):
        return call(
            functools.partial(add_kernel, len(terms)),
            sds(width, tokens),
            [VMEM] * len(terms) + [ANY] * len(deps),
            VMEM,
            (*terms, *deps),
            flops=flops,
            name="add",
        )

    graded = [grads[0]]
    grads = graded + [swap(grads[d], "group", d) for d in range(1, groups)]
    def scaled(blocks, deps):
        return call(
            functools.partial(pull_kernel, halves, blocks, tokens),
            [sds(width, tokens)] * len(blocks),
            [SMEM] + [VMEM] * 7 + [ANY] * len(deps),
            [VMEM] * len(blocks),
            (info, final, stats, own, *pulled, *deps),
            name="pull",
        )

    def beside(blocks):
        return [swap(block, "member", x) for x, block in enumerate(blocks, 1)]

    along = list(range(near))
    def scatter(own, base, deps, flops):
        return call(
            functools.partial(scatter_kernel, members, groups, own, slots, count),
            sds(rows_dev, width),
            [SMEM, VMEM, SMEM] + [VMEM] * (2 * len(own) + len(base)) + [ANY] * len(deps),
            VMEM,
            (info, got, got, *[grads[d] for d in own], *[sent[d] for d in own], *base, *deps),
            scratch=[
                pltpu.VMEM((members * count, width), F32),
                pltpu.VMEM((members * slots, width), F32),
            ],
            flops=flops,
            name="scatter",
        )

    def after(blocks, done):
        return [lax.optimization_barrier((block, done))[0] for block in blocks]

    close = [*along[1:], *[near + x for x in along[1:]]]
    farthest, *rest, nearest = scaled([3 * near + x for x in along] + [near], [])
    arrived = beside(rest)
    nearest = swap(nearest, "member", near)
    kept, far, *others = scaled([0, *[2 * near + x for x in along], *close], graded)
    others, sends = others[: near - 1], others[near - 1 :]
    total = added([farthest, *arrived], [*graded, nearest])
    others = after(others, total)
    early_groups = list(range(2))
    table_own = scatter(early_groups, [], [total], 1 << 33)
    far = added([far], [table_own, *grads[2:]])
    half = added([far, swap(total, "member", near), *beside(others)], [])
    parts = [swap(b, "member", d) for d, b in zip(close, after(sends, half))]
    parts.append(added([nearest, kept, swap(half, "member", 2 * near)], []))

    table_grad = scatter(list(range(2, groups)), [table_own], [], 0)
    encoded_grad = call(
        finish_kernel,
        sds(tokens, width),
        [VMEM] * (1 + len(parts)),
        VMEM,
        (valid.reshape(1, -1), *parts),
        name="finish",
    )
    return (encoded_grad, table_grad)


def solution(mesh):
    placed = (
        P(("group", "member"), None),
        P(("group", "member"), None),
        P(("group", "member"), None),
        P(("group", "member")),
        P(("group", "member")),
        P(("group", "member")),
    )
    return jax.shard_map(
        shards,
        mesh=mesh,
        in_specs=placed,
        out_specs=(P(("group", "member"), None), P(("group", "member"), None)),
        check_vma=False,
    )
```

```python
import functools

import jax
import jax.numpy as jnp
from jax import lax
from jax.experimental import pallas as pl
from jax.experimental.pallas import tpu as pltpu
from jax.sharding import PartitionSpec as P

F32 = jnp.float32
BF16 = jnp.bfloat16
I32 = jnp.int32
LANES = 128
VMEM = pl.BlockSpec(memory_space=pltpu.VMEM)
ANY = pl.BlockSpec(memory_space=pl.ANY)
SMEM = pl.BlockSpec(memory_space=pltpu.SMEM)
MIB = 1 << 20
BATCH = 8

NN = (((1,), (0,)), ((), ()))
NT = (((1,), (1,)), ((), ()))
TN = (((0,), (0,)), ((), ()))


def call(kernel, out_shape, ins, outs, args, scratch=(), limit=10, flops=0, moved=0, name=None):
    return pl.pallas_call(
        kernel,
        out_shape=out_shape,
        in_specs=ins,
        out_specs=outs,
        scratch_shapes=list(scratch),
        compiler_params=pltpu.CompilerParams(vmem_limit_bytes=limit * MIB),
        cost_estimate=pl.CostEstimate(flops=flops, bytes_accessed=moved, transcendentals=0),
        name=name,
    )(*args)


def iota(shape, dim):
    return lax.broadcasted_iota(I32, shape, dim)


def as_bf16(flag):
    return flag.astype(F32).astype(BF16)


def dot1(a, b, dims):
    return lax.dot_general(a, b, dims, preferred_element_type=F32)


def split(x):
    hi = x.astype(BF16)
    return hi, (x - hi.astype(F32)).astype(BF16)


def dot3(a, b, dims):
    return dot1(a[0], b[0], dims) + (dot1(a[0], b[1], dims) + dot1(a[1], b[0], dims))


def row_to_col(row):
    return jnp.transpose(jnp.broadcast_to(row, (LANES, row.shape[1])))[:, 0:1]


def split3(x):
    hi = x.astype(BF16)
    rest = x - hi.astype(F32)
    mid = rest.astype(BF16)
    return hi, mid, (rest - mid.astype(F32)).astype(BF16)


def dot6(a, b, dims):
    small = dot1(a[2], b[0], dims) + dot1(a[1], b[1], dims) + dot1(a[0], b[2], dims)
    return (small + (dot1(a[1], b[0], dims) + dot1(a[0], b[1], dims))) + dot1(a[0], b[0], dims)


def copy_rows(source, row_of, target, base, count):
    for b in range(0, count, BATCH):
        rows = [source[pl.ds(row_of(b + k), 1), :] for k in range(BATCH)] if count % BATCH == 0 else None
        if rows is None:
            for k in range(count):
                target[pl.ds(base + k, 1), :] = source[pl.ds(row_of(k), 1), :]
            return
        target[pl.ds(pl.multiple_of(base + b, BATCH), BATCH), :] = jnp.concatenate(rows, axis=0)


def front_kernel(members, rows_dev, slots, tokens, negatives, info, ints, enc_ref, out_ref, masked_ref):
    devices = out_ref.shape[0]
    shift = rows_dev.bit_length() - 1
    owner = ints[:, 0:tokens]
    local = ints[:, tokens : 2 * tokens]
    valid = ints[:, 2 * tokens : 3 * tokens]
    ids = ints[:, 3 * tokens :]
    masked_ref[...] = enc_ref[...] * row_to_col(valid.astype(F32))

    def ranks(owner_row, count):
        hot = iota((devices, count), 0) == owner_row
        before = as_bf16(iota((count, count), 0) < iota((count, count), 1))
        seen = dot1(as_bf16(hot), before, NN)
        return hot, jnp.sum(jnp.where(hot, seen, 0.0), axis=0, keepdims=True).astype(I32)

    def table(hot, value, place):
        return dot1(jnp.where(hot, value, 0.0).astype(BF16), place, NT)

    def placed(lane_row, count):
        return as_bf16(iota((LANES, count), 0) == lane_row)

    hot, rank = ranks(owner, tokens)
    place = placed(rank, tokens)
    high = table(hot, (local >> 6).astype(F32), place)
    low = table(hot, (local & 63).astype(F32), place)
    group = owner >> (members.bit_length() - 1)
    hot_member = (iota((devices, tokens), 0) & (members - 1)) == (owner & (members - 1))
    position = table(
        hot_member, (iota((1, tokens), 1) + 1).astype(F32), placed(group * slots + rank, tokens)
    )

    hot, rank = ranks(ids >> shift, negatives)
    place = placed(rank + slots, negatives)
    local = ids & (rows_dev - 1)
    high = high + table(hot, (local >> 6).astype(F32), place)
    low = low + table(hot, (local & 63).astype(F32), place)
    out_ref[:, 0, 0:LANES] = high.astype(I32) * 64 + low.astype(I32)
    out_ref[:, 0, LANES : 2 * LANES] = position.astype(I32)


def gather_kernel(members, chosen, part, count, info, got, table, *refs):
    for d, out in zip(chosen, refs[-len(chosen) :]):
        first = (info[0] ^ d) * members

        def member(mr, carry, out=out, first=first):
            asked = got.at[first + mr, 0]
            copy_rows(table, lambda k: asked[part + k], out, mr * count, count)
            return carry

        lax.fori_loop(0, members, member, 0)


def score_kernel(blocks, groups, follows, info, *refs):
    rows, refs = refs[:groups], refs[groups:]
    encs, refs = refs[: len(blocks)], refs[len(blocks) :]
    stats, prob_hi, prob_lo = refs[-3:]
    if follows:
        stats[...] = refs[0][...]
    tokens = encs[0].shape[0]
    neg = split3(jnp.concatenate([row[...] for row in rows], axis=0))
    for i, e in enumerate(blocks):
        lanes = pl.ds(pl.multiple_of((info[1] ^ e) * tokens, LANES), tokens)
        score = dot6(neg, split3(encs[i][...]), NT)
        top = jnp.max(score, axis=0, keepdims=True)
        prob = jnp.exp(score - top)
        stats[0:1, lanes] = top
        stats[1:2, lanes] = jnp.sum(prob, axis=0, keepdims=True)
        parts = split(prob)
        prob_hi[i] = parts[0]
        prob_lo[i] = parts[1]


def own_places(members, info, got):
    return got[pl.ds(info[0] * members, members), 0, LANES : 2 * LANES]


def slot_hot(members, groups, slots, info, place_rows, column, mr, tokens):
    column[...] = row_to_col(place_rows[pl.ds(mr, 1), :])
    place = [
        column[pl.ds(pl.multiple_of((info[0] ^ d) * slots, slots), slots), :]
        for d in range(groups)
    ]
    return jnp.concatenate(place, axis=0) == iota((groups * slots, tokens), 1) + 1


def pick_kernel(members, groups, slots, info, got, *refs):
    encs = refs[:members]
    outs = refs[members : members + groups]
    place_rows, column = refs[members + groups :]
    place_rows[...] = own_places(members, info, got)
    for e in range(members):
        mr = info[1] ^ e
        tokens = encs[e].shape[0]
        hot = as_bf16(slot_hot(members, groups, slots, info, place_rows, column, mr, tokens))
        hi, mid, low = split3(encs[e][...])
        found = (dot1(hot, hi, NN) + dot1(hot, mid, NN)) + dot1(hot, low, NN)
        at = pl.ds(pl.multiple_of(mr * slots, slots), slots)
        for d in range(groups):
            outs[d][at, :] = found[d * slots : (d + 1) * slots]


def positive_kernel(members, groups, slots, tokens, info, got, stats, *refs):
    rows, picked = refs[:groups], refs[groups : 2 * groups]
    joined, own, place_rows, column = refs[2 * groups :]
    place_rows[...] = own_places(members, info, got)
    for e in range(members):
        mr = info[1] ^ e
        lanes = pl.ds(pl.multiple_of(mr * tokens, LANES), tokens)
        at = pl.ds(pl.multiple_of(mr * slots, slots), slots)
        hot = slot_hot(members, groups, slots, info, place_rows, column, mr, tokens)
        row = jnp.concatenate([r[at, :] for r in rows], axis=0)
        enc = jnp.concatenate([p[at, :] for p in picked], axis=0)
        value = jnp.sum(row * enc, axis=1, keepdims=True)
        positive = jnp.sum(jnp.where(hot, value, 0.0), axis=0, keepdims=True)
        has = jnp.sum(hot.astype(F32), axis=0, keepdims=True)
        old = stats[0:1, lanes]
        top = jnp.where(has > 0, jnp.maximum(old, positive), old)
        joined[0:1, lanes] = top
        joined[1:2, lanes] = stats[1:2, lanes] * jnp.exp(old - top) + jnp.where(
            has > 0, jnp.exp(positive - top), 0.0
        )
        own[0:1, lanes] = positive
        own[1:2, lanes] = has


def pulled_kernel(members, groups, slots, blocks, info, got, *refs):
    negs, refs = refs[:groups], refs[groups:]
    rows, refs = refs[:groups], refs[groups:]
    prob_hi, prob_lo, pulled, row_t, place_rows, column = refs
    place_rows[...] = own_places(members, info, got)
    neg = jnp.concatenate([row[...] for row in negs], axis=0)
    neg_t = split(jnp.transpose(neg))
    tokens = pulled.shape[2]
    for i, e in enumerate(blocks):
        mr = info[1] ^ e
        pulled[i] = dot3(neg_t, (prob_hi[i], prob_lo[i]), NN)
        at = pl.ds(pl.multiple_of(mr * slots, slots), slots)
        hot = slot_hot(members, groups, slots, info, place_rows, column, mr, tokens)
        high, low = split(jnp.concatenate([r[at, :] for r in rows], axis=0))
        row_t[i] = dot1(high, as_bf16(hot), TN) + dot1(low, as_bf16(hot), TN)


def join(first, second):
    top = jnp.maximum(first[0:1], second[0:1])
    total = first[1:2] * jnp.exp(first[0:1] - top) + second[1:2] * jnp.exp(second[0:1] - top)
    return top, total


def join_kernel(first, second, *refs):
    out = refs[-1]
    top, total = join(first[...], second[...])
    out[0:1, :] = top
    out[1:2, :] = total


def shares(info, e, tokens, final, stats, own):
    lanes = pl.ds(pl.multiple_of((info[1] ^ e) * tokens, LANES), tokens)
    top, total = final[0:1, lanes], final[1:2, lanes]
    scale = jnp.exp(stats[0:1, lanes] - top) / total
    extra = jnp.where(
        own[1:2, lanes] > 0, jnp.exp(own[0:1, lanes] - top) / total - 1.0, 0.0
    )
    return scale, extra


def pull_kernel(halves, blocks, tokens, info, final, stats, own, *refs):
    for e, out in zip(blocks, refs[-len(blocks) :]):
        h = 0 if e in halves[0] else 1
        pulled, row_t = (ref[halves[h].index(e)] for ref in refs[2 * h : 2 * h + 2])
        scale, extra = shares(info, e, tokens, final, stats, own)
        out[...] = pulled * scale + row_t * extra


def flat(table, lane, slots):
    return jnp.concatenate(
        [table[m : m + 1, lane : lane + slots] for m in range(table.shape[0])], axis=1
    )


def grad_kernel(members, groups, slots, halves, info, got, final, stats, own, *refs):
    probs, refs = refs[: 2 * len(halves)], refs[2 * len(halves) :]
    encs = refs[:members]
    *outs, total, coef, place_rows = refs[-groups - 3 :]
    place_rows[...] = own_places(members, info, got)
    tokens, width = encs[0].shape
    for h, i, e in [(h, i, e) for h, blocks in enumerate(halves) for i, e in enumerate(blocks)]:
        mr = info[1] ^ e
        scale, extra = shares(info, e, tokens, final, stats, own)
        enc = split(encs[e][...] * row_to_col(scale))
        part = dot3((probs[2 * h][i], probs[2 * h + 1][i]), enc, NN)
        if h == 0 and i == 0:
            total[...] = part
        else:
            total[...] += part
        hot = place_rows[pl.ds(mr, 1), :] == iota((tokens, LANES), 0) + 1
        coef[pl.ds(mr, 1), :] = jnp.sum(
            jnp.where(hot, row_to_col(extra), 0.0), axis=0, keepdims=True
        )
    count = total.shape[0] // groups
    lines = [flat(coef[...], g * slots, slots) for g in range(groups)]
    for d, out in enumerate(outs):
        out[0:count, :] = total[d * count : (d + 1) * count, :]
        line = lines[0]
        for g in range(1, groups):
            line = jnp.where((info[0] ^ d) == g, lines[g], line)
        out[count:, 0 : line.shape[1]] = jnp.broadcast_to(line, (8, line.shape[1]))


def equal_in_batch(ids):
    size = ids.shape[1]
    across = jnp.broadcast_to(ids.astype(F32), (size, size))
    same = (jnp.transpose(across) == across) & (
        (iota((size, size), 0) // BATCH) == (iota((size, size), 1) // BATCH)
    )
    return same.astype(F32)


def scatter_kernel(members, groups, own, slots, count, info, got_v, got, *refs):
    size = len(own)
    grads, picked = refs[:size], refs[size : 2 * size]
    out, negs, tgts = refs[-3:]
    out[...] = refs[2 * size][...] if own[0] else jnp.zeros_like(out)

    def add_rows(asked, first, source, base, number):
        for b in range(0, number, BATCH):
            rows = [asked[first + b + k] for k in range(BATCH)]
            new = [
                out[pl.ds(rows[k], 1), :] + source[pl.ds(base + b + k, 1), :]
                for k in range(BATCH)
            ]
            for k in range(BATCH):
                out[pl.ds(rows[k], 1), :] = new[k]

    for i, d in enumerate(own):
        g = info[0] ^ d
        asked = got_v[pl.ds(g * members, members), 0, 0:LANES]
        number = members * count
        same = as_bf16(equal_in_batch(flat(asked, slots, count)) > 0)
        high, low = split(grads[i][0:number, :])
        negs[...] = dot1(same, high, NN) + dot1(same, low, NN)
        weight = equal_in_batch(flat(asked, 0, slots))
        weight = weight * grads[i][number : number + 1, 0 : members * slots]
        tgts[...] = dot3(split(weight), split(picked[i][...]), NN)
        merged = BATCH // count if count < BATCH else 1

        def member(step, carry, g=g, merged=merged):
            if merged == 1:
                add_rows(got.at[g * members + step, 0], slots, negs, step * count, count)
                add_rows(got.at[g * members + step, 0], 0, tgts, step * slots, slots)
                return carry
            first = g * members + step * merged
            rows = [
                got[first + k // count, 0, slots + k % count] for k in range(BATCH)
            ]
            new = [
                out[pl.ds(rows[k], 1), :] + negs[pl.ds(step * BATCH + k, 1), :]
                for k in range(BATCH)
            ]
            for k in range(BATCH):
                out[pl.ds(rows[k], 1), :] = new[k]
            for m in range(merged):
                add_rows(got.at[first + m, 0], 0, tgts, (step * merged + m) * slots, slots)
            return carry

        lax.fori_loop(0, members // merged, member, 0)


def add_kernel(terms, *refs):
    total = refs[0][...]
    for ref in refs[1:terms]:
        total = total + ref[...]
    refs[-1][...] = total


def finish_kernel(valid, *refs):
    total = refs[0][...]
    for ref in refs[1:-1]:
        total = total + ref[...]
    refs[-1][...] = jnp.transpose(total) * row_to_col(valid[...].astype(F32))


def swap(value, axis, d):
    return lax.ppermute(value, axis, [(i, i ^ d) for i in range(lax.axis_size(axis))])


def shards(encoded, item_table, target_owner, target_local, negative_ids, valid):
    groups, members = lax.axis_size("group"), lax.axis_size("member")
    devices = groups * members
    tokens, width = encoded.shape
    rows_dev = item_table.shape[0]
    negatives = negative_ids.shape[0]
    slots = max(2, 4 * tokens // devices)
    count = negatives // devices
    near = max(1, members // 4)
    everyone = members * tokens
    shape = jax.ShapeDtypeStruct
    sds = lambda *s: shape(s, F32)

    info = jnp.stack([lax.axis_index("group"), lax.axis_index("member")]).astype(I32)
    ints = jnp.concatenate([target_owner.reshape(-1), target_local, valid, negative_ids])
    request, masked = call(
        functools.partial(front_kernel, members, rows_dev, slots, tokens, negatives),
        [shape((devices, 1, 2 * LANES), I32), sds(tokens, width)],
        [SMEM] + [VMEM] * 2,
        [VMEM] * 2,
        (info, ints.reshape(1, -1), encoded),
        name="front",
    )
    got = lax.all_to_all(
        request, ("group", "member"), split_axis=0, concat_axis=0, tiled=True
    )

    encs = [masked] + [None] * (members - 1)
    for z in (near, 2 * near):
        encs[z] = swap(masked, "member", z)
    onward, got = lax.optimization_barrier((encs[2 * near], got))
    encs[3 * near] = swap(onward, "member", near)
    for z in (0, 2 * near, 3 * near):
        for x in range(1, near):
            encs[z ^ x] = swap(onward if z == 2 * near else encs[z], "member", x)
    halves = [[d for d in range(members) if (d < near) or d in (near, 2 * near)], []]
    halves[1] = [d for d in range(members) if d not in halves[0]]

    early = [encs[d] for d in halves[0] if d and d != near]

    def after(blocks, done):
        return [lax.optimization_barrier((block, done))[0] for block in blocks]

    def gather(chosen, part, many, deps, name):
        return call(
            functools.partial(gather_kernel, members, chosen, part, many),
            [sds(members * many, width)] * len(chosen),
            [SMEM, SMEM, VMEM] + [ANY] * len(deps),
            [VMEM] * len(chosen),
            (info, got, item_table, *deps),
            name=name,
        )

    negs = gather(range(groups), slots, count, early, "gather_negatives")
    for x in range(1, near):
        encs[near + x] = swap(lax.optimization_barrier((encs[x], negs[0]))[0], "member", near)
    negs = [negs[0]] + [swap(negs[d], "group", d) for d in range(1, groups)]
    waited = [encs[near], *encs[2 * near + 1 : 3 * near]]
    rows = gather(range(2, groups), 0, slots, waited, "gather_far_targets")
    gathered = rows
    rows = [swap(row, "group", d) for d, row in enumerate(rows, 2)]

    stats, probs = [], []
    for blocks in halves:
        many = len(blocks)
        *stats, hi, lo = call(
            functools.partial(score_kernel, blocks, groups, bool(stats)),
            [sds(2, everyone)] + [shape((many, negatives, tokens), BF16)] * 2,
            [SMEM] + [VMEM] * (groups + many + len(stats)) + [ANY] * len(gathered),
            [VMEM] * 3,
            (info, *negs, *[encs[e] for e in blocks], *stats, *gathered),
            flops=12 * many * tokens * negatives * width,
            moved=MIB,
            name="score",
        )
        probs += [hi, lo]
        if gathered:
            gathered = []
            kept, row = gather(range(2), 0, slots, stats, "gather_targets")
            rows = [kept, swap(row, "group", 1), *rows]
    stats = stats[0]
    picked = call(
        functools.partial(pick_kernel, members, groups, slots),
        [sds(members * slots, width)] * groups,
        [SMEM] + [VMEM] * (1 + members),
        [VMEM] * groups,
        (info, got, *encs),
        scratch=[pltpu.VMEM((members, LANES), I32), pltpu.VMEM((LANES, 1), I32)],
        name="pick",
    )
    sent = list(picked[:1]) + [
        swap(b, "group", d) for d, b in enumerate(after(picked[1:], stats), 1)
    ]
    joined, own = call(
        functools.partial(positive_kernel, members, groups, slots, tokens),
        [sds(2, everyone)] * 2,
        [SMEM] + [VMEM] * (2 + 2 * groups),
        [VMEM] * 2,
        (info, got, stats, *rows, *picked),
        scratch=[pltpu.VMEM((members, LANES), I32), pltpu.VMEM((LANES, 1), I32)],
        name="positive",
    )
    pulled = []
    for h, blocks in enumerate(halves):
        pulled += call(
            functools.partial(pulled_kernel, members, groups, slots, blocks),
            [sds(len(blocks), width, tokens)] * 2,
            [SMEM] + [VMEM] * (3 + 2 * groups),
            [VMEM] * 2,
            (info, got, *negs, *rows, *probs[2 * h : 2 * h + 2]),
            scratch=[pltpu.VMEM((members, LANES), I32), pltpu.VMEM((LANES, 1), I32)],
            flops=6 * len(blocks) * tokens * negatives * width,
            moved=MIB,
            name="pulled",
        )

    final = joined
    d, hops = 1, 0
    while d < members:
        late = pulled[2 * hops : 2 * hops + 2]
        hops += 1
        final = call(
            join_kernel,
            sds(2, everyone),
            [VMEM] * 2 + [ANY] * len(late),
            VMEM,
            (final, swap(final, "member", d), *late),
            name="join",
        )
        d *= 2

    grads = call(
        functools.partial(grad_kernel, members, groups, slots, halves),
        [sds(members * count + 8, width)] * groups,
        [SMEM] + [VMEM] * (4 + len(probs) + members) + [ANY] * (groups - 1),
        [VMEM] * groups,
        (info, got, final, stats, own, *probs, *encs, *sent[1:]),
        scratch=[
            pltpu.VMEM((negatives, width), F32),
            pltpu.VMEM((members, LANES), F32),
            pltpu.VMEM((members, LANES), I32),
        ],
        flops=6 * everyone * negatives * width,
        moved=8 * MIB,
        name="grad",
    )
    def added(terms, deps, flops=0):
        return call(
            functools.partial(add_kernel, len(terms)),
            sds(width, tokens),
            [VMEM] * len(terms) + [ANY] * len(deps),
            VMEM,
            (*terms, *deps),
            flops=flops,
            name="add",
        )

    graded = [grads[0]]
    grads = graded + [swap(grads[d], "group", d) for d in range(1, groups)]
    def scaled(blocks, deps):
        return call(
            functools.partial(pull_kernel, halves, blocks, tokens),
            [sds(width, tokens)] * len(blocks),
            [SMEM] + [VMEM] * 7 + [ANY] * len(deps),
            [VMEM] * len(blocks),
            (info, final, stats, own, *pulled, *deps),
            name="pull",
        )

    def beside(blocks):
        return [swap(block, "member", x) for x, block in enumerate(blocks, 1)]

    along = list(range(near))
    def scatter(own, base, deps, flops):
        return call(
            functools.partial(scatter_kernel, members, groups, own, slots, count),
            sds(rows_dev, width),
            [SMEM, VMEM, SMEM] + [VMEM] * (2 * len(own) + len(base)) + [ANY] * len(deps),
            VMEM,
            (info, got, got, *[grads[d] for d in own], *[sent[d] for d in own], *base, *deps),
            scratch=[
                pltpu.VMEM((members * count, width), F32),
                pltpu.VMEM((members * slots, width), F32),
            ],
            flops=flops,
            name="scatter",
        )

    close = [*along[1:], *[near + x for x in along[1:]]]
    farthest, *rest, nearest = scaled([3 * near + x for x in along] + [near], [])
    arrived = beside(rest)
    nearest = swap(nearest, "member", near)
    kept, far, *others = scaled([0, *[2 * near + x for x in along], *close], graded)
    others, sends = others[: near - 1], others[near - 1 :]
    total = added([farthest, *arrived], [*graded, nearest])
    others = after(others, total)
    early_groups = list(range(2))
    table_own = scatter(early_groups, [], [total], 1 << 33)
    far = added([far], [table_own, *grads[2:]])
    others = beside(others)
    half = added([far, swap(total, "member", near), *others], [])
    held = after(sends[: near - 1], half) + after(sends[near - 1 :], others[0])
    parts = [swap(b, "member", d) for d, b in zip(close, held)]
    parts.append(added([nearest, kept, swap(half, "member", 2 * near)], []))

    table_grad = scatter(list(range(2, groups)), [table_own], [], 0)
    encoded_grad = call(
        finish_kernel,
        sds(tokens, width),
        [VMEM] * (1 + len(parts)),
        VMEM,
        (valid.reshape(1, -1), *parts),
        name="finish",
    )
    return (encoded_grad, table_grad)


def solution(mesh):
    placed = (
        P(("group", "member"), None),
        P(("group", "member"), None),
        P(("group", "member"), None),
        P(("group", "member")),
        P(("group", "member")),
        P(("group", "member")),
    )
    return jax.shard_map(
        shards,
        mesh=mesh,
        in_specs=placed,
        out_specs=(P(("group", "member"), None), P(("group", "member"), None)),
        check_vma=False,
    )
```

```python
import functools

import jax
import jax.numpy as jnp
from jax import lax
from jax.experimental import pallas as pl
from jax.experimental.pallas import tpu as pltpu
from jax.sharding import PartitionSpec as P

F32 = jnp.float32
BF16 = jnp.bfloat16
I32 = jnp.int32
LANES = 128
VMEM = pl.BlockSpec(memory_space=pltpu.VMEM)
ANY = pl.BlockSpec(memory_space=pl.ANY)
SMEM = pl.BlockSpec(memory_space=pltpu.SMEM)

MIB = 1 << 20
BATCH = 8

NN = (((1,), (0,)), ((), ()))
NT = (((1,), (1,)), ((), ()))
TN = (((0,), (0,)), ((), ()))


def call(kernel, out_shape, ins, outs, args, scratch=(), limit=10, flops=0, moved=0, name=None):
    return pl.pallas_call(
        kernel,
        out_shape=out_shape,
        in_specs=ins,
        out_specs=outs,
        scratch_shapes=list(scratch),
        compiler_params=pltpu.CompilerParams(vmem_limit_bytes=limit * MIB),
        cost_estimate=pl.CostEstimate(flops=flops, bytes_accessed=moved, transcendentals=0),
        name=name,
    )(*args)


def iota(shape, dim):
    return lax.broadcasted_iota(I32, shape, dim)


def as_bf16(flag):
    return flag.astype(F32).astype(BF16)


def dot1(a, b, dims):
    return lax.dot_general(a, b, dims, preferred_element_type=F32)


def split(x):
    hi = x.astype(BF16)
    return hi, (x - hi.astype(F32)).astype(BF16)


def dot3(a, b, dims):
    return dot1(a[0], b[0], dims) + (dot1(a[0], b[1], dims) + dot1(a[1], b[0], dims))


def row_to_col(row):
    return jnp.transpose(jnp.broadcast_to(row, (LANES, row.shape[1])))[:, 0:1]


def split3(x):
    hi = x.astype(BF16)
    rest = x - hi.astype(F32)
    mid = rest.astype(BF16)
    return hi, mid, (rest - mid.astype(F32)).astype(BF16)


def dot6(a, b, dims):
    small = dot1(a[2], b[0], dims) + dot1(a[1], b[1], dims) + dot1(a[0], b[2], dims)
    return (small + (dot1(a[1], b[0], dims) + dot1(a[0], b[1], dims))) + dot1(a[0], b[0], dims)


def copy_rows(source, row_of, target, base, count):
    for b in range(0, count, BATCH):
        rows = [source[pl.ds(row_of(b + k), 1), :] for k in range(BATCH)] if count % BATCH == 0 else None
        if rows is None:
            for k in range(count):
                target[pl.ds(base + k, 1), :] = source[pl.ds(row_of(k), 1), :]
            return
        target[pl.ds(pl.multiple_of(base + b, BATCH), BATCH), :] = jnp.concatenate(rows, axis=0)


def front_kernel(members, rows_dev, slots, tokens, negatives, info, ints, enc_ref, out_ref, masked_ref):
    devices = out_ref.shape[0]
    shift = rows_dev.bit_length() - 1
    owner = ints[:, 0:tokens]
    local = ints[:, tokens : 2 * tokens]
    valid = ints[:, 2 * tokens : 3 * tokens]
    ids = ints[:, 3 * tokens :]
    masked_ref[...] = enc_ref[...] * row_to_col(valid.astype(F32))

    def ranks(owner_row, count):
        hot = iota((devices, count), 0) == owner_row
        before = as_bf16(iota((count, count), 0) < iota((count, count), 1))
        seen = dot1(as_bf16(hot), before, NN)
        return hot, jnp.sum(jnp.where(hot, seen, 0.0), axis=0, keepdims=True).astype(I32)

    def table(hot, value, place):
        return dot1(jnp.where(hot, value, 0.0).astype(BF16), place, NT)

    def placed(lane_row, count):
        return as_bf16(iota((LANES, count), 0) == lane_row)

    hot, rank = ranks(owner, tokens)
    place = placed(rank, tokens)
    high = table(hot, (local >> 6).astype(F32), place)
    low = table(hot, (local & 63).astype(F32), place)
    group = owner >> (members.bit_length() - 1)
    hot_member = (iota((devices, tokens), 0) & (members - 1)) == (owner & (members - 1))
    position = table(
        hot_member, (iota((1, tokens), 1) + 1).astype(F32), placed(group * slots + rank, tokens)
    )

    hot, rank = ranks(ids >> shift, negatives)
    place = placed(rank + slots, negatives)
    local = ids & (rows_dev - 1)
    high = high + table(hot, (local >> 6).astype(F32), place)
    low = low + table(hot, (local & 63).astype(F32), place)
    out_ref[:, 0, 0:LANES] = high.astype(I32) * 64 + low.astype(I32)
    out_ref[:, 0, LANES : 2 * LANES] = position.astype(I32)


def gather_kernel(members, chosen, part, count, info, requests, table, *refs):
    got, arrived = refs[-2:]
    copy = pltpu.make_async_copy(requests.at[:, :, 0:LANES], got, arrived)
    copy.start()
    copy.wait()
    for d, out in zip(chosen, refs[-2 - len(chosen) : -2]):
        first = (info[0] ^ d) * members

        def member(mr, carry, out=out, first=first):
            asked = got.at[first + mr, 0]
            copy_rows(table, lambda k: asked[part + k], out, mr * count, count)
            return carry

        lax.fori_loop(0, members, member, 0)


def score_kernel(blocks, groups, follows, info, *refs):
    rows, refs = refs[:groups], refs[groups:]
    encs, refs = refs[: len(blocks)], refs[len(blocks) :]
    stats, prob_hi, prob_lo = refs[-3:]
    if follows:
        stats[...] = refs[0][...]
    tokens = encs[0].shape[0]
    neg = split3(jnp.concatenate([row[...] for row in rows], axis=0))
    for i, e in enumerate(blocks):
        lanes = pl.ds(pl.multiple_of((info[1] ^ e) * tokens, LANES), tokens)
        score = dot6(neg, split3(encs[i][...]), NT)
        top = jnp.max(score, axis=0, keepdims=True)
        prob = jnp.exp(score - top)
        stats[0:1, lanes] = top
        stats[1:2, lanes] = jnp.sum(prob, axis=0, keepdims=True)
        parts = split(prob)
        prob_hi[i] = parts[0]
        prob_lo[i] = parts[1]


def own_places(members, info, got):
    return got[pl.ds(info[0] * members, members), 0, LANES : 2 * LANES]


def slot_hot(members, groups, slots, info, place_rows, column, mr, tokens):
    column[...] = row_to_col(place_rows[pl.ds(mr, 1), :])
    place = [
        column[pl.ds(pl.multiple_of((info[0] ^ d) * slots, slots), slots), :]
        for d in range(groups)
    ]
    return jnp.concatenate(place, axis=0) == iota((groups * slots, tokens), 1) + 1


def pick_kernel(members, groups, slots, info, got, *refs):
    encs = refs[:members]
    outs = refs[members : members + groups]
    place_rows, column = refs[members + groups :]
    place_rows[...] = own_places(members, info, got)
    for e in range(members):
        mr = info[1] ^ e
        tokens = encs[e].shape[0]
        hot = as_bf16(slot_hot(members, groups, slots, info, place_rows, column, mr, tokens))
        hi, mid, low = split3(encs[e][...])
        found = (dot1(hot, hi, NN) + dot1(hot, mid, NN)) + dot1(hot, low, NN)
        at = pl.ds(pl.multiple_of(mr * slots, slots), slots)
        for d in range(groups):
            outs[d][at, :] = found[d * slots : (d + 1) * slots]


def positive_kernel(members, groups, slots, tokens, info, got, stats, *refs):
    rows, picked = refs[:groups], refs[groups : 2 * groups]
    joined, own, place_rows, column = refs[2 * groups :]
    place_rows[...] = own_places(members, info, got)
    for e in range(members):
        mr = info[1] ^ e
        lanes = pl.ds(pl.multiple_of(mr * tokens, LANES), tokens)
        at = pl.ds(pl.multiple_of(mr * slots, slots), slots)
        hot = slot_hot(members, groups, slots, info, place_rows, column, mr, tokens)
        row = jnp.concatenate([r[at, :] for r in rows], axis=0)
        enc = jnp.concatenate([p[at, :] for p in picked], axis=0)
        value = jnp.sum(row * enc, axis=1, keepdims=True)
        positive = jnp.sum(jnp.where(hot, value, 0.0), axis=0, keepdims=True)
        has = jnp.sum(hot.astype(F32), axis=0, keepdims=True)
        old = stats[0:1, lanes]
        top = jnp.where(has > 0, jnp.maximum(old, positive), old)
        joined[0:1, lanes] = top
        joined[1:2, lanes] = stats[1:2, lanes] * jnp.exp(old - top) + jnp.where(
            has > 0, jnp.exp(positive - top), 0.0
        )
        own[0:1, lanes] = positive
        own[1:2, lanes] = has


def pulled_kernel(members, groups, slots, blocks, info, got, *refs):
    negs, refs = refs[:groups], refs[groups:]
    rows, refs = refs[:groups], refs[groups:]
    prob_hi, prob_lo, pulled, row_t, place_rows, column = refs
    place_rows[...] = own_places(members, info, got)
    neg = jnp.concatenate([row[...] for row in negs], axis=0)
    neg_t = split(jnp.transpose(neg))
    tokens = pulled.shape[2]
    for i, e in enumerate(blocks):
        mr = info[1] ^ e
        pulled[i] = dot3(neg_t, (prob_hi[i], prob_lo[i]), NN)
        at = pl.ds(pl.multiple_of(mr * slots, slots), slots)
        hot = slot_hot(members, groups, slots, info, place_rows, column, mr, tokens)
        high, low = split(jnp.concatenate([r[at, :] for r in rows], axis=0))
        row_t[i] = dot1(high, as_bf16(hot), TN) + dot1(low, as_bf16(hot), TN)


def join(first, second):
    top = jnp.maximum(first[0:1], second[0:1])
    total = first[1:2] * jnp.exp(first[0:1] - top) + second[1:2] * jnp.exp(second[0:1] - top)
    return top, total


def join_kernel(first, second, *refs):
    out = refs[-1]
    top, total = join(first[...], second[...])
    out[0:1, :] = top
    out[1:2, :] = total


def shares(info, e, tokens, final, stats, own):
    lanes = pl.ds(pl.multiple_of((info[1] ^ e) * tokens, LANES), tokens)
    top, total = final[0:1, lanes], final[1:2, lanes]
    scale = jnp.exp(stats[0:1, lanes] - top) / total
    extra = jnp.where(
        own[1:2, lanes] > 0, jnp.exp(own[0:1, lanes] - top) / total - 1.0, 0.0
    )
    return scale, extra


def pull_kernel(halves, blocks, tokens, info, final, stats, own, *refs):
    for e, out in zip(blocks, refs[-len(blocks) :]):
        h = 0 if e in halves[0] else 1
        pulled, row_t = (ref[halves[h].index(e)] for ref in refs[2 * h : 2 * h + 2])
        scale, extra = shares(info, e, tokens, final, stats, own)
        out[...] = pulled * scale + row_t * extra


def flat(table, lane, slots):
    return jnp.concatenate(
        [table[m : m + 1, lane : lane + slots] for m in range(table.shape[0])], axis=1
    )


def grad_kernel(members, groups, slots, halves, info, got, final, stats, own, *refs):
    probs, refs = refs[: 2 * len(halves)], refs[2 * len(halves) :]
    encs = refs[:members]
    *outs, total, coef, place_rows = refs[-groups - 3 :]
    place_rows[...] = own_places(members, info, got)
    tokens, width = encs[0].shape
    for h, i, e in [(h, i, e) for h, blocks in enumerate(halves) for i, e in enumerate(blocks)]:
        mr = info[1] ^ e
        scale, extra = shares(info, e, tokens, final, stats, own)
        enc = split(encs[e][...] * row_to_col(scale))
        part = dot3((probs[2 * h][i], probs[2 * h + 1][i]), enc, NN)
        if h == 0 and i == 0:
            total[...] = part
        else:
            total[...] += part
        hot = place_rows[pl.ds(mr, 1), :] == iota((tokens, LANES), 0) + 1
        coef[pl.ds(mr, 1), :] = jnp.sum(
            jnp.where(hot, row_to_col(extra), 0.0), axis=0, keepdims=True
        )
    count = total.shape[0] // groups
    lines = [flat(coef[...], g * slots, slots) for g in range(groups)]
    for d, out in enumerate(outs):
        out[0:count, :] = total[d * count : (d + 1) * count, :]
        line = lines[0]
        for g in range(1, groups):
            line = jnp.where((info[0] ^ d) == g, lines[g], line)
        out[count:, 0 : line.shape[1]] = jnp.broadcast_to(line, (8, line.shape[1]))


def equal_in_batch(ids):
    size = ids.shape[1]
    across = jnp.broadcast_to(ids.astype(F32), (size, size))
    same = (jnp.transpose(across) == across) & (
        (iota((size, size), 0) // BATCH) == (iota((size, size), 1) // BATCH)
    )
    return same.astype(F32)


def scatter_kernel(members, groups, own, slots, count, info, got_v, requests, *refs):
    size = len(own)
    grads, picked = refs[:size], refs[size : 2 * size]
    out, negs, tgts, got, arrived = refs[-5:]
    copy = pltpu.make_async_copy(requests.at[:, :, 0:LANES], got, arrived)
    copy.start()
    out[...] = refs[2 * size][...] if own[0] else jnp.zeros_like(out)

    def add_rows(asked, first, source, base, number):
        for b in range(0, number, BATCH):
            rows = [asked[first + b + k] for k in range(BATCH)]
            new = [
                out[pl.ds(rows[k], 1), :] + source[pl.ds(base + b + k, 1), :]
                for k in range(BATCH)
            ]
            for k in range(BATCH):
                out[pl.ds(rows[k], 1), :] = new[k]

    copy.wait()
    for i, d in enumerate(own):
        g = info[0] ^ d
        asked = got_v[pl.ds(g * members, members), 0, 0:LANES]
        number = members * count
        same = as_bf16(equal_in_batch(flat(asked, slots, count)) > 0)
        high, low = split(grads[i][0:number, :])
        negs[...] = dot1(same, high, NN) + dot1(same, low, NN)
        weight = equal_in_batch(flat(asked, 0, slots))
        weight = weight * grads[i][number : number + 1, 0 : members * slots]
        tgts[...] = dot3(split(weight), split(picked[i][...]), NN)
        merged = BATCH // count if count < BATCH else 1

        def member(step, carry, g=g, merged=merged):
            if merged == 1:
                add_rows(got.at[g * members + step, 0], slots, negs, step * count, count)
                add_rows(got.at[g * members + step, 0], 0, tgts, step * slots, slots)
                return carry
            first = g * members + step * merged
            rows = [
                got[first + k // count, 0, slots + k % count] for k in range(BATCH)
            ]
            new = [
                out[pl.ds(rows[k], 1), :] + negs[pl.ds(step * BATCH + k, 1), :]
                for k in range(BATCH)
            ]
            for k in range(BATCH):
                out[pl.ds(rows[k], 1), :] = new[k]
            for m in range(merged):
                add_rows(got.at[first + m, 0], 0, tgts, (step * merged + m) * slots, slots)
            return carry

        lax.fori_loop(0, members // merged, member, 0)


def add_kernel(terms, *refs):
    total = refs[0][...]
    for ref in refs[1:terms]:
        total = total + ref[...]
    refs[-1][...] = total


def finish_kernel(valid, *refs):
    total = refs[0][...]
    for ref in refs[1:-1]:
        total = total + ref[...]
    refs[-1][...] = jnp.transpose(total) * row_to_col(valid[...].astype(F32))


def swap(value, axis, d):
    return lax.ppermute(value, axis, [(i, i ^ d) for i in range(lax.axis_size(axis))])


def shards(encoded, item_table, target_owner, target_local, negative_ids, valid):
    groups, members = lax.axis_size("group"), lax.axis_size("member")
    devices = groups * members
    tokens, width = encoded.shape
    rows_dev = item_table.shape[0]
    negatives = negative_ids.shape[0]
    slots = max(2, 4 * tokens // devices)
    count = negatives // devices
    near = max(1, members // 4)
    everyone = members * tokens
    shape = jax.ShapeDtypeStruct
    sds = lambda *s: shape(s, F32)

    scalars = [pltpu.SMEM((devices, 1, LANES), I32), pltpu.SemaphoreType.DMA]
    info = jnp.stack([lax.axis_index("group"), lax.axis_index("member")]).astype(I32)
    ints = jnp.concatenate([target_owner.reshape(-1), target_local, valid, negative_ids])
    request, masked = call(
        functools.partial(front_kernel, members, rows_dev, slots, tokens, negatives),
        [shape((devices, 1, 2 * LANES), I32), sds(tokens, width)],
        [SMEM] + [VMEM] * 2,
        [VMEM] * 2,
        (info, ints.reshape(1, -1), encoded),
        name="front",
    )
    got = lax.all_to_all(
        request, ("group", "member"), split_axis=0, concat_axis=0, tiled=True
    )

    encs = [masked] + [None] * (members - 1)
    for z in (near, 2 * near):
        encs[z] = swap(masked, "member", z)
    onward, got = lax.optimization_barrier((encs[2 * near], got))
    encs[3 * near] = swap(onward, "member", near)
    for z in (0, 2 * near, 3 * near):
        for x in range(1, near):
            encs[z ^ x] = swap(onward if z == 2 * near else encs[z], "member", x)
    halves = [[d for d in range(members) if (d < near) or d in (near, 2 * near)], []]
    halves[1] = [d for d in range(members) if d not in halves[0]]

    early = [encs[d] for d in halves[0] if d and d != near]

    def after(blocks, done):
        return [lax.optimization_barrier((block, done))[0] for block in blocks]

    def gather(chosen, part, many, deps, name):
        return call(
            functools.partial(gather_kernel, members, chosen, part, many),
            [sds(members * many, width)] * len(chosen),
            [SMEM, ANY, VMEM] + [ANY] * len(deps),
            [VMEM] * len(chosen),
            (info, got, item_table, *deps),
            scratch=scalars,
            name=name,
        )

    negs = gather(range(groups), slots, count, early, "gather_negatives")
    for x in range(1, near):
        encs[near + x] = swap(lax.optimization_barrier((encs[x], negs[0]))[0], "member", near)
    negs = [negs[0]] + [swap(negs[d], "group", d) for d in range(1, groups)]
    waited = [encs[near], *encs[2 * near + 1 : 3 * near]]
    rows = gather(range(2, groups), 0, slots, waited, "gather_far_targets")
    gathered = rows
    rows = [swap(row, "group", d) for d, row in enumerate(rows, 2)]

    stats, probs = [], []
    for blocks in halves:
        many = len(blocks)
        *stats, hi, lo = call(
            functools.partial(score_kernel, blocks, groups, bool(stats)),
            [sds(2, everyone)] + [shape((many, negatives, tokens), BF16)] * 2,
            [SMEM] + [VMEM] * (groups + many + len(stats)) + [ANY] * len(gathered),
            [VMEM] * 3,
            (info, *negs, *[encs[e] for e in blocks], *stats, *gathered),
            flops=12 * many * tokens * negatives * width,
            moved=MIB,
            name="score",
        )
        probs += [hi, lo]
        if gathered:
            gathered = []
            kept, row = gather(range(2), 0, slots, stats, "gather_targets")
            rows = [kept, swap(row, "group", 1), *rows]
    stats = stats[0]
    picked = call(
        functools.partial(pick_kernel, members, groups, slots),
        [sds(members * slots, width)] * groups,
        [SMEM] + [VMEM] * (1 + members),
        [VMEM] * groups,
        (info, got, *encs),
        scratch=[pltpu.VMEM((members, LANES), I32), pltpu.VMEM((LANES, 1), I32)],
        name="pick",
    )
    sent = list(picked[:1]) + [
        swap(b, "group", d) for d, b in enumerate(after(picked[1:], stats), 1)
    ]
    joined, own = call(
        functools.partial(positive_kernel, members, groups, slots, tokens),
        [sds(2, everyone)] * 2,
        [SMEM] + [VMEM] * (2 + 2 * groups),
        [VMEM] * 2,
        (info, got, stats, *rows, *picked),
        scratch=[pltpu.VMEM((members, LANES), I32), pltpu.VMEM((LANES, 1), I32)],
        name="positive",
    )
    pulled = []
    for h, blocks in enumerate(halves):
        pulled += call(
            functools.partial(pulled_kernel, members, groups, slots, blocks),
            [sds(len(blocks), width, tokens)] * 2,
            [SMEM] + [VMEM] * (3 + 2 * groups),
            [VMEM] * 2,
            (info, got, *negs, *rows, *probs[2 * h : 2 * h + 2]),
            scratch=[pltpu.VMEM((members, LANES), I32), pltpu.VMEM((LANES, 1), I32)],
            flops=6 * len(blocks) * tokens * negatives * width,
            moved=MIB,
            name="pulled",
        )

    final = joined
    d, hops = 1, 0
    while d < members:
        late = pulled[2 * hops : 2 * hops + 2]
        hops += 1
        final = call(
            join_kernel,
            sds(2, everyone),
            [VMEM] * 2 + [ANY] * len(late),
            VMEM,
            (final, swap(final, "member", d), *late),
            name="join",
        )
        d *= 2

    grads = call(
        functools.partial(grad_kernel, members, groups, slots, halves),
        [sds(members * count + 8, width)] * groups,
        [SMEM] + [VMEM] * (4 + len(probs) + members) + [ANY] * (groups - 1),
        [VMEM] * groups,
        (info, got, final, stats, own, *probs, *encs, *sent[1:]),
        scratch=[
            pltpu.VMEM((negatives, width), F32),
            pltpu.VMEM((members, LANES), F32),
            pltpu.VMEM((members, LANES), I32),
        ],
        flops=6 * everyone * negatives * width,
        moved=8 * MIB,
        name="grad",
    )
    def added(terms, deps, flops=0):
        return call(
            functools.partial(add_kernel, len(terms)),
            sds(width, tokens),
            [VMEM] * len(terms) + [ANY] * len(deps),
            VMEM,
            (*terms, *deps),
            flops=flops,
            name="add",
        )

    graded = [grads[0]]
    grads = graded + [swap(grads[d], "group", d) for d in range(1, groups)]
    def scaled(blocks, deps):
        return call(
            functools.partial(pull_kernel, halves, blocks, tokens),
            [sds(width, tokens)] * len(blocks),
            [SMEM] + [VMEM] * 7 + [ANY] * len(deps),
            [VMEM] * len(blocks),
            (info, final, stats, own, *pulled, *deps),
            name="pull",
        )

    def beside(blocks):
        return [swap(block, "member", x) for x, block in enumerate(blocks, 1)]

    along = list(range(near))
    def scatter(own, base, deps, flops):
        return call(
            functools.partial(scatter_kernel, members, groups, own, slots, count),
            sds(rows_dev, width),
            [SMEM, VMEM, ANY] + [VMEM] * (2 * len(own) + len(base)) + [ANY] * len(deps),
            VMEM,
            (info, got, got, *[grads[d] for d in own], *[sent[d] for d in own], *base, *deps),
            scratch=[
                pltpu.VMEM((members * count, width), F32),
                pltpu.VMEM((members * slots, width), F32),
                *scalars,
            ],
            flops=flops,
            name="scatter",
        )

    farthest, *rest = scaled([*[3 * near + x for x in along], *[near + x for x in along[1:]]], [])
    rest, diagonal = rest[: near - 1], rest[near - 1 :]
    arrived = beside(rest)
    diagonal = [swap(block, "member", near) for block in diagonal]
    near_blocks = [near, *along[1:]]
    kept, far, *others = scaled(
        [0, *[2 * near + x for x in along], *near_blocks], graded
    )
    others, sends = others[: near - 1], others[near - 1 :]
    total = added([farthest, *arrived], [*graded, *diagonal])
    sums = [added([sends[x], diagonal[x - 1]], []) for x in along[1:]]
    others = after(others, total)
    table_own = scatter(list(range(2)), [], [total], 1 << 33)
    far = added([far], [table_own, *grads[2:]])
    others = beside(others)
    half = added([far, swap(total, "member", near), *others], [])
    held = after([sends[0], *sums], others[0])
    parts = [swap(b, "member", d) for d, b in zip(near_blocks, held)]
    parts.append(added([kept, swap(half, "member", 2 * near)], []))

    table_grad = scatter(list(range(2, groups)), [table_own], [], 0)
    encoded_grad = call(
        finish_kernel,
        sds(tokens, width),
        [VMEM] * (1 + len(parts)),
        VMEM,
        (valid.reshape(1, -1), *parts),
        name="finish",
    )
    return (encoded_grad, table_grad)


def solution(mesh):
    placed = (
        P(("group", "member"), None),
        P(("group", "member"), None),
        P(("group", "member"), None),
        P(("group", "member")),
        P(("group", "member")),
        P(("group", "member")),
    )
    return jax.shard_map(
        shards,
        mesh=mesh,
        in_specs=placed,
        out_specs=(P(("group", "member"), None), P(("group", "member"), None)),
        check_vma=False,
    )
```

```python
import functools

import jax
import jax.numpy as jnp
from jax import lax
from jax.experimental import pallas as pl
from jax.experimental.pallas import tpu as pltpu
from jax.sharding import PartitionSpec as P

F32 = jnp.float32
BF16 = jnp.bfloat16
I32 = jnp.int32
LANES = 128
VMEM = pl.BlockSpec(memory_space=pltpu.VMEM)
ANY = pl.BlockSpec(memory_space=pl.ANY)
SMEM = pl.BlockSpec(memory_space=pltpu.SMEM)
MIB = 1 << 20
BATCH = 8

NN = (((1,), (0,)), ((), ()))
NT = (((1,), (1,)), ((), ()))
TN = (((0,), (0,)), ((), ()))


def call(kernel, out_shape, ins, outs, args, scratch=(), limit=10, flops=0, moved=0, name=None):
    return pl.pallas_call(
        kernel,
        out_shape=out_shape,
        in_specs=ins,
        out_specs=outs,
        scratch_shapes=list(scratch),
        compiler_params=pltpu.CompilerParams(vmem_limit_bytes=limit * MIB),
        cost_estimate=pl.CostEstimate(flops=flops, bytes_accessed=moved, transcendentals=0),
        name=name,
    )(*args)


def iota(shape, dim):
    return lax.broadcasted_iota(I32, shape, dim)


def as_bf16(flag):
    return flag.astype(F32).astype(BF16)


def dot1(a, b, dims):
    return lax.dot_general(a, b, dims, preferred_element_type=F32)


def split(x):
    hi = x.astype(BF16)
    return hi, (x - hi.astype(F32)).astype(BF16)


def dot3(a, b, dims):
    return dot1(a[0], b[0], dims) + (dot1(a[0], b[1], dims) + dot1(a[1], b[0], dims))


def row_to_col(row):
    return jnp.transpose(jnp.broadcast_to(row, (LANES, row.shape[1])))[:, 0:1]


def split3(x):
    hi = x.astype(BF16)
    rest = x - hi.astype(F32)
    mid = rest.astype(BF16)
    return hi, mid, (rest - mid.astype(F32)).astype(BF16)


def dot6(a, b, dims):
    small = dot1(a[2], b[0], dims) + dot1(a[1], b[1], dims) + dot1(a[0], b[2], dims)
    return (small + (dot1(a[1], b[0], dims) + dot1(a[0], b[1], dims))) + dot1(a[0], b[0], dims)


def copy_rows(source, row_of, target, base, count):
    for b in range(0, count, BATCH):
        rows = [source[pl.ds(row_of(b + k), 1), :] for k in range(BATCH)] if count % BATCH == 0 else None
        if rows is None:
            for k in range(count):
                target[pl.ds(base + k, 1), :] = source[pl.ds(row_of(k), 1), :]
            return
        target[pl.ds(pl.multiple_of(base + b, BATCH), BATCH), :] = jnp.concatenate(rows, axis=0)


def front_kernel(members, rows_dev, slots, tokens, negatives, info, ints, enc_ref, out_ref, masked_ref):
    devices = out_ref.shape[0]
    shift = rows_dev.bit_length() - 1
    owner = ints[:, 0:tokens]
    local = ints[:, tokens : 2 * tokens]
    valid = ints[:, 2 * tokens : 3 * tokens]
    ids = ints[:, 3 * tokens :]
    masked_ref[...] = enc_ref[...] * row_to_col(valid.astype(F32))

    def ranks(owner_row, count):
        hot = iota((devices, count), 0) == owner_row
        before = as_bf16(iota((count, count), 0) < iota((count, count), 1))
        seen = dot1(as_bf16(hot), before, NN)
        return hot, jnp.sum(jnp.where(hot, seen, 0.0), axis=0, keepdims=True).astype(I32)

    def table(hot, value, place):
        return dot1(jnp.where(hot, value, 0.0).astype(BF16), place, NT)

    def placed(lane_row, count):
        return as_bf16(iota((LANES, count), 0) == lane_row)

    hot, rank = ranks(owner, tokens)
    place = placed(rank, tokens)
    high = table(hot, (local >> 6).astype(F32), place)
    low = table(hot, (local & 63).astype(F32), place)
    group = owner >> (members.bit_length() - 1)
    hot_member = (iota((devices, tokens), 0) & (members - 1)) == (owner & (members - 1))
    position = table(
        hot_member, (iota((1, tokens), 1) + 1).astype(F32), placed(group * slots + rank, tokens)
    )

    hot, rank = ranks(ids >> shift, negatives)
    place = placed(rank + slots, negatives)
    local = ids & (rows_dev - 1)
    high = high + table(hot, (local >> 6).astype(F32), place)
    low = low + table(hot, (local & 63).astype(F32), place)
    out_ref[:, 0, 0:LANES] = high.astype(I32) * 64 + low.astype(I32)
    out_ref[:, 0, LANES : 2 * LANES] = position.astype(I32)


def gather_kernel(members, chosen, part, count, info, got, table, *refs):
    for d, out in zip(chosen, refs[-len(chosen) :]):
        first = (info[0] ^ d) * members

        def member(mr, carry, out=out, first=first):
            asked = got.at[first + mr, 0]
            copy_rows(table, lambda k: asked[part + k], out, mr * count, count)
            return carry

        lax.fori_loop(0, members, member, 0)


def score_kernel(blocks, groups, follows, info, *refs):
    rows, refs = refs[:groups], refs[groups:]
    encs, refs = refs[: len(blocks)], refs[len(blocks) :]
    stats, prob_hi, prob_lo = refs[-3:]
    if follows:
        stats[...] = refs[0][...]
    tokens = encs[0].shape[0]
    neg = split3(jnp.concatenate([row[...] for row in rows], axis=0))
    for i, e in enumerate(blocks):
        lanes = pl.ds(pl.multiple_of((info[1] ^ e) * tokens, LANES), tokens)
        score = dot6(neg, split3(encs[i][...]), NT)
        top = jnp.max(score, axis=0, keepdims=True)
        prob = jnp.exp(score - top)
        stats[0:1, lanes] = top
        stats[1:2, lanes] = jnp.sum(prob, axis=0, keepdims=True)
        parts = split(prob)
        prob_hi[i] = parts[0]
        prob_lo[i] = parts[1]


def own_places(members, info, got):
    return got[pl.ds(info[0] * members, members), 0, LANES : 2 * LANES]


def slot_hot(members, groups, slots, info, place_rows, column, mr, tokens):
    column[...] = row_to_col(place_rows[pl.ds(mr, 1), :])
    place = [
        column[pl.ds(pl.multiple_of((info[0] ^ d) * slots, slots), slots), :]
        for d in range(groups)
    ]
    return jnp.concatenate(place, axis=0) == iota((groups * slots, tokens), 1) + 1


def pick_kernel(members, groups, slots, info, got, *refs):
    encs = refs[:members]
    outs = refs[members : members + groups]
    place_rows, column = refs[members + groups :]
    place_rows[...] = own_places(members, info, got)
    for e in range(members):
        mr = info[1] ^ e
        tokens = encs[e].shape[0]
        hot = as_bf16(slot_hot(members, groups, slots, info, place_rows, column, mr, tokens))
        hi, mid, low = split3(encs[e][...])
        found = (dot1(hot, hi, NN) + dot1(hot, mid, NN)) + dot1(hot, low, NN)
        at = pl.ds(pl.multiple_of(mr * slots, slots), slots)
        for d in range(groups):
            outs[d][at, :] = found[d * slots : (d + 1) * slots]


def positive_kernel(members, groups, slots, tokens, info, got, stats, *refs):
    rows, picked = refs[:groups], refs[groups : 2 * groups]
    joined, own, place_rows, column = refs[2 * groups :]
    place_rows[...] = own_places(members, info, got)
    for e in range(members):
        mr = info[1] ^ e
        lanes = pl.ds(pl.multiple_of(mr * tokens, LANES), tokens)
        at = pl.ds(pl.multiple_of(mr * slots, slots), slots)
        hot = slot_hot(members, groups, slots, info, place_rows, column, mr, tokens)
        row = jnp.concatenate([r[at, :] for r in rows], axis=0)
        enc = jnp.concatenate([p[at, :] for p in picked], axis=0)
        value = jnp.sum(row * enc, axis=1, keepdims=True)
        positive = jnp.sum(jnp.where(hot, value, 0.0), axis=0, keepdims=True)
        has = jnp.sum(hot.astype(F32), axis=0, keepdims=True)
        old = stats[0:1, lanes]
        top = jnp.where(has > 0, jnp.maximum(old, positive), old)
        joined[0:1, lanes] = top
        joined[1:2, lanes] = stats[1:2, lanes] * jnp.exp(old - top) + jnp.where(
            has > 0, jnp.exp(positive - top), 0.0
        )
        own[0:1, lanes] = positive
        own[1:2, lanes] = has


def pulled_kernel(members, groups, slots, blocks, info, got, *refs):
    negs, refs = refs[:groups], refs[groups:]
    rows, refs = refs[:groups], refs[groups:]
    prob_hi, prob_lo, pulled, row_t, place_rows, column = refs
    place_rows[...] = own_places(members, info, got)
    neg = jnp.concatenate([row[...] for row in negs], axis=0)
    neg_t = split(jnp.transpose(neg))
    tokens = pulled.shape[2]
    for i, e in enumerate(blocks):
        mr = info[1] ^ e
        pulled[i] = dot3(neg_t, (prob_hi[i], prob_lo[i]), NN)
        at = pl.ds(pl.multiple_of(mr * slots, slots), slots)
        hot = slot_hot(members, groups, slots, info, place_rows, column, mr, tokens)
        high, low = split(jnp.concatenate([r[at, :] for r in rows], axis=0))
        row_t[i] = dot1(high, as_bf16(hot), TN) + dot1(low, as_bf16(hot), TN)


def join(first, second):
    top = jnp.maximum(first[0:1], second[0:1])
    total = first[1:2] * jnp.exp(first[0:1] - top) + second[1:2] * jnp.exp(second[0:1] - top)
    return top, total


def join_kernel(first, second, *refs):
    out = refs[-1]
    top, total = join(first[...], second[...])
    out[0:1, :] = top
    out[1:2, :] = total


def shares(info, e, tokens, final, stats, own):
    lanes = pl.ds(pl.multiple_of((info[1] ^ e) * tokens, LANES), tokens)
    top, total = final[0:1, lanes], final[1:2, lanes]
    scale = jnp.exp(stats[0:1, lanes] - top) / total
    extra = jnp.where(
        own[1:2, lanes] > 0, jnp.exp(own[0:1, lanes] - top) / total - 1.0, 0.0
    )
    return scale, extra


def pull_kernel(halves, blocks, tokens, info, final, stats, own, *refs):
    for e, out in zip(blocks, refs[-len(blocks) :]):
        h = 0 if e in halves[0] else 1
        pulled, row_t = (ref[halves[h].index(e)] for ref in refs[2 * h : 2 * h + 2])
        scale, extra = shares(info, e, tokens, final, stats, own)
        out[...] = pulled * scale + row_t * extra


def flat(table, lane, slots):
    return jnp.concatenate(
        [table[m : m + 1, lane : lane + slots] for m in range(table.shape[0])], axis=1
    )


def grad_kernel(members, groups, slots, halves, info, got, final, stats, own, *refs):
    probs, refs = refs[: 2 * len(halves)], refs[2 * len(halves) :]
    encs = refs[:members]
    *outs, total, coef, place_rows = refs[-groups - 3 :]
    place_rows[...] = own_places(members, info, got)
    tokens, width = encs[0].shape
    for h, i, e in [(h, i, e) for h, blocks in enumerate(halves) for i, e in enumerate(blocks)]:
        mr = info[1] ^ e
        scale, extra = shares(info, e, tokens, final, stats, own)
        enc = split(encs[e][...] * row_to_col(scale))
        part = dot3((probs[2 * h][i], probs[2 * h + 1][i]), enc, NN)
        if h == 0 and i == 0:
            total[...] = part
        else:
            total[...] += part
        hot = place_rows[pl.ds(mr, 1), :] == iota((tokens, LANES), 0) + 1
        coef[pl.ds(mr, 1), :] = jnp.sum(
            jnp.where(hot, row_to_col(extra), 0.0), axis=0, keepdims=True
        )
    count = total.shape[0] // groups
    lines = [flat(coef[...], g * slots, slots) for g in range(groups)]
    for d, out in enumerate(outs):
        out[0:count, :] = total[d * count : (d + 1) * count, :]
        line = lines[0]
        for g in range(1, groups):
            line = jnp.where((info[0] ^ d) == g, lines[g], line)
        out[count:, 0 : line.shape[1]] = jnp.broadcast_to(line, (8, line.shape[1]))


def equal_in_batch(ids):
    size = ids.shape[1]
    across = jnp.broadcast_to(ids.astype(F32), (size, size))
    same = (jnp.transpose(across) == across) & (
        (iota((size, size), 0) // BATCH) == (iota((size, size), 1) // BATCH)
    )
    return same.astype(F32)


def scatter_kernel(members, groups, own, slots, count, info, got_v, got, *refs):
    size = len(own)
    grads, picked = refs[:size], refs[size : 2 * size]
    out, negs, tgts = refs[-3:]
    out[...] = refs[2 * size][...] if own[0] else jnp.zeros_like(out)

    def add_rows(asked, first, source, base, number):
        for b in range(0, number, BATCH):
            rows = [asked[first + b + k] for k in range(BATCH)]
            new = [
                out[pl.ds(rows[k], 1), :] + source[pl.ds(base + b + k, 1), :]
                for k in range(BATCH)
            ]
            for k in range(BATCH):
                out[pl.ds(rows[k], 1), :] = new[k]

    for i, d in enumerate(own):
        g = info[0] ^ d
        asked = got_v[pl.ds(g * members, members), 0, 0:LANES]
        number = members * count
        same = as_bf16(equal_in_batch(flat(asked, slots, count)) > 0)
        high, low = split(grads[i][0:number, :])
        negs[...] = dot1(same, high, NN) + dot1(same, low, NN)
        weight = equal_in_batch(flat(asked, 0, slots))
        weight = weight * grads[i][number : number + 1, 0 : members * slots]
        tgts[...] = dot3(split(weight), split(picked[i][...]), NN)
        merged = BATCH // count if count < BATCH else 1

        def member(step, carry, g=g, merged=merged):
            if merged == 1:
                add_rows(got.at[g * members + step, 0], slots, negs, step * count, count)
                add_rows(got.at[g * members + step, 0], 0, tgts, step * slots, slots)
                return carry
            first = g * members + step * merged
            rows = [
                got[first + k // count, 0, slots + k % count] for k in range(BATCH)
            ]
            new = [
                out[pl.ds(rows[k], 1), :] + negs[pl.ds(step * BATCH + k, 1), :]
                for k in range(BATCH)
            ]
            for k in range(BATCH):
                out[pl.ds(rows[k], 1), :] = new[k]
            for m in range(merged):
                add_rows(got.at[first + m, 0], 0, tgts, (step * merged + m) * slots, slots)
            return carry

        lax.fori_loop(0, members // merged, member, 0)


def add_kernel(terms, *refs):
    total = refs[0][...]
    for ref in refs[1:terms]:
        total = total + ref[...]
    refs[-1][...] = total


def finish_kernel(valid, *refs):
    total = refs[0][...]
    for ref in refs[1:-1]:
        total = total + ref[...]
    refs[-1][...] = jnp.transpose(total) * row_to_col(valid[...].astype(F32))


def swap(value, axis, d):
    return lax.ppermute(value, axis, [(i, i ^ d) for i in range(lax.axis_size(axis))])


def shards(encoded, item_table, target_owner, target_local, negative_ids, valid):
    groups, members = lax.axis_size("group"), lax.axis_size("member")
    devices = groups * members
    tokens, width = encoded.shape
    rows_dev = item_table.shape[0]
    negatives = negative_ids.shape[0]
    slots = max(2, 4 * tokens // devices)
    count = negatives // devices
    near = max(1, members // 4)
    everyone = members * tokens
    shape = jax.ShapeDtypeStruct
    sds = lambda *s: shape(s, F32)

    info = jnp.stack([lax.axis_index("group"), lax.axis_index("member")]).astype(I32)
    ints = jnp.concatenate([target_owner.reshape(-1), target_local, valid, negative_ids])
    request, masked = call(
        functools.partial(front_kernel, members, rows_dev, slots, tokens, negatives),
        [shape((devices, 1, 2 * LANES), I32), sds(tokens, width)],
        [SMEM] + [VMEM] * 2,
        [VMEM] * 2,
        (info, ints.reshape(1, -1), encoded),
        name="front",
    )
    got = lax.all_to_all(
        request, ("group", "member"), split_axis=0, concat_axis=0, tiled=True
    )

    encs = [masked] + [None] * (members - 1)
    for z in (near, 2 * near):
        encs[z] = swap(masked, "member", z)
    onward, got = lax.optimization_barrier((encs[2 * near], got))
    encs[3 * near] = swap(onward, "member", near)
    for z in (0, 2 * near):
        for x in range(1, near):
            encs[z ^ x] = swap(onward if z == 2 * near else encs[z], "member", x)
    halves = [[d for d in range(members) if (d < near) or d in (near, 2 * near)], []]
    halves[1] = [d for d in range(members) if d not in halves[0]]

    early = [encs[d] for d in halves[0] if d and d != near]

    def after(blocks, done):
        return [lax.optimization_barrier((block, done))[0] for block in blocks]

    def gather(chosen, part, many, deps, name):
        return call(
            functools.partial(gather_kernel, members, chosen, part, many),
            [sds(members * many, width)] * len(chosen),
            [SMEM, SMEM, VMEM] + [ANY] * len(deps),
            [VMEM] * len(chosen),
            (info, got, item_table, *deps),
            name=name,
        )

    negs = gather(range(groups), slots, count, early, "gather_negatives")
    for x in range(1, near):
        encs[near + x] = swap(lax.optimization_barrier((encs[x], negs[0]))[0], "member", near)
    negs = [negs[0]] + [swap(negs[d], "group", d) for d in range(1, groups)]
    waited = [encs[near], *encs[2 * near + 1 : 3 * near]]
    rows = gather(range(2, groups), 0, slots, waited, "gather_far_targets")
    gathered = rows
    for x in range(1, near):
        encs[3 * near + x] = swap(after([encs[3 * near]], rows[0])[0], "member", x)
    rows = [swap(row, "group", d) for d, row in enumerate(rows, 2)]

    stats, probs = [], []
    for blocks in halves:
        many = len(blocks)
        *stats, hi, lo = call(
            functools.partial(score_kernel, blocks, groups, bool(stats)),
            [sds(2, everyone)] + [shape((many, negatives, tokens), BF16)] * 2,
            [SMEM] + [VMEM] * (groups + many + len(stats)) + [ANY] * len(gathered),
            [VMEM] * 3,
            (info, *negs, *[encs[e] for e in blocks], *stats, *gathered),
            flops=12 * many * tokens * negatives * width,
            moved=MIB,
            name="score",
        )
        probs += [hi, lo]
        if gathered:
            gathered = []
            kept, row = gather(range(2), 0, slots, stats, "gather_targets")
            rows = [kept, swap(row, "group", 1), *rows]
    stats = stats[0]
    picked = call(
        functools.partial(pick_kernel, members, groups, slots),
        [sds(members * slots, width)] * groups,
        [SMEM] + [VMEM] * (1 + members),
        [VMEM] * groups,
        (info, got, *encs),
        scratch=[pltpu.VMEM((members, LANES), I32), pltpu.VMEM((LANES, 1), I32)],
        name="pick",
    )
    sent = list(picked[:1]) + [
        swap(b, "group", d) for d, b in enumerate(after(picked[1:], stats), 1)
    ]
    joined, own = call(
        functools.partial(positive_kernel, members, groups, slots, tokens),
        [sds(2, everyone)] * 2,
        [SMEM] + [VMEM] * (2 + 2 * groups),
        [VMEM] * 2,
        (info, got, stats, *rows, *picked),
        scratch=[pltpu.VMEM((members, LANES), I32), pltpu.VMEM((LANES, 1), I32)],
        name="positive",
    )
    pulled = []
    for h, blocks in enumerate(halves):
        pulled += call(
            functools.partial(pulled_kernel, members, groups, slots, blocks),
            [sds(len(blocks), width, tokens)] * 2,
            [SMEM] + [VMEM] * (3 + 2 * groups),
            [VMEM] * 2,
            (info, got, *negs, *rows, *probs[2 * h : 2 * h + 2]),
            scratch=[pltpu.VMEM((members, LANES), I32), pltpu.VMEM((LANES, 1), I32)],
            flops=6 * len(blocks) * tokens * negatives * width,
            moved=MIB,
            name="pulled",
        )

    final = joined
    d, hops = 1, 0
    while d < members:
        late = pulled[2 * hops : 2 * hops + 2]
        hops += 1
        final = call(
            join_kernel,
            sds(2, everyone),
            [VMEM] * 2 + [ANY] * len(late),
            VMEM,
            (final, swap(final, "member", d), *late),
            name="join",
        )
        d *= 2

    grads = call(
        functools.partial(grad_kernel, members, groups, slots, halves),
        [sds(members * count + 8, width)] * groups,
        [SMEM] + [VMEM] * (4 + len(probs) + members) + [ANY] * (groups - 1),
        [VMEM] * groups,
        (info, got, final, stats, own, *probs, *encs, *sent[1:]),
        scratch=[
            pltpu.VMEM((negatives, width), F32),
            pltpu.VMEM((members, LANES), F32),
            pltpu.VMEM((members, LANES), I32),
        ],
        flops=6 * everyone * negatives * width,
        moved=8 * MIB,
        name="grad",
    )
    def added(terms, deps, flops=0):
        return call(
            functools.partial(add_kernel, len(terms)),
            sds(width, tokens),
            [VMEM] * len(terms) + [ANY] * len(deps),
            VMEM,
            (*terms, *deps),
            flops=flops,
            name="add",
        )

    graded = [grads[0]]
    grads = graded + [swap(grads[d], "group", d) for d in range(1, groups)]
    def scaled(blocks, deps):
        return call(
            functools.partial(pull_kernel, halves, blocks, tokens),
            [sds(width, tokens)] * len(blocks),
            [SMEM] + [VMEM] * 7 + [ANY] * len(deps),
            [VMEM] * len(blocks),
            (info, final, stats, own, *pulled, *deps),
            name="pull",
        )

    def beside(blocks):
        return [swap(block, "member", x) for x, block in enumerate(blocks, 1)]

    along = list(range(near))
    def scatter(own, base, deps, flops):
        return call(
            functools.partial(scatter_kernel, members, groups, own, slots, count),
            sds(rows_dev, width),
            [SMEM, VMEM, SMEM] + [VMEM] * (2 * len(own) + len(base)) + [ANY] * len(deps),
            VMEM,
            (info, got, got, *[grads[d] for d in own], *[sent[d] for d in own], *base, *deps),
            scratch=[
                pltpu.VMEM((members * count, width), F32),
                pltpu.VMEM((members * slots, width), F32),
            ],
            flops=flops,
            name="scatter",
        )

    farthest, *rest = scaled([*[3 * near + x for x in along], *[near + x for x in along[1:]]], [])
    rest, diagonal = rest[: near - 1], rest[near - 1 :]
    arrived = beside(rest)
    diagonal = [swap(block, "member", near) for block in diagonal]
    near_blocks = [near, *along[1:]]
    kept, far, *others = scaled(
        [0, *[2 * near + x for x in along], *near_blocks], graded
    )
    others, sends = others[: near - 1], others[near - 1 :]
    total = added([farthest, *arrived], [*graded, *diagonal])
    sums = [added([sends[x], diagonal[x - 1]], []) for x in along[1:]]
    others = after(others, total)
    table_own = scatter(list(range(2)), [], [total], 1 << 33)
    far = added([far], [table_own, *grads[2:]])
    others = beside(others)
    half = added([far, swap(total, "member", near), *others], [])
    held = after(sends[:1], others[0]) + after(sums, half)
    parts = [swap(b, "member", d) for d, b in zip(near_blocks, held)]
    parts.append(added([kept, swap(half, "member", 2 * near)], []))

    table_grad = scatter(list(range(2, groups)), [table_own], [], 0)
    encoded_grad = call(
        finish_kernel,
        sds(tokens, width),
        [VMEM] * (1 + len(parts)),
        VMEM,
        (valid.reshape(1, -1), *parts),
        name="finish",
    )
    return (encoded_grad, table_grad)


def solution(mesh):
    placed = (
        P(("group", "member"), None),
        P(("group", "member"), None),
        P(("group", "member"), None),
        P(("group", "member")),
        P(("group", "member")),
        P(("group", "member")),
    )
    return jax.shard_map(
        shards,
        mesh=mesh,
        in_specs=placed,
        out_specs=(P(("group", "member"), None), P(("group", "member"), None)),
        check_vma=False,
    )
```

```python
import functools

import jax
import jax.numpy as jnp
from jax import lax
from jax.experimental import pallas as pl
from jax.experimental.pallas import tpu as pltpu
from jax.sharding import PartitionSpec as P

F32 = jnp.float32
BF16 = jnp.bfloat16
I32 = jnp.int32
LANES = 128
VMEM = pl.BlockSpec(memory_space=pltpu.VMEM)
ANY = pl.BlockSpec(memory_space=pl.ANY)
SMEM = pl.BlockSpec(memory_space=pltpu.SMEM)
MIB = 1 << 20
BATCH = 8

NN = (((1,), (0,)), ((), ()))
NT = (((1,), (1,)), ((), ()))
TN = (((0,), (0,)), ((), ()))


PLACE = object()


def located(kernel):
    def run(*refs):
        kernel((lax.axis_index("group"), lax.axis_index("member")), *refs)

    return run


def call(kernel, out_shape, ins, outs, args, scratch=(), limit=10, flops=0, moved=0, name=None):
    if args[0] is PLACE:
        kernel, ins, args = located(kernel), ins[1:], args[1:]
    return pl.pallas_call(
        kernel,
        out_shape=out_shape,
        in_specs=ins,
        out_specs=outs,
        scratch_shapes=list(scratch),
        compiler_params=pltpu.CompilerParams(vmem_limit_bytes=limit * MIB),
        cost_estimate=pl.CostEstimate(flops=flops, bytes_accessed=moved, transcendentals=0),
        name=name,
    )(*args)


def iota(shape, dim):
    return lax.broadcasted_iota(I32, shape, dim)


def as_bf16(flag):
    return flag.astype(F32).astype(BF16)


def dot1(a, b, dims):
    return lax.dot_general(a, b, dims, preferred_element_type=F32)


def split(x):
    hi = x.astype(BF16)
    return hi, (x - hi.astype(F32)).astype(BF16)


def dot3(a, b, dims):
    return dot1(a[0], b[0], dims) + (dot1(a[0], b[1], dims) + dot1(a[1], b[0], dims))


def row_to_col(row):
    return jnp.transpose(jnp.broadcast_to(row, (LANES, row.shape[1])))[:, 0:1]


def split3(x):
    hi = x.astype(BF16)
    rest = x - hi.astype(F32)
    mid = rest.astype(BF16)
    return hi, mid, (rest - mid.astype(F32)).astype(BF16)


def dot6(a, b, dims):
    small = dot1(a[2], b[0], dims) + dot1(a[1], b[1], dims) + dot1(a[0], b[2], dims)
    return (small + (dot1(a[1], b[0], dims) + dot1(a[0], b[1], dims))) + dot1(a[0], b[0], dims)


def copy_rows(source, row_of, target, base, count):
    for b in range(0, count, BATCH):
        rows = [source[pl.ds(row_of(b + k), 1), :] for k in range(BATCH)] if count % BATCH == 0 else None
        if rows is None:
            for k in range(count):
                target[pl.ds(base + k, 1), :] = source[pl.ds(row_of(k), 1), :]
            return
        target[pl.ds(pl.multiple_of(base + b, BATCH), BATCH), :] = jnp.concatenate(rows, axis=0)


def front_kernel(members, rows_dev, slots, tokens, negatives, info, ints, enc_ref, out_ref, masked_ref):
    devices = out_ref.shape[0]
    shift = rows_dev.bit_length() - 1
    owner = ints[:, 0:tokens]
    local = ints[:, tokens : 2 * tokens]
    valid = ints[:, 2 * tokens : 3 * tokens]
    ids = ints[:, 3 * tokens :]
    masked_ref[...] = enc_ref[...] * row_to_col(valid.astype(F32))

    def ranks(owner_row, count):
        hot = iota((devices, count), 0) == owner_row
        before = as_bf16(iota((count, count), 0) < iota((count, count), 1))
        seen = dot1(as_bf16(hot), before, NN)
        return hot, jnp.sum(jnp.where(hot, seen, 0.0), axis=0, keepdims=True).astype(I32)

    def table(hot, value, place):
        return dot1(jnp.where(hot, value, 0.0).astype(BF16), place, NT)

    def placed(lane_row, count):
        return as_bf16(iota((LANES, count), 0) == lane_row)

    hot, rank = ranks(owner, tokens)
    place = placed(rank, tokens)
    high = table(hot, (local >> 6).astype(F32), place)
    low = table(hot, (local & 63).astype(F32), place)
    group = owner >> (members.bit_length() - 1)
    hot_member = (iota((devices, tokens), 0) & (members - 1)) == (owner & (members - 1))
    position = table(
        hot_member, (iota((1, tokens), 1) + 1).astype(F32), placed(group * slots + rank, tokens)
    )

    hot, rank = ranks(ids >> shift, negatives)
    place = placed(rank + slots, negatives)
    local = ids & (rows_dev - 1)
    high = high + table(hot, (local >> 6).astype(F32), place)
    low = low + table(hot, (local & 63).astype(F32), place)
    out_ref[:, 0, 0:LANES] = high.astype(I32) * 64 + low.astype(I32)
    out_ref[:, 0, LANES : 2 * LANES] = position.astype(I32)


def gather_kernel(members, chosen, part, count, info, got, table, *refs):
    for d, out in zip(chosen, refs[-len(chosen) :]):
        first = (info[0] ^ d) * members

        def member(mr, carry, out=out, first=first):
            asked = got.at[first + mr, 0]
            copy_rows(table, lambda k: asked[part + k], out, mr * count, count)
            return carry

        lax.fori_loop(0, members, member, 0)


def score_kernel(blocks, groups, follows, info, *refs):
    rows, refs = refs[:groups], refs[groups:]
    encs, refs = refs[: len(blocks)], refs[len(blocks) :]
    stats, prob_hi, prob_lo = refs[-3:]
    if follows:
        stats[...] = refs[0][...]
    tokens = encs[0].shape[0]
    neg = split3(jnp.concatenate([row[...] for row in rows], axis=0))
    for i, e in enumerate(blocks):
        lanes = pl.ds(pl.multiple_of((info[1] ^ e) * tokens, LANES), tokens)
        score = dot6(neg, split3(encs[i][...]), NT)
        top = jnp.max(score, axis=0, keepdims=True)
        prob = jnp.exp(score - top)
        stats[0:1, lanes] = top
        stats[1:2, lanes] = jnp.sum(prob, axis=0, keepdims=True)
        parts = split(prob)
        prob_hi[i] = parts[0]
        prob_lo[i] = parts[1]


def own_places(members, info, got):
    return got[pl.ds(info[0] * members, members), 0, LANES : 2 * LANES]


def slot_hot(members, groups, slots, info, place_rows, column, mr, tokens):
    column[...] = row_to_col(place_rows[pl.ds(mr, 1), :])
    place = [
        column[pl.ds(pl.multiple_of((info[0] ^ d) * slots, slots), slots), :]
        for d in range(groups)
    ]
    return jnp.concatenate(place, axis=0) == iota((groups * slots, tokens), 1) + 1


def pick_kernel(members, groups, slots, info, got, *refs):
    encs = refs[:members]
    outs = refs[members : members + groups]
    place_rows, column = refs[members + groups :]
    place_rows[...] = own_places(members, info, got)
    for e in range(members):
        mr = info[1] ^ e
        tokens = encs[e].shape[0]
        hot = as_bf16(slot_hot(members, groups, slots, info, place_rows, column, mr, tokens))
        hi, mid, low = split3(encs[e][...])
        found = (dot1(hot, hi, NN) + dot1(hot, mid, NN)) + dot1(hot, low, NN)
        at = pl.ds(pl.multiple_of(mr * slots, slots), slots)
        for d in range(groups):
            outs[d][at, :] = found[d * slots : (d + 1) * slots]


def positive_kernel(members, groups, slots, tokens, info, got, stats, *refs):
    rows, picked = refs[:groups], refs[groups : 2 * groups]
    joined, own, place_rows, column = refs[2 * groups :]
    place_rows[...] = own_places(members, info, got)
    for e in range(members):
        mr = info[1] ^ e
        lanes = pl.ds(pl.multiple_of(mr * tokens, LANES), tokens)
        at = pl.ds(pl.multiple_of(mr * slots, slots), slots)
        hot = slot_hot(members, groups, slots, info, place_rows, column, mr, tokens)
        row = jnp.concatenate([r[at, :] for r in rows], axis=0)
        enc = jnp.concatenate([p[at, :] for p in picked], axis=0)
        value = jnp.sum(row * enc, axis=1, keepdims=True)
        positive = jnp.sum(jnp.where(hot, value, 0.0), axis=0, keepdims=True)
        has = jnp.sum(hot.astype(F32), axis=0, keepdims=True)
        old = stats[0:1, lanes]
        top = jnp.where(has > 0, jnp.maximum(old, positive), old)
        joined[0:1, lanes] = top
        joined[1:2, lanes] = stats[1:2, lanes] * jnp.exp(old - top) + jnp.where(
            has > 0, jnp.exp(positive - top), 0.0
        )
        own[0:1, lanes] = positive
        own[1:2, lanes] = has


def pulled_kernel(members, groups, slots, blocks, info, got, *refs):
    negs, refs = refs[:groups], refs[groups:]
    rows, refs = refs[:groups], refs[groups:]
    prob_hi, prob_lo, pulled, row_t, place_rows, column = refs
    place_rows[...] = own_places(members, info, got)
    neg = jnp.concatenate([row[...] for row in negs], axis=0)
    neg_t = split(jnp.transpose(neg))
    tokens = pulled.shape[2]
    for i, e in enumerate(blocks):
        mr = info[1] ^ e
        pulled[i] = dot3(neg_t, (prob_hi[i], prob_lo[i]), NN)
        at = pl.ds(pl.multiple_of(mr * slots, slots), slots)
        hot = slot_hot(members, groups, slots, info, place_rows, column, mr, tokens)
        high, low = split(jnp.concatenate([r[at, :] for r in rows], axis=0))
        row_t[i] = dot1(high, as_bf16(hot), TN) + dot1(low, as_bf16(hot), TN)


def join(first, second):
    top = jnp.maximum(first[0:1], second[0:1])
    total = first[1:2] * jnp.exp(first[0:1] - top) + second[1:2] * jnp.exp(second[0:1] - top)
    return top, total


def join_kernel(first, second, *refs):
    out = refs[-1]
    top, total = join(first[...], second[...])
    out[0:1, :] = top
    out[1:2, :] = total


def shares(info, e, tokens, final, stats, own):
    lanes = pl.ds(pl.multiple_of((info[1] ^ e) * tokens, LANES), tokens)
    top, total = final[0:1, lanes], final[1:2, lanes]
    scale = jnp.exp(stats[0:1, lanes] - top) / total
    extra = jnp.where(
        own[1:2, lanes] > 0, jnp.exp(own[0:1, lanes] - top) / total - 1.0, 0.0
    )
    return scale, extra


def pull_kernel(halves, blocks, tokens, info, final, stats, own, *refs):
    for e, out in zip(blocks, refs[-len(blocks) :]):
        h = 0 if e in halves[0] else 1
        pulled, row_t = (ref[halves[h].index(e)] for ref in refs[2 * h : 2 * h + 2])
        scale, extra = shares(info, e, tokens, final, stats, own)
        out[...] = pulled * scale + row_t * extra


def flat(table, lane, slots):
    return jnp.concatenate(
        [table[m : m + 1, lane : lane + slots] for m in range(table.shape[0])], axis=1
    )


def grad_kernel(members, groups, slots, halves, info, got, final, stats, own, *refs):
    probs, refs = refs[: 2 * len(halves)], refs[2 * len(halves) :]
    encs = refs[:members]
    *outs, total, coef, place_rows = refs[-groups - 3 :]
    place_rows[...] = own_places(members, info, got)
    tokens, width = encs[0].shape
    for h, i, e in [(h, i, e) for h, blocks in enumerate(halves) for i, e in enumerate(blocks)]:
        mr = info[1] ^ e
        scale, extra = shares(info, e, tokens, final, stats, own)
        enc = split(encs[e][...] * row_to_col(scale))
        part = dot3((probs[2 * h][i], probs[2 * h + 1][i]), enc, NN)
        if h == 0 and i == 0:
            total[...] = part
        else:
            total[...] += part
        hot = place_rows[pl.ds(mr, 1), :] == iota((tokens, LANES), 0) + 1
        coef[pl.ds(mr, 1), :] = jnp.sum(
            jnp.where(hot, row_to_col(extra), 0.0), axis=0, keepdims=True
        )
    count = total.shape[0] // groups
    lines = [flat(coef[...], g * slots, slots) for g in range(groups)]
    for d, out in enumerate(outs):
        out[0:count, :] = total[d * count : (d + 1) * count, :]
        line = lines[0]
        for g in range(1, groups):
            line = jnp.where((info[0] ^ d) == g, lines[g], line)
        out[count:, 0 : line.shape[1]] = jnp.broadcast_to(line, (8, line.shape[1]))


def equal_in_batch(ids):
    size = ids.shape[1]
    across = jnp.broadcast_to(ids.astype(F32), (size, size))
    same = (jnp.transpose(across) == across) & (
        (iota((size, size), 0) // BATCH) == (iota((size, size), 1) // BATCH)
    )
    return same.astype(F32)


def scatter_kernel(members, groups, own, slots, count, info, got_v, got, *refs):
    size = len(own)
    grads, picked = refs[:size], refs[size : 2 * size]
    out, negs, tgts = refs[-3:]
    out[...] = refs[2 * size][...] if own[0] else jnp.zeros_like(out)

    def add_rows(asked, first, source, base, number):
        for b in range(0, number, BATCH):
            rows = [asked[first + b + k] for k in range(BATCH)]
            new = [
                out[pl.ds(rows[k], 1), :] + source[pl.ds(base + b + k, 1), :]
                for k in range(BATCH)
            ]
            for k in range(BATCH):
                out[pl.ds(rows[k], 1), :] = new[k]

    for i, d in enumerate(own):
        g = info[0] ^ d
        asked = got_v[pl.ds(g * members, members), 0, 0:LANES]
        number = members * count
        same = as_bf16(equal_in_batch(flat(asked, slots, count)) > 0)
        high, low = split(grads[i][0:number, :])
        negs[...] = dot1(same, high, NN) + dot1(same, low, NN)
        weight = equal_in_batch(flat(asked, 0, slots))
        weight = weight * grads[i][number : number + 1, 0 : members * slots]
        tgts[...] = dot3(split(weight), split(picked[i][...]), NN)
        merged = BATCH // count if count < BATCH else 1

        def member(step, carry, g=g, merged=merged):
            if merged == 1:
                add_rows(got.at[g * members + step, 0], slots, negs, step * count, count)
                add_rows(got.at[g * members + step, 0], 0, tgts, step * slots, slots)
                return carry
            first = g * members + step * merged
            rows = [
                got[first + k // count, 0, slots + k % count] for k in range(BATCH)
            ]
            new = [
                out[pl.ds(rows[k], 1), :] + negs[pl.ds(step * BATCH + k, 1), :]
                for k in range(BATCH)
            ]
            for k in range(BATCH):
                out[pl.ds(rows[k], 1), :] = new[k]
            for m in range(merged):
                add_rows(got.at[first + m, 0], 0, tgts, (step * merged + m) * slots, slots)
            return carry

        lax.fori_loop(0, members // merged, member, 0)


def add_kernel(terms, *refs):
    total = refs[0][...]
    for ref in refs[1:terms]:
        total = total + ref[...]
    refs[-1][...] = total


def finish_kernel(valid, *refs):
    total = refs[0][...]
    for ref in refs[1:-1]:
        total = total + ref[...]
    refs[-1][...] = jnp.transpose(total) * row_to_col(valid[...].astype(F32))


def swap(value, axis, d):
    return lax.ppermute(value, axis, [(i, i ^ d) for i in range(lax.axis_size(axis))])


def shards(encoded, item_table, target_owner, target_local, negative_ids, valid):
    groups, members = lax.axis_size("group"), lax.axis_size("member")
    devices = groups * members
    tokens, width = encoded.shape
    rows_dev = item_table.shape[0]
    negatives = negative_ids.shape[0]
    slots = max(2, 4 * tokens // devices)
    count = negatives // devices
    near = max(1, members // 4)
    everyone = members * tokens
    shape = jax.ShapeDtypeStruct
    sds = lambda *s: shape(s, F32)

    info = PLACE
    ints = jnp.concatenate([target_owner.reshape(-1), target_local, valid, negative_ids])
    request, masked = call(
        functools.partial(front_kernel, members, rows_dev, slots, tokens, negatives),
        [shape((devices, 1, 2 * LANES), I32), sds(tokens, width)],
        [SMEM] + [VMEM] * 2,
        [VMEM] * 2,
        (info, ints.reshape(1, -1), encoded),
        name="front",
    )
    got = lax.all_to_all(
        request, ("group", "member"), split_axis=0, concat_axis=0, tiled=True
    )

    encs = [masked] + [None] * (members - 1)
    for z in (near, 2 * near):
        encs[z] = swap(masked, "member", z)
    onward, got = lax.optimization_barrier((encs[2 * near], got))
    encs[3 * near] = swap(onward, "member", near)
    for z in (0, 2 * near):
        for x in range(1, near):
            encs[z ^ x] = swap(onward if z == 2 * near else encs[z], "member", x)
    halves = [[d for d in range(members) if (d < near) or d in (near, 2 * near)], []]
    halves[1] = [d for d in range(members) if d not in halves[0]]

    early = [encs[d] for d in halves[0] if d and d != near]

    def after(blocks, done):
        return [lax.optimization_barrier((block, done))[0] for block in blocks]

    def gather(chosen, part, many, deps, name):
        return call(
            functools.partial(gather_kernel, members, chosen, part, many),
            [sds(members * many, width)] * len(chosen),
            [SMEM, SMEM, VMEM] + [ANY] * len(deps),
            [VMEM] * len(chosen),
            (info, got, item_table, *deps),
            name=name,
        )

    negs = gather(range(groups), slots, count, early, "gather_negatives")
    for x in range(1, near):
        encs[near + x] = swap(lax.optimization_barrier((encs[x], negs[0]))[0], "member", near)
    negs = [negs[0]] + [swap(negs[d], "group", d) for d in range(1, groups)]
    waited = [encs[near], *encs[2 * near + 1 : 3 * near]]
    rows = gather(range(2, groups), 0, slots, waited, "gather_far_targets")
    gathered = rows
    for x in range(1, near):
        encs[3 * near + x] = swap(after([encs[3 * near]], rows[0])[0], "member", x)
    rows = [swap(row, "group", d) for d, row in enumerate(rows, 2)]

    stats, probs = [], []
    for blocks in halves:
        many = len(blocks)
        *stats, hi, lo = call(
            functools.partial(score_kernel, blocks, groups, bool(stats)),
            [sds(2, everyone)] + [shape((many, negatives, tokens), BF16)] * 2,
            [SMEM] + [VMEM] * (groups + many + len(stats)) + [ANY] * len(gathered),
            [VMEM] * 3,
            (info, *negs, *[encs[e] for e in blocks], *stats, *gathered),
            flops=12 * many * tokens * negatives * width,
            moved=MIB,
            name="score",
        )
        probs += [hi, lo]
        if gathered:
            gathered = []
            kept, row = gather(range(2), 0, slots, stats, "gather_targets")
            rows = [kept, swap(row, "group", 1), *rows]
    stats = stats[0]
    picked = call(
        functools.partial(pick_kernel, members, groups, slots),
        [sds(members * slots, width)] * groups,
        [SMEM] + [VMEM] * (1 + members),
        [VMEM] * groups,
        (info, got, *encs),
        scratch=[pltpu.VMEM((members, LANES), I32), pltpu.VMEM((LANES, 1), I32)],
        name="pick",
    )
    sent = list(picked[:1]) + [
        swap(b, "group", d) for d, b in enumerate(after(picked[1:], stats), 1)
    ]
    joined, own = call(
        functools.partial(positive_kernel, members, groups, slots, tokens),
        [sds(2, everyone)] * 2,
        [SMEM] + [VMEM] * (2 + 2 * groups),
        [VMEM] * 2,
        (info, got, stats, *rows, *picked),
        scratch=[pltpu.VMEM((members, LANES), I32), pltpu.VMEM((LANES, 1), I32)],
        name="positive",
    )
    pulled = []
    for h, blocks in enumerate(halves):
        pulled += call(
            functools.partial(pulled_kernel, members, groups, slots, blocks),
            [sds(len(blocks), width, tokens)] * 2,
            [SMEM] + [VMEM] * (3 + 2 * groups),
            [VMEM] * 2,
            (info, got, *negs, *rows, *probs[2 * h : 2 * h + 2]),
            scratch=[pltpu.VMEM((members, LANES), I32), pltpu.VMEM((LANES, 1), I32)],
            flops=6 * len(blocks) * tokens * negatives * width,
            moved=MIB,
            name="pulled",
        )

    final = joined
    d, hops = 1, 0
    while d < members:
        late = pulled[2 * hops : 2 * hops + 2]
        hops += 1
        final = call(
            join_kernel,
            sds(2, everyone),
            [VMEM] * 2 + [ANY] * len(late),
            VMEM,
            (final, swap(final, "member", d), *late),
            name="join",
        )
        d *= 2

    grads = call(
        functools.partial(grad_kernel, members, groups, slots, halves),
        [sds(members * count + 8, width)] * groups,
        [SMEM] + [VMEM] * (4 + len(probs) + members) + [ANY] * (groups - 1),
        [VMEM] * groups,
        (info, got, final, stats, own, *probs, *encs, *sent[1:]),
        scratch=[
            pltpu.VMEM((negatives, width), F32),
            pltpu.VMEM((members, LANES), F32),
            pltpu.VMEM((members, LANES), I32),
        ],
        flops=6 * everyone * negatives * width,
        moved=8 * MIB,
        name="grad",
    )
    def added(terms, deps, flops=0):
        return call(
            functools.partial(add_kernel, len(terms)),
            sds(width, tokens),
            [VMEM] * len(terms) + [ANY] * len(deps),
            VMEM,
            (*terms, *deps),
            flops=flops,
            name="add",
        )

    graded = [grads[0]]
    grads = graded + [swap(grads[d], "group", d) for d in range(1, groups)]
    def scaled(blocks, deps):
        return call(
            functools.partial(pull_kernel, halves, blocks, tokens),
            [sds(width, tokens)] * len(blocks),
            [SMEM] + [VMEM] * 7 + [ANY] * len(deps),
            [VMEM] * len(blocks),
            (info, final, stats, own, *pulled, *deps),
            name="pull",
        )

    def beside(blocks):
        return [swap(block, "member", x) for x, block in enumerate(blocks, 1)]

    along = list(range(near))
    def scatter(own, base, deps, flops):
        return call(
            functools.partial(scatter_kernel, members, groups, own, slots, count),
            sds(rows_dev, width),
            [SMEM, VMEM, SMEM] + [VMEM] * (2 * len(own) + len(base)) + [ANY] * len(deps),
            VMEM,
            (info, got, got, *[grads[d] for d in own], *[sent[d] for d in own], *base, *deps),
            scratch=[
                pltpu.VMEM((members * count, width), F32),
                pltpu.VMEM((members * slots, width), F32),
            ],
            flops=flops,
            name="scatter",
        )

    farthest, *rest = scaled([*[3 * near + x for x in along], *[near + x for x in along[1:]]], [])
    rest, diagonal = rest[: near - 1], rest[near - 1 :]
    arrived = beside(rest)
    diagonal = [swap(block, "member", near) for block in diagonal]
    near_blocks = [near, *along[1:]]
    kept, far, *others = scaled(
        [0, *[2 * near + x for x in along], *near_blocks], graded
    )
    others, sends = others[: near - 1], others[near - 1 :]
    total = added([farthest, *arrived], [*graded, *diagonal])
    sums = [added([sends[x], diagonal[x - 1]], []) for x in along[1:]]
    others = after(others, total)
    table_own = scatter(list(range(2)), [], [total], 1 << 33)
    far = added([far], [table_own, *grads[2:]])
    others = beside(others)
    half = added([far, swap(total, "member", near), *others], [])
    held = after(sends[:1], others[0]) + after(sums, half)
    parts = [swap(b, "member", d) for d, b in zip(near_blocks, held)]
    parts.append(added([kept, swap(half, "member", 2 * near)], []))

    table_grad = scatter(list(range(2, groups)), [table_own], [], 0)
    encoded_grad = call(
        finish_kernel,
        sds(tokens, width),
        [VMEM] * (1 + len(parts)),
        VMEM,
        (valid.reshape(1, -1), *parts),
        name="finish",
    )
    return (encoded_grad, table_grad)


def solution(mesh):
    placed = (
        P(("group", "member"), None),
        P(("group", "member"), None),
        P(("group", "member"), None),
        P(("group", "member")),
        P(("group", "member")),
        P(("group", "member")),
    )
    return jax.shard_map(
        shards,
        mesh=mesh,
        in_specs=placed,
        out_specs=(P(("group", "member"), None), P(("group", "member"), None)),
        check_vma=False,
    )
```

```python
import functools

import jax
import jax.numpy as jnp
from jax import lax
from jax.experimental import pallas as pl
from jax.experimental.pallas import tpu as pltpu
from jax.sharding import PartitionSpec as P

F32 = jnp.float32
BF16 = jnp.bfloat16
I32 = jnp.int32
LANES = 128
VMEM = pl.BlockSpec(memory_space=pltpu.VMEM)
ANY = pl.BlockSpec(memory_space=pl.ANY)
SMEM = pl.BlockSpec(memory_space=pltpu.SMEM)
MIB = 1 << 20
BATCH = 8

NN = (((1,), (0,)), ((), ()))
NT = (((1,), (1,)), ((), ()))
TN = (((0,), (0,)), ((), ()))


PLACE = object()


def located(kernel):
    def run(*refs):
        kernel((lax.axis_index("group"), lax.axis_index("member")), *refs)

    return run


def call(kernel, out_shape, ins, outs, args, scratch=(), limit=10, flops=0, moved=0, name=None):
    if args[0] is PLACE:
        kernel, ins, args = located(kernel), ins[1:], args[1:]
    return pl.pallas_call(
        kernel,
        out_shape=out_shape,
        in_specs=ins,
        out_specs=outs,
        scratch_shapes=list(scratch),
        compiler_params=pltpu.CompilerParams(vmem_limit_bytes=limit * MIB),
        cost_estimate=pl.CostEstimate(flops=flops, bytes_accessed=moved, transcendentals=0),
        name=name,
    )(*args)


def iota(shape, dim):
    return lax.broadcasted_iota(I32, shape, dim)


def as_bf16(flag):
    return flag.astype(F32).astype(BF16)


def dot1(a, b, dims):
    return lax.dot_general(a, b, dims, preferred_element_type=F32)


def split(x):
    hi = x.astype(BF16)
    return hi, (x - hi.astype(F32)).astype(BF16)


def dot3(a, b, dims):
    return dot1(a[0], b[0], dims) + (dot1(a[0], b[1], dims) + dot1(a[1], b[0], dims))


def row_to_col(row):
    return jnp.transpose(jnp.broadcast_to(row, (LANES, row.shape[1])))[:, 0:1]


def split3(x):
    hi = x.astype(BF16)
    rest = x - hi.astype(F32)
    mid = rest.astype(BF16)
    return hi, mid, (rest - mid.astype(F32)).astype(BF16)


def dot6(a, b, dims):
    small = dot1(a[2], b[0], dims) + dot1(a[1], b[1], dims) + dot1(a[0], b[2], dims)
    return (small + (dot1(a[1], b[0], dims) + dot1(a[0], b[1], dims))) + dot1(a[0], b[0], dims)


def copy_rows(source, row_of, target, base, count):
    for b in range(0, count, BATCH):
        rows = [source[pl.ds(row_of(b + k), 1), :] for k in range(BATCH)] if count % BATCH == 0 else None
        if rows is None:
            for k in range(count):
                target[pl.ds(base + k, 1), :] = source[pl.ds(row_of(k), 1), :]
            return
        target[pl.ds(pl.multiple_of(base + b, BATCH), BATCH), :] = jnp.concatenate(rows, axis=0)


def front_kernel(members, rows_dev, slots, tokens, negatives, info, ints, enc_ref, out_ref, masked_ref):
    devices = out_ref.shape[0]
    shift = rows_dev.bit_length() - 1
    owner = ints[:, 0:tokens]
    local = ints[:, tokens : 2 * tokens]
    valid = ints[:, 2 * tokens : 3 * tokens]
    ids = ints[:, 3 * tokens :]
    masked_ref[...] = enc_ref[...] * row_to_col(valid.astype(F32))

    def ranks(owner_row, count):
        hot = iota((devices, count), 0) == owner_row
        before = as_bf16(iota((count, count), 0) < iota((count, count), 1))
        seen = dot1(as_bf16(hot), before, NN)
        return hot, jnp.sum(jnp.where(hot, seen, 0.0), axis=0, keepdims=True).astype(I32)

    def table(hot, value, place):
        return dot1(jnp.where(hot, value, 0.0).astype(BF16), place, NT)

    def placed(lane_row, count):
        return as_bf16(iota((LANES, count), 0) == lane_row)

    hot, rank = ranks(owner, tokens)
    place = placed(rank, tokens)
    high = table(hot, (local >> 6).astype(F32), place)
    low = table(hot, (local & 63).astype(F32), place)
    group = owner >> (members.bit_length() - 1)
    hot_member = (iota((devices, tokens), 0) & (members - 1)) == (owner & (members - 1))
    position = table(
        hot_member, (iota((1, tokens), 1) + 1).astype(F32), placed(group * slots + rank, tokens)
    )

    hot, rank = ranks(ids >> shift, negatives)
    place = placed(rank + slots, negatives)
    local = ids & (rows_dev - 1)
    high = high + table(hot, (local >> 6).astype(F32), place)
    low = low + table(hot, (local & 63).astype(F32), place)
    out_ref[:, 0, 0:LANES] = high.astype(I32) * 64 + low.astype(I32)
    out_ref[:, 0, LANES : 2 * LANES] = position.astype(I32)


def gather_kernel(members, chosen, part, count, info, got, table, *refs):
    for d, out in zip(chosen, refs[-len(chosen) :]):
        first = (info[0] ^ d) * members

        def member(mr, carry, out=out, first=first):
            asked = got.at[first + mr, 0]
            copy_rows(table, lambda k: asked[part + k], out, mr * count, count)
            return carry

        lax.fori_loop(0, members, member, 0)


def score_kernel(blocks, groups, follows, info, *refs):
    rows, refs = refs[:groups], refs[groups:]
    encs, refs = refs[: len(blocks)], refs[len(blocks) :]
    stats, prob_hi, prob_lo = refs[-3:]
    if follows:
        stats[...] = refs[0][...]
    tokens = encs[0].shape[0]
    neg = split3(jnp.concatenate([row[...] for row in rows], axis=0))
    for i, e in enumerate(blocks):
        lanes = pl.ds(pl.multiple_of((info[1] ^ e) * tokens, LANES), tokens)
        score = dot6(neg, split3(encs[i][...]), NT)
        top = jnp.max(score, axis=0, keepdims=True)
        prob = jnp.exp(score - top)
        stats[0:1, lanes] = top
        stats[1:2, lanes] = jnp.sum(prob, axis=0, keepdims=True)
        parts = split(prob)
        prob_hi[i] = parts[0]
        prob_lo[i] = parts[1]


def own_places(members, info, got):
    return got[pl.ds(info[0] * members, members), 0, LANES : 2 * LANES]


def slot_hot(members, groups, slots, info, place_rows, column, mr, tokens):
    column[...] = row_to_col(place_rows[pl.ds(mr, 1), :])
    place = [
        column[pl.ds(pl.multiple_of((info[0] ^ d) * slots, slots), slots), :]
        for d in range(groups)
    ]
    return jnp.concatenate(place, axis=0) == iota((groups * slots, tokens), 1) + 1


def pick_kernel(members, groups, slots, info, got, *refs):
    encs = refs[:members]
    outs = refs[members : members + groups]
    place_rows, column = refs[members + groups :]
    place_rows[...] = own_places(members, info, got)
    for e in range(members):
        mr = info[1] ^ e
        tokens = encs[e].shape[0]
        hot = as_bf16(slot_hot(members, groups, slots, info, place_rows, column, mr, tokens))
        hi, mid, low = split3(encs[e][...])
        found = (dot1(hot, hi, NN) + dot1(hot, mid, NN)) + dot1(hot, low, NN)
        at = pl.ds(pl.multiple_of(mr * slots, slots), slots)
        for d in range(groups):
            outs[d][at, :] = found[d * slots : (d + 1) * slots]


def positive_kernel(members, groups, slots, tokens, info, got, stats, *refs):
    rows, picked = refs[:groups], refs[groups : 2 * groups]
    joined, own, place_rows, column = refs[2 * groups :]
    place_rows[...] = own_places(members, info, got)
    for e in range(members):
        mr = info[1] ^ e
        lanes = pl.ds(pl.multiple_of(mr * tokens, LANES), tokens)
        at = pl.ds(pl.multiple_of(mr * slots, slots), slots)
        hot = slot_hot(members, groups, slots, info, place_rows, column, mr, tokens)
        row = jnp.concatenate([r[at, :] for r in rows], axis=0)
        enc = jnp.concatenate([p[at, :] for p in picked], axis=0)
        value = jnp.sum(row * enc, axis=1, keepdims=True)
        positive = jnp.sum(jnp.where(hot, value, 0.0), axis=0, keepdims=True)
        has = jnp.sum(hot.astype(F32), axis=0, keepdims=True)
        old = stats[0:1, lanes]
        top = jnp.where(has > 0, jnp.maximum(old, positive), old)
        joined[0:1, lanes] = top
        joined[1:2, lanes] = stats[1:2, lanes] * jnp.exp(old - top) + jnp.where(
            has > 0, jnp.exp(positive - top), 0.0
        )
        own[0:1, lanes] = positive
        own[1:2, lanes] = has


def pulled_kernel(members, groups, slots, blocks, info, got, *refs):
    negs, refs = refs[:groups], refs[groups:]
    rows, refs = refs[:groups], refs[groups:]
    prob_hi, prob_lo, pulled, row_t, place_rows, column = refs
    place_rows[...] = own_places(members, info, got)
    neg = jnp.concatenate([row[...] for row in negs], axis=0)
    neg_t = split(jnp.transpose(neg))
    tokens = pulled.shape[2]
    for i, e in enumerate(blocks):
        mr = info[1] ^ e
        pulled[i] = dot3(neg_t, (prob_hi[i], prob_lo[i]), NN)
        at = pl.ds(pl.multiple_of(mr * slots, slots), slots)
        hot = slot_hot(members, groups, slots, info, place_rows, column, mr, tokens)
        high, low = split(jnp.concatenate([r[at, :] for r in rows], axis=0))
        row_t[i] = dot1(high, as_bf16(hot), TN) + dot1(low, as_bf16(hot), TN)


def join(first, second):
    top = jnp.maximum(first[0:1], second[0:1])
    total = first[1:2] * jnp.exp(first[0:1] - top) + second[1:2] * jnp.exp(second[0:1] - top)
    return top, total


def join_kernel(first, second, *refs):
    out = refs[-1]
    top, total = join(first[...], second[...])
    out[0:1, :] = top
    out[1:2, :] = total


def shares(info, e, tokens, final, stats, own):
    lanes = pl.ds(pl.multiple_of((info[1] ^ e) * tokens, LANES), tokens)
    top, total = final[0:1, lanes], final[1:2, lanes]
    scale = jnp.exp(stats[0:1, lanes] - top) / total
    extra = jnp.where(
        own[1:2, lanes] > 0, jnp.exp(own[0:1, lanes] - top) / total - 1.0, 0.0
    )
    return scale, extra


def pull_kernel(halves, blocks, tokens, info, final, stats, own, *refs):
    for e, out in zip(blocks, refs[-len(blocks) :]):
        h = 0 if e in halves[0] else 1
        pulled, row_t = (ref[halves[h].index(e)] for ref in refs[2 * h : 2 * h + 2])
        scale, extra = shares(info, e, tokens, final, stats, own)
        out[...] = pulled * scale + row_t * extra


def flat(table, lane, slots):
    return jnp.concatenate(
        [table[m : m + 1, lane : lane + slots] for m in range(table.shape[0])], axis=1
    )


def grad_kernel(members, groups, slots, halves, info, got, final, stats, own, *refs):
    probs, refs = refs[: 2 * len(halves)], refs[2 * len(halves) :]
    encs = refs[:members]
    *outs, total, coef, place_rows = refs[-groups - 3 :]
    place_rows[...] = own_places(members, info, got)
    tokens, width = encs[0].shape
    for h, i, e in [(h, i, e) for h, blocks in enumerate(halves) for i, e in enumerate(blocks)]:
        mr = info[1] ^ e
        scale, extra = shares(info, e, tokens, final, stats, own)
        enc = split(encs[e][...] * row_to_col(scale))
        part = dot3((probs[2 * h][i], probs[2 * h + 1][i]), enc, NN)
        if h == 0 and i == 0:
            total[...] = part
        else:
            total[...] += part
        hot = place_rows[pl.ds(mr, 1), :] == iota((tokens, LANES), 0) + 1
        coef[pl.ds(mr, 1), :] = jnp.sum(
            jnp.where(hot, row_to_col(extra), 0.0), axis=0, keepdims=True
        )
    count = total.shape[0] // groups
    lines = [flat(coef[...], g * slots, slots) for g in range(groups)]
    for d, out in enumerate(outs):
        out[0:count, :] = total[d * count : (d + 1) * count, :]
        line = lines[0]
        for g in range(1, groups):
            line = jnp.where((info[0] ^ d) == g, lines[g], line)
        out[count:, 0 : line.shape[1]] = jnp.broadcast_to(line, (8, line.shape[1]))


def equal_in_batch(ids):
    size = ids.shape[1]
    across = jnp.broadcast_to(ids.astype(F32), (size, size))
    same = (jnp.transpose(across) == across) & (
        (iota((size, size), 0) // BATCH) == (iota((size, size), 1) // BATCH)
    )
    return same.astype(F32)


def scatter_kernel(members, groups, own, slots, count, info, got_v, requests, *refs):
    size = len(own)
    grads, picked = refs[:size], refs[size : 2 * size]
    out, negs, tgts, got, arrived = refs[-5:]
    copy = pltpu.make_async_copy(requests, got, arrived)
    copy.start()
    out[...] = refs[2 * size][...] if own[0] else jnp.zeros_like(out)

    def add_rows(asked, first, source, base, number):
        for b in range(0, number, BATCH):
            rows = [asked[first + b + k] for k in range(BATCH)]
            new = [
                out[pl.ds(rows[k], 1), :] + source[pl.ds(base + b + k, 1), :]
                for k in range(BATCH)
            ]
            for k in range(BATCH):
                out[pl.ds(rows[k], 1), :] = new[k]

    copy.wait()
    for i, d in enumerate(own):
        g = info[0] ^ d
        asked = got_v[pl.ds(g * members, members), 0, 0:LANES]
        number = members * count
        same = as_bf16(equal_in_batch(flat(asked, slots, count)) > 0)
        high, low = split(grads[i][0:number, :])
        negs[...] = dot1(same, high, NN) + dot1(same, low, NN)
        weight = equal_in_batch(flat(asked, 0, slots))
        weight = weight * grads[i][number : number + 1, 0 : members * slots]
        tgts[...] = dot3(split(weight), split(picked[i][...]), NN)
        merged = BATCH // count if count < BATCH else 1

        def member(step, carry, g=g, merged=merged):
            if merged == 1:
                add_rows(got.at[g * members + step, 0], slots, negs, step * count, count)
                add_rows(got.at[g * members + step, 0], 0, tgts, step * slots, slots)
                return carry
            first = g * members + step * merged
            rows = [
                got[first + k // count, 0, slots + k % count] for k in range(BATCH)
            ]
            new = [
                out[pl.ds(rows[k], 1), :] + negs[pl.ds(step * BATCH + k, 1), :]
                for k in range(BATCH)
            ]
            for k in range(BATCH):
                out[pl.ds(rows[k], 1), :] = new[k]
            for m in range(merged):
                add_rows(got.at[first + m, 0], 0, tgts, (step * merged + m) * slots, slots)
            return carry

        lax.fori_loop(0, members // merged, member, 0)


def add_kernel(terms, *refs):
    total = refs[0][...]
    for ref in refs[1:terms]:
        total = total + ref[...]
    refs[-1][...] = total


def finish_kernel(valid, *refs):
    total = refs[0][...]
    for ref in refs[1:-1]:
        total = total + ref[...]
    refs[-1][...] = jnp.transpose(total) * row_to_col(valid[...].astype(F32))


def swap(value, axis, d):
    return lax.ppermute(value, axis, [(i, i ^ d) for i in range(lax.axis_size(axis))])


def shards(encoded, item_table, target_owner, target_local, negative_ids, valid):
    groups, members = lax.axis_size("group"), lax.axis_size("member")
    devices = groups * members
    tokens, width = encoded.shape
    rows_dev = item_table.shape[0]
    negatives = negative_ids.shape[0]
    slots = max(2, 4 * tokens // devices)
    count = negatives // devices
    near = max(1, members // 4)
    everyone = members * tokens
    shape = jax.ShapeDtypeStruct
    sds = lambda *s: shape(s, F32)

    info = PLACE
    ints = jnp.concatenate([target_owner.reshape(-1), target_local, valid, negative_ids])
    request, masked = call(
        functools.partial(front_kernel, members, rows_dev, slots, tokens, negatives),
        [shape((devices, 1, 2 * LANES), I32), sds(tokens, width)],
        [SMEM] + [VMEM] * 2,
        [VMEM] * 2,
        (info, ints.reshape(1, -1), encoded),
        name="front",
    )
    got = lax.all_to_all(
        request, ("group", "member"), split_axis=0, concat_axis=0, tiled=True
    )

    encs = [masked] + [None] * (members - 1)
    for z in (near, 2 * near):
        encs[z] = swap(masked, "member", z)
    onward, got = lax.optimization_barrier((encs[2 * near], got))
    encs[3 * near] = swap(onward, "member", near)
    for z in (0, 2 * near):
        for x in range(1, near):
            encs[z ^ x] = swap(onward if z == 2 * near else encs[z], "member", x)
    halves = [[d for d in range(members) if (d < near) or d in (near, 2 * near)], []]
    halves[1] = [d for d in range(members) if d not in halves[0]]

    early = [encs[d] for d in halves[0] if d and d != near]

    def after(blocks, done):
        return [lax.optimization_barrier((block, done))[0] for block in blocks]

    def gather(chosen, part, many, deps, name):
        return call(
            functools.partial(gather_kernel, members, chosen, part, many),
            [sds(members * many, width)] * len(chosen),
            [SMEM, SMEM, VMEM] + [ANY] * len(deps),
            [VMEM] * len(chosen),
            (info, got, item_table, *deps),
            name=name,
        )

    negs = gather(range(groups), slots, count, early, "gather_negatives")
    for x in range(1, near):
        encs[near + x] = swap(lax.optimization_barrier((encs[x], negs[0]))[0], "member", near)
    negs = [negs[0]] + [swap(negs[d], "group", d) for d in range(1, groups)]
    waited = [encs[near], *encs[2 * near + 1 : 3 * near]]
    rows = gather(range(2, groups), 0, slots, waited, "gather_far_targets")
    gathered = rows
    for x in range(1, near):
        encs[3 * near + x] = swap(after([encs[3 * near]], rows[0])[0], "member", x)
    rows = [swap(row, "group", d) for d, row in enumerate(rows, 2)]

    stats, probs = [], []
    for blocks in halves:
        many = len(blocks)
        *stats, hi, lo = call(
            functools.partial(score_kernel, blocks, groups, bool(stats)),
            [sds(2, everyone)] + [shape((many, negatives, tokens), BF16)] * 2,
            [SMEM] + [VMEM] * (groups + many + len(stats)) + [ANY] * len(gathered),
            [VMEM] * 3,
            (info, *negs, *[encs[e] for e in blocks], *stats, *gathered),
            flops=12 * many * tokens * negatives * width,
            moved=MIB,
            name="score",
        )
        probs += [hi, lo]
        if gathered:
            gathered = []
            kept, row = gather(range(2), 0, slots, stats, "gather_targets")
            rows = [kept, swap(row, "group", 1), *rows]
    stats = stats[0]
    picked = call(
        functools.partial(pick_kernel, members, groups, slots),
        [sds(members * slots, width)] * groups,
        [SMEM] + [VMEM] * (1 + members),
        [VMEM] * groups,
        (info, got, *encs),
        scratch=[pltpu.VMEM((members, LANES), I32), pltpu.VMEM((LANES, 1), I32)],
        name="pick",
    )
    sent = list(picked[:1]) + [
        swap(b, "group", d) for d, b in enumerate(after(picked[1:], stats), 1)
    ]
    joined, own = call(
        functools.partial(positive_kernel, members, groups, slots, tokens),
        [sds(2, everyone)] * 2,
        [SMEM] + [VMEM] * (2 + 2 * groups),
        [VMEM] * 2,
        (info, got, stats, *rows, *picked),
        scratch=[pltpu.VMEM((members, LANES), I32), pltpu.VMEM((LANES, 1), I32)],
        name="positive",
    )
    pulled = []
    for h, blocks in enumerate(halves):
        pulled += call(
            functools.partial(pulled_kernel, members, groups, slots, blocks),
            [sds(len(blocks), width, tokens)] * 2,
            [SMEM] + [VMEM] * (3 + 2 * groups),
            [VMEM] * 2,
            (info, got, *negs, *rows, *probs[2 * h : 2 * h + 2]),
            scratch=[pltpu.VMEM((members, LANES), I32), pltpu.VMEM((LANES, 1), I32)],
            flops=6 * len(blocks) * tokens * negatives * width,
            moved=MIB,
            name="pulled",
        )

    final = joined
    d, hops = 1, 0
    while d < members:
        late = pulled[2 * hops : 2 * hops + 2]
        hops += 1
        final = call(
            join_kernel,
            sds(2, everyone),
            [VMEM] * 2 + [ANY] * len(late),
            VMEM,
            (final, swap(final, "member", d), *late),
            name="join",
        )
        d *= 2

    grads = call(
        functools.partial(grad_kernel, members, groups, slots, halves),
        [sds(members * count + 8, width)] * groups,
        [SMEM] + [VMEM] * (4 + len(probs) + members) + [ANY] * (groups - 1),
        [VMEM] * groups,
        (info, got, final, stats, own, *probs, *encs, *sent[1:]),
        scratch=[
            pltpu.VMEM((negatives, width), F32),
            pltpu.VMEM((members, LANES), F32),
            pltpu.VMEM((members, LANES), I32),
        ],
        flops=6 * everyone * negatives * width,
        moved=8 * MIB,
        name="grad",
    )
    def added(terms, deps, flops=0):
        return call(
            functools.partial(add_kernel, len(terms)),
            sds(width, tokens),
            [VMEM] * len(terms) + [ANY] * len(deps),
            VMEM,
            (*terms, *deps),
            flops=flops,
            name="add",
        )

    graded = [grads[0]]
    grads = graded + [swap(grads[d], "group", d) for d in range(1, groups)]
    def scaled(blocks, deps):
        return call(
            functools.partial(pull_kernel, halves, blocks, tokens),
            [sds(width, tokens)] * len(blocks),
            [SMEM] + [VMEM] * 7 + [ANY] * len(deps),
            [VMEM] * len(blocks),
            (info, final, stats, own, *pulled, *deps),
            name="pull",
        )

    def beside(blocks):
        return [swap(block, "member", x) for x, block in enumerate(blocks, 1)]

    along = list(range(near))
    def scatter(own, base, deps, flops):
        return call(
            functools.partial(scatter_kernel, members, groups, own, slots, count),
            sds(rows_dev, width),
            [SMEM, VMEM, ANY] + [VMEM] * (2 * len(own) + len(base)) + [ANY] * len(deps),
            VMEM,
            (info, got, got, *[grads[d] for d in own], *[sent[d] for d in own], *base, *deps),
            scratch=[
                pltpu.VMEM((members * count, width), F32),
                pltpu.VMEM((members * slots, width), F32),
                pltpu.SMEM(got.shape, I32),
                pltpu.SemaphoreType.DMA,
            ],
            flops=flops,
            name="scatter",
        )

    farthest, *rest = scaled([*[3 * near + x for x in along], *[near + x for x in along[1:]]], [])
    rest, diagonal = rest[: near - 1], rest[near - 1 :]
    arrived = beside(rest)
    diagonal = [swap(block, "member", near) for block in diagonal]
    near_blocks = [near, *along[1:]]
    kept, far, *others = scaled(
        [0, *[2 * near + x for x in along], *near_blocks], graded
    )
    others, sends = others[: near - 1], others[near - 1 :]
    total = added([farthest, *arrived], [*graded, *diagonal])
    sums = [added([sends[x], diagonal[x - 1]], []) for x in along[1:]]
    others = after(others, total)
    table_own = scatter(list(range(2)), [], [total], 1 << 33)
    far = added([far], [table_own, *grads[2:]])
    others = beside(others)
    half = added([far, swap(total, "member", near), *others], [])
    held = after(sends[:1], others[0]) + after(sums, half)
    parts = [swap(b, "member", d) for d, b in zip(near_blocks, held)]
    parts.append(added([kept, swap(half, "member", 2 * near)], []))

    table_grad = scatter(list(range(2, groups)), [table_own], [], 0)
    encoded_grad = call(
        finish_kernel,
        sds(tokens, width),
        [VMEM] * (1 + len(parts)),
        VMEM,
        (valid.reshape(1, -1), *parts),
        name="finish",
    )
    return (encoded_grad, table_grad)


def solution(mesh):
    placed = (
        P(("group", "member"), None),
        P(("group", "member"), None),
        P(("group", "member"), None),
        P(("group", "member")),
        P(("group", "member")),
        P(("group", "member")),
    )
    return jax.shard_map(
        shards,
        mesh=mesh,
        in_specs=placed,
        out_specs=(P(("group", "member"), None), P(("group", "member"), None)),
        check_vma=False,
    )
```

```python
import functools

import jax
import jax.numpy as jnp
from jax import lax
from jax.experimental import pallas as pl
from jax.experimental.pallas import tpu as pltpu
from jax.sharding import PartitionSpec as P

F32 = jnp.float32
BF16 = jnp.bfloat16
I32 = jnp.int32
LANES = 128
VMEM = pl.BlockSpec(memory_space=pltpu.VMEM)
ANY = pl.BlockSpec(memory_space=pl.ANY)
SMEM = pl.BlockSpec(memory_space=pltpu.SMEM)
MIB = 1 << 20
BATCH = 8

NN = (((1,), (0,)), ((), ()))
NT = (((1,), (1,)), ((), ()))
TN = (((0,), (0,)), ((), ()))


PLACE = object()


def located(kernel):
    def run(*refs):
        kernel((lax.axis_index("group"), lax.axis_index("member")), *refs)

    return run


def call(kernel, out_shape, ins, outs, args, scratch=(), limit=10, flops=0, moved=0, name=None):
    if args[0] is PLACE:
        kernel, ins, args = located(kernel), ins[1:], args[1:]
    return pl.pallas_call(
        kernel,
        out_shape=out_shape,
        in_specs=ins,
        out_specs=outs,
        scratch_shapes=list(scratch),
        compiler_params=pltpu.CompilerParams(vmem_limit_bytes=limit * MIB),
        cost_estimate=pl.CostEstimate(flops=flops, bytes_accessed=moved, transcendentals=0),
        name=name,
    )(*args)


def iota(shape, dim):
    return lax.broadcasted_iota(I32, shape, dim)


def as_bf16(flag):
    return flag.astype(F32).astype(BF16)


def dot1(a, b, dims):
    return lax.dot_general(a, b, dims, preferred_element_type=F32)


def split(x):
    hi = x.astype(BF16)
    return hi, (x - hi.astype(F32)).astype(BF16)


def dot3(a, b, dims):
    return dot1(a[0], b[0], dims) + (dot1(a[0], b[1], dims) + dot1(a[1], b[0], dims))


def row_to_col(row):
    return jnp.transpose(jnp.broadcast_to(row, (LANES, row.shape[1])))[:, 0:1]


def split3(x):
    hi = x.astype(BF16)
    rest = x - hi.astype(F32)
    mid = rest.astype(BF16)
    return hi, mid, (rest - mid.astype(F32)).astype(BF16)


def dot6(a, b, dims):
    small = dot1(a[2], b[0], dims) + dot1(a[1], b[1], dims) + dot1(a[0], b[2], dims)
    return (small + (dot1(a[1], b[0], dims) + dot1(a[0], b[1], dims))) + dot1(a[0], b[0], dims)


def copy_rows(source, row_of, target, base, count):
    for b in range(0, count, BATCH):
        rows = [source[pl.ds(row_of(b + k), 1), :] for k in range(BATCH)] if count % BATCH == 0 else None
        if rows is None:
            for k in range(count):
                target[pl.ds(base + k, 1), :] = source[pl.ds(row_of(k), 1), :]
            return
        target[pl.ds(pl.multiple_of(base + b, BATCH), BATCH), :] = jnp.concatenate(rows, axis=0)


def front_kernel(members, rows_dev, slots, tokens, negatives, info, ints, enc_ref, out_ref, masked_ref):
    devices = out_ref.shape[0]
    shift = rows_dev.bit_length() - 1
    owner = ints[:, 0:tokens]
    local = ints[:, tokens : 2 * tokens]
    valid = ints[:, 2 * tokens : 3 * tokens]
    ids = ints[:, 3 * tokens :]
    masked_ref[...] = enc_ref[...] * row_to_col(valid.astype(F32))

    def ranks(owner_row, count):
        hot = iota((devices, count), 0) == owner_row
        before = as_bf16(iota((count, count), 0) < iota((count, count), 1))
        seen = dot1(as_bf16(hot), before, NN)
        return hot, jnp.sum(jnp.where(hot, seen, 0.0), axis=0, keepdims=True).astype(I32)

    def table(hot, value, place):
        return dot1(jnp.where(hot, value, 0.0).astype(BF16), place, NT)

    def placed(lane_row, count):
        return as_bf16(iota((LANES, count), 0) == lane_row)

    hot, rank = ranks(owner, tokens)
    place = placed(rank, tokens)
    high = table(hot, (local >> 6).astype(F32), place)
    low = table(hot, (local & 63).astype(F32), place)
    group = owner >> (members.bit_length() - 1)
    hot_member = (iota((devices, tokens), 0) & (members - 1)) == (owner & (members - 1))
    position = table(
        hot_member, (iota((1, tokens), 1) + 1).astype(F32), placed(group * slots + rank, tokens)
    )

    hot, rank = ranks(ids >> shift, negatives)
    place = placed(rank + slots, negatives)
    local = ids & (rows_dev - 1)
    high = high + table(hot, (local >> 6).astype(F32), place)
    low = low + table(hot, (local & 63).astype(F32), place)
    out_ref[:, 0, 0:LANES] = high.astype(I32) * 64 + low.astype(I32)
    out_ref[:, 0, LANES : 2 * LANES] = position.astype(I32)


def gather_kernel(members, chosen, part, count, info, got, table, *refs):
    for d, out in zip(chosen, refs[-len(chosen) :]):
        first = (info[0] ^ d) * members

        def member(mr, carry, out=out, first=first):
            asked = got.at[first + mr, 0]
            copy_rows(table, lambda k: asked[part + k], out, mr * count, count)
            return carry

        lax.fori_loop(0, members, member, 0)


def score_kernel(blocks, groups, follows, info, *refs):
    rows, refs = refs[:groups], refs[groups:]
    encs, refs = refs[: len(blocks)], refs[len(blocks) :]
    stats, prob_hi, prob_lo = refs[-3:]
    if follows:
        stats[...] = refs[0][...]
    tokens = encs[0].shape[0]
    neg = split3(jnp.concatenate([row[...] for row in rows], axis=0))
    for i, e in enumerate(blocks):
        lanes = pl.ds(pl.multiple_of((info[1] ^ e) * tokens, LANES), tokens)
        score = dot6(neg, split3(encs[i][...]), NT)
        top = jnp.max(score, axis=0, keepdims=True)
        prob = jnp.exp(score - top)
        stats[0:1, lanes] = top
        stats[1:2, lanes] = jnp.sum(prob, axis=0, keepdims=True)
        parts = split(prob)
        prob_hi[i] = parts[0]
        prob_lo[i] = parts[1]


def own_places(members, info, got):
    return got[pl.ds(info[0] * members, members), 0, LANES : 2 * LANES]


def slot_hot(members, groups, slots, info, place_rows, column, mr, tokens):
    column[...] = row_to_col(place_rows[pl.ds(mr, 1), :])
    place = [
        column[pl.ds(pl.multiple_of((info[0] ^ d) * slots, slots), slots), :]
        for d in range(groups)
    ]
    return jnp.concatenate(place, axis=0) == iota((groups * slots, tokens), 1) + 1


def pick_kernel(members, groups, slots, info, got, *refs):
    encs = refs[:members]
    outs = refs[members : members + groups]
    place_rows, column = refs[members + groups :]
    place_rows[...] = own_places(members, info, got)
    for e in range(members):
        mr = info[1] ^ e
        tokens = encs[e].shape[0]
        hot = as_bf16(slot_hot(members, groups, slots, info, place_rows, column, mr, tokens))
        hi, mid, low = split3(encs[e][...])
        found = (dot1(hot, hi, NN) + dot1(hot, mid, NN)) + dot1(hot, low, NN)
        at = pl.ds(pl.multiple_of(mr * slots, slots), slots)
        for d in range(groups):
            outs[d][at, :] = found[d * slots : (d + 1) * slots]


def positive_kernel(members, groups, slots, tokens, info, got, stats, *refs):
    rows, picked = refs[:groups], refs[groups : 2 * groups]
    joined, own, place_rows, column = refs[2 * groups :]
    place_rows[...] = own_places(members, info, got)
    for e in range(members):
        mr = info[1] ^ e
        lanes = pl.ds(pl.multiple_of(mr * tokens, LANES), tokens)
        at = pl.ds(pl.multiple_of(mr * slots, slots), slots)
        hot = slot_hot(members, groups, slots, info, place_rows, column, mr, tokens)
        row = jnp.concatenate([r[at, :] for r in rows], axis=0)
        enc = jnp.concatenate([p[at, :] for p in picked], axis=0)
        value = jnp.sum(row * enc, axis=1, keepdims=True)
        positive = jnp.sum(jnp.where(hot, value, 0.0), axis=0, keepdims=True)
        has = jnp.sum(hot.astype(F32), axis=0, keepdims=True)
        old = stats[0:1, lanes]
        top = jnp.where(has > 0, jnp.maximum(old, positive), old)
        joined[0:1, lanes] = top
        joined[1:2, lanes] = stats[1:2, lanes] * jnp.exp(old - top) + jnp.where(
            has > 0, jnp.exp(positive - top), 0.0
        )
        own[0:1, lanes] = positive
        own[1:2, lanes] = has


def pulled_kernel(members, groups, slots, blocks, info, got, *refs):
    negs, refs = refs[:groups], refs[groups:]
    rows, refs = refs[:groups], refs[groups:]
    prob_hi, prob_lo, pulled, row_t, place_rows, column = refs
    place_rows[...] = own_places(members, info, got)
    neg = jnp.concatenate([row[...] for row in negs], axis=0)
    neg_t = split(jnp.transpose(neg))
    tokens = pulled.shape[2]
    for i, e in enumerate(blocks):
        mr = info[1] ^ e
        pulled[i] = dot3(neg_t, (prob_hi[i], prob_lo[i]), NN)
        at = pl.ds(pl.multiple_of(mr * slots, slots), slots)
        hot = slot_hot(members, groups, slots, info, place_rows, column, mr, tokens)
        high, low = split(jnp.concatenate([r[at, :] for r in rows], axis=0))
        row_t[i] = dot1(high, as_bf16(hot), TN) + dot1(low, as_bf16(hot), TN)


def join(first, second):
    top = jnp.maximum(first[0:1], second[0:1])
    total = first[1:2] * jnp.exp(first[0:1] - top) + second[1:2] * jnp.exp(second[0:1] - top)
    return top, total


def join_kernel(first, second, *refs):
    out = refs[-1]
    top, total = join(first[...], second[...])
    out[0:1, :] = top
    out[1:2, :] = total


def shares(info, e, tokens, final, stats, own):
    lanes = pl.ds(pl.multiple_of((info[1] ^ e) * tokens, LANES), tokens)
    top, total = final[0:1, lanes], final[1:2, lanes]
    scale = jnp.exp(stats[0:1, lanes] - top) / total
    extra = jnp.where(
        own[1:2, lanes] > 0, jnp.exp(own[0:1, lanes] - top) / total - 1.0, 0.0
    )
    return scale, extra


def pull_kernel(halves, blocks, tokens, info, final, stats, own, *refs):
    for e, out in zip(blocks, refs[-len(blocks) :]):
        h = 0 if e in halves[0] else 1
        pulled, row_t = (ref[halves[h].index(e)] for ref in refs[2 * h : 2 * h + 2])
        scale, extra = shares(info, e, tokens, final, stats, own)
        out[...] = pulled * scale + row_t * extra


def flat(table, lane, slots):
    return jnp.concatenate(
        [table[m : m + 1, lane : lane + slots] for m in range(table.shape[0])], axis=1
    )


def grad_kernel(members, groups, slots, halves, info, got, final, stats, own, *refs):
    probs, refs = refs[: 2 * len(halves)], refs[2 * len(halves) :]
    encs = refs[:members]
    *outs, total, coef, place_rows = refs[-groups - 3 :]
    place_rows[...] = own_places(members, info, got)
    tokens, width = encs[0].shape
    for h, i, e in [(h, i, e) for h, blocks in enumerate(halves) for i, e in enumerate(blocks)]:
        mr = info[1] ^ e
        scale, extra = shares(info, e, tokens, final, stats, own)
        enc = split(encs[e][...] * row_to_col(scale))
        part = dot3((probs[2 * h][i], probs[2 * h + 1][i]), enc, NN)
        if h == 0 and i == 0:
            total[...] = part
        else:
            total[...] += part
        hot = place_rows[pl.ds(mr, 1), :] == iota((tokens, LANES), 0) + 1
        coef[pl.ds(mr, 1), :] = jnp.sum(
            jnp.where(hot, row_to_col(extra), 0.0), axis=0, keepdims=True
        )
    count = total.shape[0] // groups
    lines = [flat(coef[...], g * slots, slots) for g in range(groups)]
    for d, out in enumerate(outs):
        out[0:count, :] = total[d * count : (d + 1) * count, :]
        line = lines[0]
        for g in range(1, groups):
            line = jnp.where((info[0] ^ d) == g, lines[g], line)
        out[count:, 0 : line.shape[1]] = jnp.broadcast_to(line, (8, line.shape[1]))


def equal_in_batch(ids):
    size = ids.shape[1]
    across = jnp.broadcast_to(ids.astype(F32), (size, size))
    same = (jnp.transpose(across) == across) & (
        (iota((size, size), 0) // BATCH) == (iota((size, size), 1) // BATCH)
    )
    return same.astype(F32)


def scatter_kernel(members, groups, own, slots, count, info, got_v, requests, *refs):
    size = len(own)
    grads, picked = refs[:size], refs[size : 2 * size]
    out, negs, tgts, got, arrived = refs[-5:]
    copy = pltpu.make_async_copy(requests, got, arrived)
    copy.start()
    out[...] = refs[2 * size][...] if own[0] else jnp.zeros_like(out)

    def add_rows(asked, first, source, base, number):
        for b in range(0, number, BATCH):
            rows = [asked[first + b + k] for k in range(BATCH)]
            new = [
                out[pl.ds(rows[k], 1), :] + source[pl.ds(base + b + k, 1), :]
                for k in range(BATCH)
            ]
            for k in range(BATCH):
                out[pl.ds(rows[k], 1), :] = new[k]

    copy.wait()
    for i, d in enumerate(own):
        g = info[0] ^ d
        asked = got_v[pl.ds(g * members, members), 0, 0:LANES]
        number = members * count
        same = as_bf16(equal_in_batch(flat(asked, slots, count)) > 0)
        high, low = split(grads[i][0:number, :])
        negs[...] = dot1(same, high, NN) + dot1(same, low, NN)
        weight = equal_in_batch(flat(asked, 0, slots))
        weight = weight * grads[i][number : number + 1, 0 : members * slots]
        tgts[...] = dot3(split(weight), split(picked[i][...]), NN)
        merged = BATCH // count if count < BATCH else 1

        def member(step, carry, g=g, merged=merged):
            if merged == 1:
                add_rows(got.at[g * members + step, 0], slots, negs, step * count, count)
                add_rows(got.at[g * members + step, 0], 0, tgts, step * slots, slots)
                return carry
            first = g * members + step * merged
            rows = [
                got[first + k // count, 0, slots + k % count] for k in range(BATCH)
            ]
            new = [
                out[pl.ds(rows[k], 1), :] + negs[pl.ds(step * BATCH + k, 1), :]
                for k in range(BATCH)
            ]
            for k in range(BATCH):
                out[pl.ds(rows[k], 1), :] = new[k]
            for m in range(merged):
                add_rows(got.at[first + m, 0], 0, tgts, (step * merged + m) * slots, slots)
            return carry

        lax.fori_loop(0, members // merged, member, 0)


def add_kernel(terms, *refs):
    total = refs[0][...]
    for ref in refs[1:terms]:
        total = total + ref[...]
    refs[-1][...] = total


def finish_kernel(valid, *refs):
    total = refs[0][...]
    for ref in refs[1:-1]:
        total = total + ref[...]
    refs[-1][...] = jnp.transpose(total) * row_to_col(valid[...].astype(F32))


def swap(value, axis, d):
    return lax.ppermute(value, axis, [(i, i ^ d) for i in range(lax.axis_size(axis))])


def shards(encoded, item_table, target_owner, target_local, negative_ids, valid):
    groups, members = lax.axis_size("group"), lax.axis_size("member")
    devices = groups * members
    tokens, width = encoded.shape
    rows_dev = item_table.shape[0]
    negatives = negative_ids.shape[0]
    slots = max(2, 4 * tokens // devices)
    count = negatives // devices
    near = max(1, members // 4)
    everyone = members * tokens
    shape = jax.ShapeDtypeStruct
    sds = lambda *s: shape(s, F32)

    info = PLACE
    ints = jnp.concatenate([target_owner.reshape(-1), target_local, valid, negative_ids])
    request, masked = call(
        functools.partial(front_kernel, members, rows_dev, slots, tokens, negatives),
        [shape((devices, 1, 2 * LANES), I32), sds(tokens, width)],
        [SMEM] + [VMEM] * 2,
        [VMEM] * 2,
        (info, ints.reshape(1, -1), encoded),
        name="front",
    )
    got = lax.all_to_all(
        request, ("group", "member"), split_axis=0, concat_axis=0, tiled=True
    )

    encs = [masked] + [None] * (members - 1)
    for z in (near, 2 * near):
        encs[z] = swap(masked, "member", z)
    onward, got = lax.optimization_barrier((encs[2 * near], got))
    encs[3 * near] = swap(onward, "member", near)
    for z in (0, 2 * near):
        for x in range(1, near):
            encs[z ^ x] = swap(onward if z == 2 * near else encs[z], "member", x)
    halves = [[d for d in range(members) if (d < near) or d in (near, 2 * near)], []]
    halves[1] = [d for d in range(members) if d not in halves[0]]

    early = [encs[d] for d in halves[0] if d and d != near]

    def after(blocks, done):
        return [lax.optimization_barrier((block, done))[0] for block in blocks]

    def gather(chosen, part, many, deps, name):
        return call(
            functools.partial(gather_kernel, members, chosen, part, many),
            [sds(members * many, width)] * len(chosen),
            [SMEM, SMEM, VMEM] + [ANY] * len(deps),
            [VMEM] * len(chosen),
            (info, got, item_table, *deps),
            name=name,
        )

    negs = gather(range(groups), slots, count, early, "gather_negatives")
    for x in range(1, near):
        encs[near + x] = swap(lax.optimization_barrier((encs[x], negs[0]))[0], "member", near)
    negs = [negs[0]] + [swap(negs[d], "group", d) for d in range(1, groups)]
    waited = [encs[near], *encs[2 * near + 1 : 3 * near]]
    rows = gather(range(2, groups), 0, slots, waited, "gather_far_targets")
    gathered = rows
    for x in range(1, near):
        encs[3 * near + x] = swap(after([encs[3 * near]], rows[0])[0], "member", x)
    rows = [swap(row, "group", d) for d, row in enumerate(rows, 2)]

    stats, probs = [], []
    for blocks in halves:
        many = len(blocks)
        *stats, hi, lo = call(
            functools.partial(score_kernel, blocks, groups, bool(stats)),
            [sds(2, everyone)] + [shape((many, negatives, tokens), BF16)] * 2,
            [SMEM] + [VMEM] * (groups + many + len(stats)) + [ANY] * len(gathered),
            [VMEM] * 3,
            (info, *negs, *[encs[e] for e in blocks], *stats, *gathered),
            flops=12 * many * tokens * negatives * width,
            moved=MIB,
            name="score",
        )
        probs += [hi, lo]
        if gathered:
            gathered = []
            kept, row = gather(range(2), 0, slots, stats, "gather_targets")
            rows = [kept, swap(row, "group", 1), *rows]
    stats = stats[0]
    picked = call(
        functools.partial(pick_kernel, members, groups, slots),
        [sds(members * slots, width)] * groups,
        [SMEM] + [VMEM] * (1 + members),
        [VMEM] * groups,
        (info, got, *encs),
        scratch=[pltpu.VMEM((members, LANES), I32), pltpu.VMEM((LANES, 1), I32)],
        name="pick",
    )
    sent = list(picked[:2]) + [
        swap(b, "group", d) for d, b in enumerate(after(picked[2:], stats), 2)
    ]
    joined, own = call(
        functools.partial(positive_kernel, members, groups, slots, tokens),
        [sds(2, everyone)] * 2,
        [SMEM] + [VMEM] * (2 + 2 * groups),
        [VMEM] * 2,
        (info, got, stats, *rows, *picked),
        scratch=[pltpu.VMEM((members, LANES), I32), pltpu.VMEM((LANES, 1), I32)],
        name="positive",
    )
    pulled = []
    for h, blocks in enumerate(halves):
        pulled += call(
            functools.partial(pulled_kernel, members, groups, slots, blocks),
            [sds(len(blocks), width, tokens)] * 2,
            [SMEM] + [VMEM] * (3 + 2 * groups),
            [VMEM] * 2,
            (info, got, *negs, *rows, *probs[2 * h : 2 * h + 2]),
            scratch=[pltpu.VMEM((members, LANES), I32), pltpu.VMEM((LANES, 1), I32)],
            flops=6 * len(blocks) * tokens * negatives * width,
            moved=MIB,
            name="pulled",
        )

    final = joined
    d, hops = 1, 0
    while d < members:
        late = pulled[2 * hops : 2 * hops + 2]
        hops += 1
        final = call(
            join_kernel,
            sds(2, everyone),
            [VMEM] * 2 + [ANY] * len(late),
            VMEM,
            (final, swap(final, "member", d), *late),
            name="join",
        )
        d *= 2

    grads = call(
        functools.partial(grad_kernel, members, groups, slots, halves),
        [sds(members * count + 8, width)] * groups,
        [SMEM] + [VMEM] * (4 + len(probs) + members) + [ANY] * (groups - 2),
        [VMEM] * groups,
        (info, got, final, stats, own, *probs, *encs, *sent[2:]),
        scratch=[
            pltpu.VMEM((negatives, width), F32),
            pltpu.VMEM((members, LANES), F32),
            pltpu.VMEM((members, LANES), I32),
        ],
        flops=6 * everyone * negatives * width,
        moved=8 * MIB,
        name="grad",
    )
    def added(terms, deps, flops=0):
        return call(
            functools.partial(add_kernel, len(terms)),
            sds(width, tokens),
            [VMEM] * len(terms) + [ANY] * len(deps),
            VMEM,
            (*terms, *deps),
            flops=flops,
            name="add",
        )

    graded = [grads[0]]
    sent[1] = swap(after([sent[1]], grads[0])[0], "group", 1)
    grads = graded + [swap(grads[d], "group", d) for d in range(1, groups)]
    def scaled(blocks, deps):
        return call(
            functools.partial(pull_kernel, halves, blocks, tokens),
            [sds(width, tokens)] * len(blocks),
            [SMEM] + [VMEM] * 7 + [ANY] * len(deps),
            [VMEM] * len(blocks),
            (info, final, stats, own, *pulled, *deps),
            name="pull",
        )

    def beside(blocks):
        return [swap(block, "member", x) for x, block in enumerate(blocks, 1)]

    along = list(range(near))
    def scatter(own, base, deps, flops):
        return call(
            functools.partial(scatter_kernel, members, groups, own, slots, count),
            sds(rows_dev, width),
            [SMEM, VMEM, ANY] + [VMEM] * (2 * len(own) + len(base)) + [ANY] * len(deps),
            VMEM,
            (info, got, got, *[grads[d] for d in own], *[sent[d] for d in own], *base, *deps),
            scratch=[
                pltpu.VMEM((members * count, width), F32),
                pltpu.VMEM((members * slots, width), F32),
                pltpu.SMEM(got.shape, I32),
                pltpu.SemaphoreType.DMA,
            ],
            flops=flops,
            name="scatter",
        )

    farthest, *rest = scaled([*[3 * near + x for x in along], *[near + x for x in along[1:]]], [])
    rest, diagonal = rest[: near - 1], rest[near - 1 :]
    arrived = beside(rest)
    diagonal = [swap(block, "member", near) for block in diagonal]
    near_blocks = [near, *along[1:]]
    kept, far, *others = scaled(
        [0, *[2 * near + x for x in along], *near_blocks], graded
    )
    others, sends = others[: near - 1], others[near - 1 :]
    total = added([farthest, *arrived], [*graded, *diagonal])
    sums = [added([sends[x], diagonal[x - 1]], []) for x in along[1:]]
    others = after(others, total)
    table_own = scatter(list(range(2)), [], [total], 1 << 33)
    far = added([far], [table_own, *grads[2:]])
    others = beside(others)
    half = added([far, swap(total, "member", near), *others], [])
    held = after(sends[:1], others[0]) + after(sums, half)
    parts = [swap(b, "member", d) for d, b in zip(near_blocks, held)]
    parts.append(added([kept, swap(half, "member", 2 * near)], []))

    table_grad = scatter(list(range(2, groups)), [table_own], [], 0)
    encoded_grad = call(
        finish_kernel,
        sds(tokens, width),
        [VMEM] * (1 + len(parts)),
        VMEM,
        (valid.reshape(1, -1), *parts),
        name="finish",
    )
    return (encoded_grad, table_grad)


def solution(mesh):
    placed = (
        P(("group", "member"), None),
        P(("group", "member"), None),
        P(("group", "member"), None),
        P(("group", "member")),
        P(("group", "member")),
        P(("group", "member")),
    )
    return jax.shard_map(
        shards,
        mesh=mesh,
        in_specs=placed,
        out_specs=(P(("group", "member"), None), P(("group", "member"), None)),
        check_vma=False,
    )
```
